32 devices in a mesh: cand: 8 (over y, x, core), tensor: 4 (over z).
Axes of the slice: x: 2, y: 2, z: 4, core: 2. Of those that a mesh axis runs over, the one named last changes fastest.
Arguments:
- hidden_in: bfloat16 [4096, 5120], P('cand', 'tensor')
- lengths: int32 [8], P('cand'), may hold values from 256 to 512, as said below
- summary_pos: int32 [8, 128], P('cand'), may hold values from 0 to 511, as said below
- w_query: bfloat16 [5120, 4096], P(None, 'tensor')
- w_key: bfloat16 [5120, 512], P(None, 'tensor')
- w_value: bfloat16 [5120, 512], P(None, 'tensor'), may hold values from -0.078125 to 0.078125
- w_out: bfloat16 [4096, 5120], P('tensor'), may hold values from -0.09375 to 0.09375
- q_gain: float32 [128], replicated
- k_gain: float32 [128], replicated
Outputs:
- mixed: bfloat16 [4096, 5120], P(('cand', 'tensor'))
The draws below stay inside these ranges and needn't reach their ends.
Inputs may be any that keep to these rules, and one draw needn't show every extreme that they name: `lengths`: some candidate has exactly 512 valid tokens and some exactly half of 512. `summary_pos`: each candidate's positions are distinct, ascending and below its length; the first is 0 and the last is its length minus one.
All inputs are finite; a program needn't handle non-finite values.
Results may differ from the reference program's by a relative error of at most 0.013.
The reference program's roundings to bfloat16 on the way count: a program that leaves them out, or rounds other values in their place, can miss the bound.
Values may be sent and summed in bfloat16 or wider, within the bound.
No kernel may reach another device: no remote copies, remote signals or barrier semaphores. Data moves between devices by JAX's collectives and lax.ppermute only.
A program may use at most 128 MiB of HBM per device.

```python
import jax
import jax.numpy as jnp
from jax import lax

D = 5120
HEAD = 128
QH = 32
KVH = 4
TOK = 512
SUMM = 128
CAND = 8
N_CAND = 8


def candidate_lengths(key):
    key = jax.random.fold_in(key, 103)
    drawn = jax.random.randint(jax.random.fold_in(key, 1), (CAND,), TOK // 2, TOK + 1)
    order = jax.random.permutation(jax.random.fold_in(key, 2), CAND)
    drawn = drawn.at[order[0]].set(TOK).at[order[1]].set(TOK // 2)
    return drawn.astype(jnp.int32)


def draw_lengths(key, part):
    return candidate_lengths(key)


def draw_summary_pos(key, part):
    bounds = candidate_lengths(key)
    key = jax.random.fold_in(key, 7)

    def pick(sub_key, bound):
        shuffled = jax.random.permutation(sub_key, TOK).astype(jnp.int32)
        usable = (shuffled >= 1) & (shuffled <= bound - 2)
        ranking = jnp.where(usable, 0, 1) * TOK + jnp.arange(TOK, dtype=jnp.int32)
        chosen = shuffled[jnp.argsort(ranking)[:SUMM - 2]]
        whole = jnp.concatenate([jnp.zeros((1,), jnp.int32), chosen, (bound - 1)[None].astype(jnp.int32)])
        return jnp.sort(whole)
    sub_keys = jax.random.split(key, CAND)
    return jax.vmap(pick)(sub_keys, bounds).astype(jnp.int32)


def draw_hidden_in(key, part):
    key = jax.random.fold_in(key, 11)
    noise = jax.random.normal(key, (CAND, TOK, D), jnp.float32)
    noise = jnp.clip(noise, -6.0, 6.0)
    return noise.reshape(CAND * TOK, D).astype(jnp.bfloat16)


def draw_w_query(key, part):
    key = jax.random.fold_in(key, 12)
    matrix = jax.random.normal(key, (D, QH * HEAD), jnp.float32) * D ** (-0.5)
    return matrix.astype(jnp.bfloat16)


def draw_w_key(key, part):
    key = jax.random.fold_in(key, 13)
    matrix = jax.random.normal(key, (D, KVH * HEAD), jnp.float32) * D ** (-0.5)
    return matrix.astype(jnp.bfloat16)


def draw_q_gain(key, part):
    key = jax.random.fold_in(key, 14)
    return jnp.exp(jax.random.uniform(key, (HEAD,), jnp.float32, 0.0, 0.9163))


def draw_k_gain(key, part):
    key = jax.random.fold_in(key, 15)
    return jnp.exp(jax.random.uniform(key, (HEAD,), jnp.float32, 0.0, 0.9163))


def shard_levels(rng, extent, shards, smallest, high):
    factor_of, own = 1.0, jax.random.fold_in(rng, 6)
    for dim, shards_of in shards:
        draws = jnp.exp(jax.random.uniform(jax.random.fold_in(own, dim), (shards_of,), jnp.float32, smallest / len(shards), high / len(shards)))
        factor_of = factor_of * jnp.repeat(draws, extent[dim] // shards_of).reshape([-1 if axis == dim else 1 for axis in range(len(extent))])
    return factor_of


def normal_values(rng, shape, spread, most, pieces=(), kind=jnp.bfloat16):
    values = spread * jax.random.normal(rng, shape, jnp.float32)
    if pieces:
        values = values * shard_levels(rng, shape, pieces, -0.22, 0.18)
    return jnp.clip(values, -most, most).astype(kind)


def setup_inputs(seed: int = 0) -> dict:
    keys = jax.random.split(jax.random.key(seed), 10)
    hidden_in = draw_hidden_in(jax.random.fold_in(keys[9], 71), 0)
    lengths = draw_lengths(jax.random.fold_in(keys[9], 71), 0)
    summary_pos = draw_summary_pos(jax.random.fold_in(keys[9], 71), 0)
    w_query = draw_w_query(jax.random.fold_in(keys[9], 71), 0)
    w_key = draw_w_key(jax.random.fold_in(keys[9], 71), 0)
    w_value = normal_values(keys[5], (D, KVH * HEAD), D ** -0.5, 0.078125, ((1, 4),))
    w_out = normal_values(keys[6], (QH * HEAD, D), (QH * HEAD) ** -0.5, 0.09375, ((0, 4),))
    q_gain = draw_q_gain(jax.random.fold_in(keys[9], 71), 0)
    k_gain = draw_k_gain(jax.random.fold_in(keys[9], 71), 0)
    return dict(hidden_in=hidden_in, lengths=lengths, summary_pos=summary_pos, w_query=w_query, w_key=w_key, w_value=w_value, w_out=w_out, q_gain=q_gain, k_gain=k_gain)


def rope_tables(rows, width):
    half_width = width // 2
    frequency = 1000000.0 ** (-(jnp.arange(half_width, dtype=jnp.float32) * 2.0 / width))
    angle = jnp.arange(rows, dtype=jnp.float32)[:, None] * frequency[None, :]
    angle = jnp.concatenate([angle, angle], axis=1)
    return (jnp.cos(angle), jnp.sin(angle))

def rotate(vectors, cosine, sine):
    half_width = vectors.shape[-1] // 2
    turned = jnp.concatenate([-vectors[..., half_width:], vectors[..., :half_width]], axis=-1)
    return vectors * cosine + turned * sine

def head_norm(vectors, gain):
    return vectors * lax.rsqrt(lax.optimization_barrier(jnp.mean(vectors * vectors, axis=-1, keepdims=True)) + 1e-06) * gain

def reference(hidden_in, lengths, summary_pos, w_query, w_key, w_value, w_out, q_gain, k_gain):
    cands = N_CAND
    per_group = QH // KVH
    cosine, sine = rope_tables(TOK, HEAD)
    proj_query = jnp.dot(hidden_in, w_query, preferred_element_type=jnp.float32)
    proj_query = proj_query.reshape(cands, TOK, QH, HEAD).transpose(0, 2, 1, 3)
    queries = rotate(head_norm(proj_query, q_gain), cosine, sine).astype(jnp.bfloat16)
    proj_key = jnp.dot(hidden_in, w_key, preferred_element_type=jnp.float32)
    proj_key = proj_key.reshape(cands, TOK, KVH, HEAD).transpose(0, 2, 1, 3)
    keys_all = rotate(head_norm(proj_key, k_gain), cosine, sine).astype(jnp.bfloat16)
    values_all = jnp.dot(hidden_in, w_value, preferred_element_type=jnp.float32).astype(jnp.bfloat16)
    values_all = values_all.reshape(cands, TOK, KVH, HEAD).transpose(0, 2, 1, 3)
    summary_keys = jax.vmap(lambda block, picks: block[:, picks, :])(keys_all, summary_pos)
    summary_values = jax.vmap(lambda block, picks: block[:, picks, :])(values_all, summary_pos)
    flat_keys = summary_keys.transpose(1, 0, 2, 3).reshape(KVH, cands * SUMM, HEAD)
    flat_values = summary_values.transpose(1, 0, 2, 3).reshape(KVH, cands * SUMM, HEAD)
    columns = jnp.arange(TOK + cands * SUMM, dtype=jnp.int32)
    row_index = jnp.arange(TOK, dtype=jnp.int32)
    block_of = (columns - TOK) // SUMM

    def one_candidate(index):
        length = lengths[index]
        query_f = queries[index].astype(jnp.float32).reshape(KVH, per_group, TOK, HEAD)
        keys_f = jnp.concatenate([keys_all[index], flat_keys], axis=1).astype(jnp.float32)
        values_f = jnp.concatenate([values_all[index], flat_values], axis=1).astype(jnp.float32)
        scores = jnp.einsum('kgth,ksh->kgts', query_f, keys_f) * HEAD ** (-0.5)
        own_keys = (columns[None, :] <= row_index[:, None]) & (columns[None, :] < length)
        other_keys = (block_of != index)[None, :]
        allowed = jnp.where((columns < TOK)[None, :], own_keys, other_keys)
        scores = jnp.where(allowed, scores, -1e+30)
        largest = lax.optimization_barrier(jnp.max(scores, axis=-1))
        expo = jnp.exp(scores - largest[..., None])
        total = lax.optimization_barrier(jnp.sum(expo, axis=-1))
        weights = expo.astype(jnp.bfloat16).astype(jnp.float32)
        mixed_heads = jnp.einsum('kgts,ksh->kgth', weights, values_f) / total[..., None]
        attended = mixed_heads.reshape(QH, TOK, HEAD).transpose(1, 0, 2).reshape(TOK, QH * HEAD)
        return jnp.where(row_index[:, None] < length, attended, 0.0).astype(jnp.bfloat16)
    attended = lax.map(one_candidate, jnp.arange(cands, dtype=jnp.int32)).reshape(cands * TOK, QH * HEAD)
    return jnp.dot(attended, w_out, preferred_element_type=jnp.float32).astype(jnp.bfloat16)
```

```python
import functools

import jax
import jax.numpy as jnp
from jax import lax
from jax.experimental import pallas as pl
from jax.experimental.pallas import tpu as pltpu
from jax.sharding import PartitionSpec as P

VMEM_LIMIT = 48 * 1024 * 1024
LOG2E = 1.4426950408889634


def rope_tables(rows, width):
    half_width = width // 2
    frequency = 1000000.0 ** (-(jnp.arange(half_width, dtype=jnp.float32) * 2.0 / width))
    angle = jnp.arange(rows, dtype=jnp.float32)[:, None] * frequency[None, :]
    cosine, sine = jnp.cos(angle), jnp.sin(angle)
    return (
        jnp.concatenate([cosine, cosine], axis=1),
        jnp.concatenate([-sine, sine], axis=1),
    )


def norm_rope(vectors, gain, cosine, sine):
    scale = lax.rsqrt(jnp.mean(vectors * vectors, axis=-1, keepdims=True) + 1e-06)
    vectors = vectors * scale * gain
    return vectors * cosine + pltpu.roll(vectors, vectors.shape[-1] // 2, 1) * sine


def params():
    return pltpu.CompilerParams(vmem_limit_bytes=VMEM_LIMIT)


def partial_kernel(n_hidden, with_acc, block_ref, *refs):
    hidden = refs[0][...]
    for ref in refs[1:n_hidden]:
        hidden = hidden + ref[...]
    w_ref, out_ref = refs[n_hidden], refs[-1]
    product = jnp.dot(hidden, w_ref[...], preferred_element_type=jnp.float32)
    if with_acc:
        product = product + refs[n_hidden + 1][...]
    out_ref[...] = product


def partial_projection(block, hidden, weights, acc):
    rows, features = hidden[0].shape
    width = weights.shape[1]
    tile = 256
    in_specs = [pl.BlockSpec((rows, features), lambda i, b: (0, 0)) for _ in hidden]
    in_specs.append(pl.BlockSpec((features, tile), lambda i, b: (b[0], i)))
    operands = [*hidden, weights]
    if acc is not None:
        in_specs.append(pl.BlockSpec((rows, tile), lambda i, b: (0, i)))
        operands.append(acc)
    return pl.pallas_call(
        functools.partial(partial_kernel, len(hidden), acc is not None),
        grid_spec=pltpu.PrefetchScalarGridSpec(
            num_scalar_prefetch=1,
            grid=(width // tile,),
            in_specs=in_specs,
            out_specs=pl.BlockSpec((rows, tile), lambda i, b: (0, i)),
        ),
        out_shape=jax.ShapeDtypeStruct((rows, width), jnp.float32),
        compiler_params=params(),
        cost_estimate=pl.CostEstimate(
            flops=2 * rows * features * width,
            bytes_accessed=2 * features * (rows + width) + 8 * rows * width,
            transcendentals=0,
        ),
        name="partial_projection",
    )(block, *operands)


def keys_values_kernel(
    n_hidden, head, block_ref, *refs
):
    hidden = refs[0][...]
    for ref in refs[1:n_hidden]:
        hidden = hidden + ref[...]
    w_ref, acc_ref, gain_ref, cos_ref, sin_ref, pos_ref, k_ref, v_ref, s_ref = refs[n_hidden:]
    proj = acc_ref[...] + jnp.dot(hidden, w_ref[...], preferred_element_type=jnp.float32)
    keys = norm_rope(proj[:, :head], gain_ref[...], cos_ref[...], sin_ref[...])
    keys = keys.astype(jnp.bfloat16)
    values = proj[:, head:].astype(jnp.bfloat16)
    k_ref[...] = keys
    v_ref[...] = values
    picks = pos_ref.shape[0]
    rows = keys.shape[0]
    chosen = lax.broadcasted_iota(jnp.int32, (picks, rows), 1) == pos_ref[...]
    chosen = jnp.where(chosen, 1.0, 0.0).astype(jnp.bfloat16)
    both = jnp.concatenate([keys, values], axis=1)
    picked = jnp.dot(chosen, both, preferred_element_type=jnp.float32).astype(jnp.bfloat16)
    s_ref[:picks, :] = picked[:, :head]
    s_ref[picks:, :] = picked[:, head:]


def keys_values(block, hidden, weights, acc, gain, cosine, sine, positions):
    rows, features = hidden[0].shape
    head = gain.shape[1]
    picks = positions.shape[0]
    whole = lambda *shape: pl.BlockSpec(shape, lambda i, b: (0, 0))
    return pl.pallas_call(
        functools.partial(keys_values_kernel, len(hidden), head),
        grid_spec=pltpu.PrefetchScalarGridSpec(
            num_scalar_prefetch=1,
            grid=(1,),
            in_specs=[whole(rows, features) for _ in hidden]
            + [
                pl.BlockSpec((features, 2 * head), lambda i, b: (b[0], 0)),
                whole(rows, 2 * head),
                whole(1, head),
                whole(rows, head),
                whole(rows, head),
                whole(picks, 1),
            ],
            out_specs=[whole(rows, head), whole(rows, head), whole(2 * picks, head)],
        ),
        out_shape=[
            jax.ShapeDtypeStruct((rows, head), jnp.bfloat16),
            jax.ShapeDtypeStruct((rows, head), jnp.bfloat16),
            jax.ShapeDtypeStruct((2 * picks, head), jnp.bfloat16),
        ],
        compiler_params=params(),
        cost_estimate=pl.CostEstimate(
            flops=4 * rows * features * head,
            bytes_accessed=2 * features * (rows + 2 * head) + 12 * rows * head,
            transcendentals=0,
        ),
        name="keys_values",
    )(block, *hidden, weights, acc, gain, cosine, sine, positions)


def queries_kernel(n_hidden, head, block_ref, *refs):
    hidden = refs[0][...]
    for ref in refs[1:n_hidden]:
        hidden = hidden + ref[...]
    w_ref, acc_ref, gain_ref, cos_ref, sin_ref, q_ref = refs[n_hidden:]
    proj = acc_ref[...] + jnp.dot(hidden, w_ref[...], preferred_element_type=jnp.float32)
    for start in range(0, proj.shape[1], head):
        one = norm_rope(proj[:, start : start + head], gain_ref[...], cos_ref[...], sin_ref[...])
        q_ref[:, start : start + head] = one.astype(jnp.bfloat16)


def queries_of(block, hidden, weights, acc, gain, cosine, sine):
    rows, features = hidden[0].shape
    head = gain.shape[1]
    skip = 1
    tile = 2 * head
    width = weights.shape[1] - tile
    whole = lambda *shape: pl.BlockSpec(shape, lambda i, b: (0, 0))
    return pl.pallas_call(
        functools.partial(queries_kernel, len(hidden), head),
        grid_spec=pltpu.PrefetchScalarGridSpec(
            num_scalar_prefetch=1,
            grid=(width // tile,),
            in_specs=[whole(rows, features) for _ in hidden]
            + [
                pl.BlockSpec((features, tile), lambda i, b: (b[0], i + skip)),
                pl.BlockSpec((rows, tile), lambda i, b: (0, i + skip)),
                whole(1, head),
                whole(rows, head),
                whole(rows, head),
            ],
            out_specs=pl.BlockSpec((rows, tile), lambda i, b: (0, i)),
        ),
        out_shape=jax.ShapeDtypeStruct((rows, width), jnp.bfloat16),
        compiler_params=params(),
        cost_estimate=pl.CostEstimate(
            flops=2 * rows * features * width,
            bytes_accessed=2 * features * (rows + width) + 6 * rows * width,
            transcendentals=0,
        ),
        name="queries",
    )(block, *hidden, weights, acc, gain, cosine, sine)


def attention_kernel(n_others, length_ref, q_ref, k_ref, v_ref, *refs):
    others = refs[:n_others]
    o_ref, keys_all, values_all = refs[n_others:]
    rows, head = q_ref.shape
    picks = others[0].shape[0] // 2
    cross = n_others * picks

    @pl.when(pl.program_id(0) == 0)
    def _():
        for index, ref in enumerate(others):
            keys_all[index * picks : (index + 1) * picks, :] = ref[:picks, :]
            values_all[index * picks : (index + 1) * picks, :] = ref[picks:, :]
        keys_all[cross:, :] = k_ref[...]
        values_all[cross:, :] = v_ref[...]

    scale = head ** (-0.5) * LOG2E
    tile = 256
    for start in range(0, rows, tile):
        reach = cross + start + tile
        scores = lax.dot_general(
            q_ref[start : start + tile, :],
            keys_all[:reach, :],
            (((1,), (1,)), ((), ())),
            preferred_element_type=jnp.float32,
        )
        row = lax.broadcasted_iota(jnp.int32, (tile, tile), 0)
        column = lax.broadcasted_iota(jnp.int32, (tile, tile), 1)
        own = jnp.where(column <= row, scores[:, reach - tile :], -1e30)
        free = scores[:, : reach - tile]
        largest = jnp.maximum(
            jnp.max(free, axis=1, keepdims=True), jnp.max(own, axis=1, keepdims=True)
        )
        free = jnp.exp2((free - largest) * scale)
        own = jnp.exp2((own - largest) * scale)
        total = jnp.sum(free, axis=1, keepdims=True) + jnp.sum(own, axis=1, keepdims=True)
        mixed = jnp.dot(
            free.astype(jnp.bfloat16),
            values_all[: reach - tile, :],
            preferred_element_type=jnp.float32,
        ) + jnp.dot(
            own.astype(jnp.bfloat16),
            values_all[reach - tile : reach, :],
            preferred_element_type=jnp.float32,
        )
        position = lax.broadcasted_iota(jnp.int32, (tile, head), 0) + start
        mixed = jnp.where(position < length_ref[0], mixed / total, 0.0)
        o_ref[start : start + tile, :] = mixed.astype(jnp.bfloat16)


def attention(lengths, queries, keys, values, others):
    rows, width = queries.shape
    head = keys.shape[1]
    picks = others[0].shape[0] // 2
    reach = rows + len(others) * picks
    whole = lambda *shape: pl.BlockSpec(shape, lambda i, b: (0, 0))
    one_head = pl.BlockSpec((rows, head), lambda i, b: (0, i))
    return pl.pallas_call(
        functools.partial(attention_kernel, len(others)),
        grid_spec=pltpu.PrefetchScalarGridSpec(
            num_scalar_prefetch=1,
            grid=(width // head,),
            in_specs=[one_head, whole(rows, head), whole(rows, head)]
            + [whole(2 * picks, head) for _ in others],
            out_specs=one_head,
            scratch_shapes=[
                pltpu.VMEM((reach, head), jnp.bfloat16),
                pltpu.VMEM((reach, head), jnp.bfloat16),
            ],
        ),
        out_shape=jax.ShapeDtypeStruct((rows, width), jnp.bfloat16),
        compiler_params=params(),
        cost_estimate=pl.CostEstimate(
            flops=4 * rows * width * reach,
            bytes_accessed=4 * rows * width + 4 * reach * head,
            transcendentals=rows * width // head * reach,
        ),
        name="attention",
    )(lengths, queries, keys, values, *others)


def shards(hidden_in, lengths, summary_pos, w_query, w_key, w_value, w_out, q_gain, k_gain):
    rows_here = hidden_in.shape[0]
    head_width = q_gain.shape[0]
    place = lax.axis_index("tensor")
    n_cand = lax.axis_size("cand")
    assert lax.axis_size("tensor") == 4 and w_key.shape[1] == head_width

    def swap(array):
        return lax.ppermute(array, "tensor", [(0, 1), (1, 0), (2, 3), (3, 2)])

    def across(array):
        return lax.ppermute(array, "tensor", [(1, 2), (2, 1)])

    def outward(array):
        return lax.ppermute(array, "tensor", [(1, 0), (2, 3)])

    def inward(array):
        return lax.ppermute(array, "tensor", [(0, 1), (3, 2)])

    low = place < 2
    near = jnp.bitwise_xor(place, 1)
    third = jnp.where(low, 2, 1)
    last = jnp.where(low, 3, 0)
    index = lambda block: block.astype(jnp.int32).reshape(1)

    weights = jnp.concatenate([w_key, w_value, w_query], axis=1)
    cosine, sine = rope_tables(rows_here, head_width)

    from_near = swap(hidden_in)
    from_mid = across(hidden_in)
    acc = partial_projection(index(place), [hidden_in], weights, None)
    to_outer = outward(from_mid)
    to_inner = across(from_near)
    acc = partial_projection(index(near), [from_near], weights, acc)
    end = outward(to_inner)
    acc = partial_projection(index(third), [from_mid, to_outer], weights, acc)
    final = [to_inner, end]
    keys, values, summary = keys_values(
        index(last), final, weights, acc, k_gain[None], cosine, sine, summary_pos.reshape(-1, 1)
    )
    others = [
        lax.ppermute(summary, "cand", [(i, (i + by) % n_cand) for i in range(n_cand)])
        for by in range(1, n_cand)
    ]
    queries = queries_of(index(last), final, weights, acc, q_gain[None], cosine, sine)
    attended = attention(lengths, queries, keys, values, others)

    part = rows_here // 4

    def mix(block):
        rows = lax.dynamic_slice_in_dim(attended, block * part, part, 0)
        return jnp.dot(rows, w_out, preferred_element_type=jnp.float32)

    far_sum = mix(last)
    far_sum = across((far_sum + inward(far_sum.astype(jnp.bfloat16))).astype(jnp.bfloat16))
    third_sum = mix(third)
    third_sum = across((third_sum + inward(third_sum.astype(jnp.bfloat16))).astype(jnp.bfloat16))
    near_sum = swap((mix(near) + far_sum).astype(jnp.bfloat16))
    return (mix(place) + near_sum + third_sum).astype(jnp.bfloat16)


def solution(mesh):
    return jax.shard_map(
        shards,
        mesh=mesh,
        in_specs=(
            P("cand", "tensor"),
            P("cand"),
            P("cand", None),
            P(None, "tensor"),
            P(None, "tensor"),
            P(None, "tensor"),
            P("tensor", None),
            P(),
            P(),
        ),
        out_specs=P(("cand", "tensor"), None),
        check_vma=False,
    )
```

```python
import functools

import jax
import jax.numpy as jnp
from jax import lax
from jax.experimental import pallas as pl
from jax.experimental.pallas import tpu as pltpu
from jax.sharding import PartitionSpec as P

VMEM_LIMIT = 48 * 1024 * 1024
LOG2E = 1.4426950408889634
OFFSETS = (0, 6, 2, 4, 1, 7, 3, 5)


def rope_tables(rows, width):
    half_width = width // 2
    frequency = 1000000.0 ** (-(jnp.arange(half_width, dtype=jnp.float32) * 2.0 / width))
    angle = jnp.arange(rows, dtype=jnp.float32)[:, None] * frequency[None, :]
    cosine, sine = jnp.cos(angle), jnp.sin(angle)
    return (
        jnp.concatenate([cosine, cosine], axis=1),
        jnp.concatenate([-sine, sine], axis=1),
    )


def norm_rope(vectors, gain, cosine, sine):
    scale = lax.rsqrt(jnp.mean(vectors * vectors, axis=-1, keepdims=True) + 1e-06)
    vectors = vectors * scale * gain
    return vectors * cosine + pltpu.roll(vectors, vectors.shape[-1] // 2, 1) * sine


def params():
    return pltpu.CompilerParams(vmem_limit_bytes=VMEM_LIMIT)


def after(array, cue):
    return lax.optimization_barrier((array, cue))[0]


def whole(*shape):
    return pl.BlockSpec(shape, lambda *_: (0,) * len(shape))


def summed(refs):
    total = refs[0][...]
    for ref in refs[1:]:
        total = total + ref[...]
    return total


def partial_kernel(counts, with_acc, block_ref, *refs):
    rows = []
    for count in counts:
        rows.append(summed(refs[:count]))
        refs = refs[count:]
    w_ref, out_ref = refs[0], refs[-1]
    start = 0
    for hidden in rows:
        stop = start + hidden.shape[0]
        product = jnp.dot(hidden, w_ref[...], preferred_element_type=jnp.float32)
        if with_acc:
            product = product + refs[1][start:stop, :]
        out_ref[start:stop, :] = product
        start = stop


def partial_projection(block, parts, weights, acc, tile):
    features = parts[0][0].shape[1]
    rows = sum(part[0].shape[0] for part in parts)
    width = weights.shape[1]
    arrivals = [array for part in parts for array in part]
    in_specs = [whole(*array.shape) for array in arrivals]
    in_specs.append(pl.BlockSpec((features, tile), lambda i, b: (b[0], i)))
    operands = [*arrivals, weights]
    if acc is not None:
        in_specs.append(pl.BlockSpec((rows, tile), lambda i, b: (0, i)))
        operands.append(acc)
    return pl.pallas_call(
        functools.partial(partial_kernel, [len(part) for part in parts], acc is not None),
        grid_spec=pltpu.PrefetchScalarGridSpec(
            num_scalar_prefetch=1,
            grid=(width // tile,),
            in_specs=in_specs,
            out_specs=pl.BlockSpec((rows, tile), lambda i, b: (0, i)),
        ),
        out_shape=jax.ShapeDtypeStruct((rows, width), jnp.float32),
        compiler_params=params(),
        name="partial_projection",
    )(block, *operands)


def keys_values_kernel(count, head, block_ref, *refs):
    hidden = summed(refs[:count])
    w_ref, acc_ref, gain_ref, cos_ref, sin_ref, out_ref = refs[count:]
    proj = acc_ref[...] + jnp.dot(hidden, w_ref[...], preferred_element_type=jnp.float32)
    keys = norm_rope(proj[:, :head], gain_ref[...], cos_ref[...], sin_ref[...])
    out_ref[:, :head] = keys.astype(jnp.bfloat16)
    out_ref[:, head:] = proj[:, head:].astype(jnp.bfloat16)


def last_keys_values_kernel(count, head, n_before, block_ref, *refs):
    before, (pos_ref, summary_ref) = refs[:n_before], (refs[n_before], refs[-1])
    refs = refs[n_before + 1 : -1]
    keys_values_kernel(count, head, block_ref, *refs)
    out_ref = refs[-1]
    picks = pos_ref.shape[0]
    picked, start = None, 0
    for ref in (*before, out_ref):
        rows = ref.shape[0]
        column = lax.broadcasted_iota(jnp.int32, (picks, rows), 1) + start
        chosen = jnp.where(column == pos_ref[...], 1.0, 0.0).astype(jnp.bfloat16)
        found = jnp.dot(chosen, ref[...], preferred_element_type=jnp.float32)
        picked = found if picked is None else picked + found
        start += rows
    summary_ref[...] = picked.astype(jnp.bfloat16)


def keys_values(block, hidden, part, weights, acc, gain, cosine, sine, before=(), positions=None):
    rows, features = hidden[0].shape
    head = gain.shape[1]
    row_part = lambda width: pl.BlockSpec((rows, width), lambda i, b: (part, 0))
    in_specs = [whole(rows, features) for _ in hidden] + [
        pl.BlockSpec((features, 2 * head), lambda i, b: (b[0], 0)),
        row_part(2 * head),
        whole(1, head),
        row_part(head),
        row_part(head),
    ]
    operands = [*hidden, weights, acc, gain, cosine, sine]
    out_shape = [jax.ShapeDtypeStruct((rows, 2 * head), jnp.bfloat16)]
    kernel = functools.partial(keys_values_kernel, len(hidden), head)
    if positions is not None:
        picks = positions.shape[0]
        in_specs = [whole(*array.shape) for array in (*before, positions)] + in_specs
        operands = [*before, positions, *operands]
        out_shape.append(jax.ShapeDtypeStruct((picks, 2 * head), jnp.bfloat16))
        kernel = functools.partial(last_keys_values_kernel, len(hidden), head, len(before))
    return pl.pallas_call(
        kernel,
        grid_spec=pltpu.PrefetchScalarGridSpec(
            num_scalar_prefetch=1,
            grid=(1,),
            in_specs=in_specs,
            out_specs=[whole(*shape.shape) for shape in out_shape],
        ),
        out_shape=out_shape,
        compiler_params=params(),
        name="keys_values",
    )(block, *operands)


def queries_kernel(count, head, block_ref, *refs):
    hidden = summed(refs[:count])
    w_ref, acc_ref, gain_ref, cos_ref, sin_ref, q_ref = refs[count:]
    proj = acc_ref[...] + jnp.dot(hidden, w_ref[...], preferred_element_type=jnp.float32)
    for start in range(0, proj.shape[1], head):
        one = norm_rope(proj[:, start : start + head], gain_ref[...], cos_ref[...], sin_ref[...])
        q_ref[:, start : start + head] = one.astype(jnp.bfloat16)


def queries_of(block, hidden, part, weights, acc, gain, cosine, sine):
    rows, features = hidden[0].shape
    head = gain.shape[1]
    width = weights.shape[1]
    tile = 4 * head
    row_part = pl.BlockSpec((rows, head), lambda i, b: (part, 0))
    return pl.pallas_call(
        functools.partial(queries_kernel, len(hidden), head),
        grid_spec=pltpu.PrefetchScalarGridSpec(
            num_scalar_prefetch=1,
            grid=(width // tile,),
            in_specs=[whole(rows, features) for _ in hidden]
            + [
                pl.BlockSpec((features, tile), lambda i, b: (b[0], i)),
                pl.BlockSpec((rows, tile), lambda i, b: (part, i)),
                whole(1, head),
                row_part,
                row_part,
            ],
            out_specs=pl.BlockSpec((rows, tile), lambda i, b: (0, i)),
        ),
        out_shape=jax.ShapeDtypeStruct((rows, width), jnp.bfloat16),
        compiler_params=params(),
        name="queries",
    )(block, *hidden, weights, acc, gain, cosine, sine)


def attention_kernel(n_parts, n_others, per_step, place_ref, heads_ref, length_ref, *refs):
    q_parts, refs = refs[: n_parts * per_step], refs[n_parts * per_step :]
    own_parts, refs = refs[:n_parts], refs[n_parts:]
    others, refs = refs[:n_others], refs[n_others:]
    o_ref, keys_all, values_all = refs
    part_rows, width = own_parts[0].shape
    head = width // 2
    picks = others[0].shape[0]
    cross = n_others * picks
    rows = o_ref.shape[0]

    @pl.when(pl.program_id(0) == 0)
    def _():
        start = 0
        for ref in (*others, *own_parts):
            stop = start + ref.shape[0]
            keys_all[start:stop, :] = ref[:, :head]
            values_all[start:stop, :] = ref[:, head:]
            start = stop

    scale = head ** (-0.5) * LOG2E
    first = place_ref[0] * rows
    own_rows = n_parts * part_rows
    for step in range(per_step):
        queries = q_parts[step * n_parts][...]
        if n_parts > 1:
            in_first = first < part_rows
            queries = jnp.where(in_first, queries, q_parts[step * n_parts + 1][...])
        scores = lax.dot_general(
            queries, keys_all[...], (((1,), (1,)), ((), ())), preferred_element_type=jnp.float32
        )
        row = lax.broadcasted_iota(jnp.int32, (rows, own_rows), 0) + first
        column = lax.broadcasted_iota(jnp.int32, (rows, own_rows), 1)
        own = jnp.where(column <= row, scores[:, cross:], -1e30)
        free = scores[:, :cross]
        largest = jnp.maximum(
            jnp.max(free, axis=1, keepdims=True), jnp.max(own, axis=1, keepdims=True)
        )
        free = jnp.exp2((free - largest) * scale)
        own = jnp.exp2((own - largest) * scale)
        total = jnp.sum(free, axis=1, keepdims=True) + jnp.sum(own, axis=1, keepdims=True)
        mixed = jnp.dot(
            free.astype(jnp.bfloat16), values_all[:cross, :], preferred_element_type=jnp.float32
        ) + jnp.dot(
            own.astype(jnp.bfloat16), values_all[cross:, :], preferred_element_type=jnp.float32
        )
        position = lax.broadcasted_iota(jnp.int32, (rows, head), 0) + first
        mixed = jnp.where(position < length_ref[0], mixed / total, 0.0)
        o_ref[:, step * head : (step + 1) * head] = mixed.astype(jnp.bfloat16)


def attention(place, rows, heads, lengths, queries, own, others):
    n_parts = len(own)
    part_rows, width = queries[0].shape
    head = own[0].shape[1] // 2
    picks = others[0].shape[0]
    reach = n_parts * part_rows + len(others) * picks
    per_step = 2
    per_part = part_rows // rows

    def query_spec(step, part):
        def place_of(i, p, h, n):
            at = jnp.clip(p[0] - part * per_part, 0, per_part - 1)
            return (at, h[per_step * i + step])

        return pl.BlockSpec((rows, head), place_of)

    return pl.pallas_call(
        functools.partial(attention_kernel, n_parts, len(others), per_step),
        grid_spec=pltpu.PrefetchScalarGridSpec(
            num_scalar_prefetch=3,
            grid=(width // head // per_step,),
            in_specs=[query_spec(s, p) for s in range(per_step) for p in range(n_parts)]
            + [whole(part_rows, 2 * head) for _ in own]
            + [whole(picks, 2 * head) for _ in others],
            out_specs=pl.BlockSpec((rows, per_step * head), lambda i, p, h, n: (0, i)),
            scratch_shapes=[
                pltpu.VMEM((reach, head), jnp.bfloat16),
                pltpu.VMEM((reach, head), jnp.bfloat16),
            ],
        ),
        out_shape=jax.ShapeDtypeStruct((rows, width), jnp.bfloat16),
        compiler_params=params(),
        name="attention",
    )(place, heads, lengths, *(q for _ in range(per_step) for q in queries), *own, *others)


def mix_kernel(own_ref, sent_ref, w_ref, *refs):
    pieces, out_ref = refs[:-1], refs[-1]
    sent_w = jnp.concatenate([ref[...] for ref in pieces], axis=0)
    total = jnp.dot(own_ref[...], w_ref[...], preferred_element_type=jnp.float32)
    total = total + jnp.dot(sent_ref[...], sent_w, preferred_element_type=jnp.float32)
    out_ref[...] = total.astype(out_ref.dtype)


def mix(own, sent, w_own, pieces, tile, dtype):
    rows, depth = own.shape
    width = w_own.shape[1]
    column = lambda height: pl.BlockSpec((height, tile), lambda i: (0, i))
    return pl.pallas_call(
        mix_kernel,
        grid=(width // tile,),
        in_specs=[whole(rows, depth), whole(rows, depth), column(depth)]
        + [column(piece.shape[0]) for piece in pieces],
        out_specs=column(rows),
        out_shape=jax.ShapeDtypeStruct((rows, width), dtype),
        compiler_params=params(),
        name="mix",
    )(own, sent, w_own, *pieces)


def shards(hidden_in, lengths, summary_pos, w_query, w_key, w_value, w_out, q_gain, k_gain):
    rows_here = hidden_in.shape[0]
    head_width = q_gain.shape[0]
    heads_here = w_query.shape[1] // head_width
    place = lax.axis_index("tensor")
    cand = lax.axis_index("cand")
    n_cand = lax.axis_size("cand")
    assert lax.axis_size("tensor") == 4 and w_key.shape[1] == head_width

    def swap(array):
        return lax.ppermute(array, "tensor", [(0, 1), (1, 0), (2, 3), (3, 2)])

    def across(array):
        return lax.ppermute(array, "tensor", [(1, 2), (2, 1)])

    def outward(array):
        return lax.ppermute(array, "tensor", [(1, 0), (2, 3)])

    def inward(array):
        return lax.ppermute(array, "tensor", [(0, 1), (3, 2)])

    def between(array, offset):
        return lax.ppermute(array, "cand", [(i, i ^ offset) for i in range(n_cand)])

    low = place < 2
    inner = (place == 1) | (place == 2)
    near = jnp.bitwise_xor(place, 1)
    third = jnp.where(low, 2, 1)
    last = jnp.where(low, 3, 0)
    index = lambda block: block.astype(jnp.int32).reshape(1)

    w_kv = jnp.concatenate([w_key, w_value], axis=1)
    cosine, sine = rope_tables(rows_here, head_width)
    half = rows_here // 2

    from_near, from_mid = lax.optimization_barrier((swap(hidden_in), across(hidden_in)))
    to_outer = outward(from_mid)
    to_inner = [across(lax.slice_in_dim(from_near, i * half, (i + 1) * half)) for i in (0, 1)]
    end = [outward(array) for array in to_inner]

    share = w_out.shape[0] // n_cand
    spread = n_cand == 8 and share == head_width

    def eighth(offset, cue):
        start = jnp.bitwise_xor(cand, offset) * share
        piece = lax.dynamic_slice_in_dim(w_out, start, share, 0)
        return inward(after(piece, cue))

    if spread:
        pieces = {0: eighth(0, from_near), 6: eighth(6, to_inner[0])}
        pieces[2], pieces[4] = between(pieces[0], 2), between(pieces[0], 4)
        pieces[1] = between(after(pieces[0], end[0]), 1)
        moved = jnp.bitwise_xor(cand, jnp.array(OFFSETS, jnp.int32))
        heads = jnp.where(inner, jnp.arange(heads_here, dtype=jnp.int32), moved)
    else:
        pieces = {0: lax.all_gather(eighth(0, from_near), "cand", axis=0, tiled=True)}
        heads = jnp.arange(heads_here, dtype=jnp.int32)

    steps = [(place, [[hidden_in]]), (near, [[from_near]])]
    steps.append((third, [[from_mid, to_outer]]))
    acc_q = acc_kv = None
    for block, parts in steps:
        acc_kv = partial_projection(index(block), parts, w_kv, acc_kv, 2 * head_width)
        acc_q = partial_projection(index(block), parts, w_query, acc_q, 4 * head_width)
    acc_kv, acc_q = lax.optimization_barrier((acc_kv, acc_q))

    final = [[a, b] for a, b in zip(to_inner, end)]
    tables = (cosine, sine)
    k_gain, q_gain = k_gain[None], q_gain[None]
    (own_first,) = keys_values(index(last), final[0], 0, w_kv, acc_kv, k_gain, *tables)
    first_queries = queries_of(index(last), final[0], 0, w_query, acc_q, q_gain, *tables)
    acc_kv = after(acc_kv, first_queries)
    own_second, summary = keys_values(
        index(last), final[1], 1, w_kv, acc_kv, k_gain, *tables, [own_first], summary_pos.reshape(-1, 1)
    )
    own = [own_first, own_second]
    summary, pieces = lax.optimization_barrier((summary, pieces))
    others = [between(summary, offset) for offset in range(1, n_cand)]
    second_queries = queries_of(index(last), final[1], 1, w_query, acc_q, q_gain, *tables)
    queries = [first_queries, second_queries]
    if spread:
        for offset in (6, 2, 4):
            pieces[offset ^ 1] = between(after(pieces[offset], (others, second_queries)), 1)
        pieces = [pieces[offset] for offset in OFFSETS]
    else:
        pieces = list(pieces.values())

    part = rows_here // 4
    columns = w_out.shape[1]
    tile = columns // 10

    def attend(where, rows):
        attended = attention(index(where), rows, heads, lengths, queries, own, others)
        return attended, inward(attended)

    def mixed(rows, dtype):
        return mix(*rows, w_out, pieces, columns // 10, dtype)

    far_rows = attend(last, part)
    third_rows = attend(after(third, far_rows[0]), part)
    far_rows = (after(far_rows[0], third_rows[0]), far_rows[1])
    far = mixed(far_rows, jnp.bfloat16)
    third_rows = (after(third_rows[0], far), third_rows[1])
    far_inner = mixed(third_rows, jnp.bfloat16)
    rest_rows = attend(after(place // 2, far_inner), 2 * part)
    far, far_inner = across(far), across(far_inner)
    rest = mixed(rest_rows, jnp.float32)
    outer_at = jnp.where(low, 0, part)
    outer_rest = lax.dynamic_slice_in_dim(rest, outer_at, part, 0)
    inner_rest = lax.dynamic_slice_in_dim(rest, part - outer_at, part, 0)
    sent = outward((outer_rest + far).astype(jnp.bfloat16))
    kept = (inner_rest + far_inner).astype(jnp.bfloat16)
    return jnp.where(inner, kept, sent)


def solution(mesh):
    return jax.shard_map(
        shards,
        mesh=mesh,
        in_specs=(
            P("cand", "tensor"),
            P("cand"),
            P("cand", None),
            P(None, "tensor"),
            P(None, "tensor"),
            P(None, "tensor"),
            P("tensor", None),
            P(),
            P(),
        ),
        out_specs=P(("cand", "tensor"), None),
        check_vma=False,
    )
```

```python
import functools

import jax
import jax.numpy as jnp
from jax import lax
from jax.experimental import pallas as pl
from jax.experimental.pallas import tpu as pltpu
from jax.sharding import PartitionSpec as P

VMEM_LIMIT = 28 * 1024 * 1024
LOG2E = 1.4426950408889634


def rope_tables(rows, width):
    half_width = width // 2
    frequency = 1000000.0 ** (-(jnp.arange(half_width, dtype=jnp.float32) * 2.0 / width))
    angle = jnp.arange(rows, dtype=jnp.float32)[:, None] * frequency[None, :]
    cosine, sine = jnp.cos(angle), jnp.sin(angle)
    return (
        jnp.concatenate([cosine, cosine], axis=1),
        jnp.concatenate([-sine, sine], axis=1),
    )


def norm_rope(vectors, gain, cosine, sine):
    scale = lax.rsqrt(jnp.mean(vectors * vectors, axis=-1, keepdims=True) + 1e-06)
    vectors = vectors * scale * gain
    return vectors * cosine + pltpu.roll(vectors, vectors.shape[-1] // 2, 1) * sine


def params():
    return pltpu.CompilerParams(vmem_limit_bytes=VMEM_LIMIT)


def after(array, cue):
    return lax.optimization_barrier((array, cue))[0]


def whole(*shape):
    return pl.BlockSpec(shape, lambda *_: (0,) * len(shape))


def summed(refs):
    total = refs[0][...]
    for ref in refs[1:]:
        total = total + ref[...]
    return total


def partial_kernel(counts, with_acc, block_ref, *refs):
    rows = []
    for count in counts:
        rows.append(summed(refs[:count]))
        refs = refs[count:]
    w_ref, out_ref = refs[0], refs[-1]
    start = 0
    for hidden in rows:
        stop = start + hidden.shape[0]
        product = jnp.dot(hidden, w_ref[...], preferred_element_type=jnp.float32)
        if with_acc:
            product = product + refs[1][start:stop, :]
        out_ref[start:stop, :] = product
        start = stop


def partial_projection(block, parts, weights, acc, tile):
    features = parts[0][0].shape[1]
    rows = sum(part[0].shape[0] for part in parts)
    width = weights.shape[1]
    arrivals = [array for part in parts for array in part]
    in_specs = [whole(*array.shape) for array in arrivals]
    in_specs.append(pl.BlockSpec((features, tile), lambda i, b: (b[0], i)))
    operands = [*arrivals, weights]
    if acc is not None:
        in_specs.append(pl.BlockSpec((rows, tile), lambda i, b: (0, i)))
        operands.append(acc)
    return pl.pallas_call(
        functools.partial(partial_kernel, [len(part) for part in parts], acc is not None),
        grid_spec=pltpu.PrefetchScalarGridSpec(
            num_scalar_prefetch=1,
            grid=(width // tile,),
            in_specs=in_specs,
            out_specs=pl.BlockSpec((rows, tile), lambda i, b: (0, i)),
        ),
        out_shape=jax.ShapeDtypeStruct((rows, width), jnp.float32),
        compiler_params=params(),
        name="partial_projection",
    )(block, *operands)


def keys_values_kernel(count, head, block_ref, *refs):
    hidden = summed(refs[:count])
    w_ref, acc_ref, gain_ref, cos_ref, sin_ref, out_ref = refs[count:]
    proj = acc_ref[...] + jnp.dot(hidden, w_ref[...], preferred_element_type=jnp.float32)
    keys = norm_rope(proj[:, :head], gain_ref[...], cos_ref[...], sin_ref[...])
    out_ref[:, :head] = keys.astype(jnp.bfloat16)
    out_ref[:, head:] = proj[:, head:].astype(jnp.bfloat16)


def last_keys_values_kernel(count, head, n_before, block_ref, *refs):
    before, (pos_ref, summary_ref) = refs[:n_before], (refs[n_before], refs[-1])
    refs = refs[n_before + 1 : -1]
    keys_values_kernel(count, head, block_ref, *refs)
    out_ref = refs[-1]
    picks = pos_ref.shape[0]
    picked, start = None, 0
    for ref in (*before, out_ref):
        rows = ref.shape[0]
        column = lax.broadcasted_iota(jnp.int32, (picks, rows), 1) + start
        chosen = jnp.where(column == pos_ref[...], 1.0, 0.0).astype(jnp.bfloat16)
        found = jnp.dot(chosen, ref[...], preferred_element_type=jnp.float32)
        picked = found if picked is None else picked + found
        start += rows
    summary_ref[...] = picked.astype(jnp.bfloat16)


def keys_values(block, hidden, part, weights, acc, gain, cosine, sine, before=(), positions=None):
    rows, features = hidden[0].shape
    head = gain.shape[1]
    row_part = lambda width: pl.BlockSpec((rows, width), lambda i, b: (part, 0))
    in_specs = [whole(rows, features) for _ in hidden] + [
        pl.BlockSpec((features, 2 * head), lambda i, b: (b[0], 0)),
        row_part(2 * head),
        whole(1, head),
        row_part(head),
        row_part(head),
    ]
    operands = [*hidden, weights, acc, gain, cosine, sine]
    out_shape = [jax.ShapeDtypeStruct((rows, 2 * head), jnp.bfloat16)]
    kernel = functools.partial(keys_values_kernel, len(hidden), head)
    if positions is not None:
        picks = positions.shape[0]
        in_specs = [whole(*array.shape) for array in (*before, positions)] + in_specs
        operands = [*before, positions, *operands]
        out_shape.append(jax.ShapeDtypeStruct((picks, 2 * head), jnp.bfloat16))
        kernel = functools.partial(last_keys_values_kernel, len(hidden), head, len(before))
    return pl.pallas_call(
        kernel,
        grid_spec=pltpu.PrefetchScalarGridSpec(
            num_scalar_prefetch=1,
            grid=(1,),
            in_specs=in_specs,
            out_specs=[whole(*shape.shape) for shape in out_shape],
        ),
        out_shape=out_shape,
        compiler_params=params(),
        name="keys_values",
    )(block, *operands)


def queries_kernel(count, head, block_ref, *refs):
    hidden = summed(refs[:count])
    w_ref, acc_ref, gain_ref, cos_ref, sin_ref, q_ref = refs[count:]
    proj = acc_ref[...] + jnp.dot(hidden, w_ref[...], preferred_element_type=jnp.float32)
    for start in range(0, proj.shape[1], head):
        one = norm_rope(proj[:, start : start + head], gain_ref[...], cos_ref[...], sin_ref[...])
        q_ref[:, start : start + head] = one.astype(jnp.bfloat16)


def queries_of(block, hidden, part, weights, acc, gain, cosine, sine):
    rows, features = hidden[0].shape
    head = gain.shape[1]
    width = weights.shape[1]
    tile = 4 * head
    row_part = pl.BlockSpec((rows, head), lambda i, b: (part, 0))
    return pl.pallas_call(
        functools.partial(queries_kernel, len(hidden), head),
        grid_spec=pltpu.PrefetchScalarGridSpec(
            num_scalar_prefetch=1,
            grid=(width // tile,),
            in_specs=[whole(rows, features) for _ in hidden]
            + [
                pl.BlockSpec((features, tile), lambda i, b: (b[0], i)),
                pl.BlockSpec((rows, tile), lambda i, b: (part, i)),
                whole(1, head),
                row_part,
                row_part,
            ],
            out_specs=pl.BlockSpec((rows, tile), lambda i, b: (0, i)),
        ),
        out_shape=jax.ShapeDtypeStruct((rows, width), jnp.bfloat16),
        compiler_params=params(),
        name="queries",
    )(block, *hidden, weights, acc, gain, cosine, sine)


def attention_kernel(n_parts, n_others, stack, place_ref, length_ref, *refs):
    q_parts, refs = refs[:n_parts], refs[n_parts:]
    own_parts, refs = refs[:n_parts], refs[n_parts:]
    others, refs = refs[:n_others], refs[n_others:]
    o_ref, keys_all, values_all = refs
    part_rows, width = own_parts[0].shape
    head = width // 2
    picks = others[0].shape[0]
    cross = n_others * picks
    rows = o_ref.shape[0]

    start = 0
    for ref in (*others, *own_parts):
        stop = start + ref.shape[0]
        keys_all[start:stop, :] = ref[:, :head]
        values_all[start:stop, :] = ref[:, head:]
        start = stop

    scale = head ** (-0.5) * LOG2E
    first = place_ref[0] * rows
    own_rows = n_parts * part_rows
    offset = pl.multiple_of(lax.rem(first, part_rows), rows)
    row = lax.broadcasted_iota(jnp.int32, (rows, own_rows), 0) + first
    column = lax.broadcasted_iota(jnp.int32, (rows, own_rows), 1)
    allowed = jnp.concatenate([column <= row] * stack, axis=0)
    position = lax.broadcasted_iota(jnp.int32, (rows, head), 0) + first
    kept = jnp.concatenate([position < length_ref[0]] * stack, axis=0)
    for left in range(0, o_ref.shape[1], stack * head):
        lanes = [slice(left + i * head, left + (i + 1) * head) for i in range(stack)]
        queries = [q_parts[0][pl.ds(offset, rows), lane] for lane in lanes]
        for part in range(1, n_parts):
            here = first >= part * part_rows
            queries = [
                jnp.where(here, q_parts[part][pl.ds(offset, rows), lane], query)
                for lane, query in zip(lanes, queries)
            ]
        scores = lax.dot_general(
            jnp.concatenate(queries, axis=0),
            keys_all[...],
            (((1,), (1,)), ((), ())),
            preferred_element_type=jnp.float32,
        )
        own = jnp.where(allowed, scores[:, cross:], -1e30)
        free = scores[:, :cross]
        largest = jnp.maximum(
            jnp.max(free, axis=1, keepdims=True), jnp.max(own, axis=1, keepdims=True)
        )
        free = jnp.exp2((free - largest) * scale)
        own = jnp.exp2((own - largest) * scale)
        total = jnp.sum(free, axis=1, keepdims=True) + jnp.sum(own, axis=1, keepdims=True)
        mixed = jnp.dot(
            free.astype(jnp.bfloat16), values_all[:cross, :], preferred_element_type=jnp.float32
        ) + jnp.dot(
            own.astype(jnp.bfloat16), values_all[cross:, :], preferred_element_type=jnp.float32
        )
        mixed = jnp.where(kept, mixed / total, 0.0).astype(jnp.bfloat16)
        for index, lane in enumerate(lanes):
            o_ref[:, lane] = mixed[index * rows : (index + 1) * rows, :]


def attention(place, rows, lengths, queries, own, others):
    n_parts = len(own)
    part_rows, width = queries[0].shape
    head = own[0].shape[1] // 2
    picks = others[0].shape[0]
    reach = n_parts * part_rows + len(others) * picks
    stack = 512 // rows
    return pl.pallas_call(
        functools.partial(attention_kernel, n_parts, len(others), stack),
        grid_spec=pltpu.PrefetchScalarGridSpec(
            num_scalar_prefetch=2,
            grid=(1,),
            in_specs=[whole(*array.shape) for array in (*queries, *own, *others)],
            out_specs=whole(rows, width),
            scratch_shapes=[
                pltpu.VMEM((reach, head), jnp.bfloat16),
                pltpu.VMEM((reach, head), jnp.bfloat16),
            ],
        ),
        out_shape=jax.ShapeDtypeStruct((rows, width), jnp.bfloat16),
        compiler_params=params(),
        name="attention",
    )(place, lengths, *queries, *own, *others)


def mix_kernel(own_ref, w_ref, out_ref):
    total = jnp.dot(own_ref[...], w_ref[...], preferred_element_type=jnp.float32)
    out_ref[...] = total.astype(out_ref.dtype)


def mix(attended, w_out, first, tiles, tile):
    rows, depth = attended.shape
    return pl.pallas_call(
        mix_kernel,
        grid=(tiles,),
        in_specs=[whole(rows, depth), pl.BlockSpec((depth, tile), lambda i: (0, i + first))],
        out_specs=pl.BlockSpec((rows, tile), lambda i: (0, i)),
        out_shape=jax.ShapeDtypeStruct((rows, tiles * tile), jnp.bfloat16),
        compiler_params=params(),
        name="mix",
    )(attended, w_out)


def shards(hidden_in, lengths, summary_pos, w_query, w_key, w_value, w_out, q_gain, k_gain):
    rows_here = hidden_in.shape[0]
    head_width = q_gain.shape[0]
    place = lax.axis_index("tensor")
    n_cand = lax.axis_size("cand")
    assert lax.axis_size("tensor") == 4 and w_key.shape[1] == head_width

    def swap(array):
        return lax.ppermute(array, "tensor", [(0, 1), (1, 0), (2, 3), (3, 2)])

    def across(array):
        return lax.ppermute(array, "tensor", [(1, 2), (2, 1)])

    def outward(array):
        return lax.ppermute(array, "tensor", [(1, 0), (2, 3)])

    def inward(array):
        return lax.ppermute(array, "tensor", [(0, 1), (3, 2)])

    def between(array, offset):
        return lax.ppermute(array, "cand", [(i, i ^ offset) for i in range(n_cand)])

    low = place < 2
    near = jnp.bitwise_xor(place, 1)
    third = jnp.where(low, 2, 1)
    last = jnp.where(low, 3, 0)
    index = lambda block: block.astype(jnp.int32).reshape(1)

    w_kv = jnp.concatenate([w_key, w_value], axis=1)
    cosine, sine = rope_tables(rows_here, head_width)
    half = rows_here // 2

    def project(accs, block, arrivals):
        return (
            partial_projection(index(block), [arrivals], w_kv, accs[0], 2 * head_width),
            partial_projection(index(block), [arrivals], w_query, accs[1], 4 * head_width),
        )

    from_near, from_mid = swap(hidden_in), across(hidden_in)
    accs = project((None, None), place, [hidden_in])
    from_near, from_mid, accs = lax.optimization_barrier((from_near, from_mid, accs))
    to_outer = outward(from_mid)
    to_inner = [across(lax.slice_in_dim(from_near, i * half, (i + 1) * half)) for i in (0, 1)]
    accs = project(accs, near, [from_near])
    to_inner[0], accs = lax.optimization_barrier((to_inner[0], accs))
    end = [outward(array) for array in to_inner]
    accs = project(accs, third, [from_mid, to_outer])
    acc_kv, acc_q = lax.optimization_barrier(accs)

    final = [[a, b] for a, b in zip(to_inner, end)]
    tables = (cosine, sine)
    k_gain, q_gain = k_gain[None], q_gain[None]
    (own_first,) = keys_values(index(last), final[0], 0, w_kv, acc_kv, k_gain, *tables)
    first_queries = queries_of(index(last), final[0], 0, w_query, acc_q, q_gain, *tables)
    acc_kv = after(acc_kv, first_queries)
    own_second, summary = keys_values(
        index(last), final[1], 1, w_kv, acc_kv, k_gain, *tables, [own_first], summary_pos.reshape(-1, 1)
    )
    own = [own_first, own_second]
    others = [between(summary, offset) for offset in range(1, n_cand)]
    second_queries = queries_of(index(last), final[1], 1, w_query, acc_q, q_gain, *tables)
    queries = [first_queries, second_queries]

    part = rows_here // 4
    tiles = 5
    tile = w_out.shape[1] // (2 * tiles)

    def attend(where, rows):
        return attention(index(where), rows, lengths, queries, own, others)

    def mixed(rows):
        return [mix(rows, w_out, first, tiles, tile) for first in (0, tiles)]

    def added(*arrays):
        total = arrays[0].astype(jnp.float32)
        for array in arrays[1:]:
            total = total + array.astype(jnp.float32)
        return total.astype(jnp.bfloat16)

    far = mixed(attend(last, part))
    third_rows = attend(after(third, far), part)
    mid = mixed(third_rows)
    rest_rows = attend(after(place // 2, mid), 2 * part)
    far_in, mid_in = [inward(a) for a in far], [inward(a) for a in mid]
    outer_first = lax.rem(near, 2) * part
    neighbour = mixed(lax.dynamic_slice_in_dim(rest_rows, outer_first, part, 0))
    kept = mixed(lax.dynamic_slice_in_dim(rest_rows, part - outer_first, part, 0))
    result = []
    for i in (0, 1):
        far_sum = across(added(far[i], far_in[i]))
        mid_sum = across(added(mid[i], mid_in[i]))
        near_sum = swap(added(neighbour[i], far_sum))
        result.append(added(kept[i], near_sum, mid_sum))
    return jnp.concatenate(result, axis=1)


def solution(mesh):
    return jax.shard_map(
        shards,
        mesh=mesh,
        in_specs=(
            P("cand", "tensor"),
            P("cand"),
            P("cand", None),
            P(None, "tensor"),
            P(None, "tensor"),
            P(None, "tensor"),
            P("tensor", None),
            P(),
            P(),
        ),
        out_specs=P(("cand", "tensor"), None),
        check_vma=False,
    )
```

```python
import functools

import jax
import jax.numpy as jnp
import numpy as np
from jax import lax
from jax.experimental import pallas as pl
from jax.experimental.pallas import tpu as pltpu
from jax.sharding import PartitionSpec as P

MIB = 1024 * 1024
LOG2E = 1.4426950408889634
OWN, NEAR, THIRD, LAST = range(4)


def rope_tables(rows, width):
    half_width = width // 2
    frequency = (1000000.0 ** (-(np.arange(half_width) * 2.0 / width))).astype(np.float32)
    angle = np.arange(rows, dtype=np.float32)[:, None] * frequency[None, :]
    angle = angle.astype(np.float64)
    cosine, sine = np.cos(angle), np.sin(angle)
    return (
        jnp.asarray(np.concatenate([cosine, cosine], axis=1).astype(np.float32)),
        jnp.asarray(np.concatenate([-sine, sine], axis=1).astype(np.float32)),
    )


def norm_rope(vectors, gain, cosine, sine):
    scale = lax.rsqrt(jnp.mean(vectors * vectors, axis=-1, keepdims=True) + 1e-06)
    vectors = vectors * scale * gain
    return vectors * cosine + pltpu.roll(vectors, vectors.shape[-1] // 2, 1) * sine


def params(mebibytes):
    return pltpu.CompilerParams(vmem_limit_bytes=mebibytes * MIB)


def cost(flops):
    return pl.CostEstimate(flops=flops, bytes_accessed=1, transcendentals=0)


def after(array, cue):
    return lax.optimization_barrier((array, cue))[0]


def whole(*shape):
    return pl.BlockSpec(shape, lambda *_: (0,) * len(shape))


def summed(refs):
    total = refs[0][...]
    for ref in refs[1:]:
        total = total + ref[...]
    return total


def partial_kernel(counts, with_acc, places_ref, *refs):
    rows = []
    for count in counts:
        rows.append(summed(refs[:count]))
        refs = refs[count:]
    hidden = jnp.concatenate(rows, axis=0) if len(rows) > 1 else rows[0]
    weights, outs = refs[:3], refs[-3:]
    accs = refs[3:6] if with_acc else (None,) * 3
    step = pl.program_id(0)

    def add(w_ref, acc_ref, out_ref):
        product = jnp.dot(hidden, w_ref[...], preferred_element_type=jnp.float32)
        out_ref[...] = product if acc_ref is None else product + acc_ref[...]

    add(weights[0], accs[0], outs[0])

    @pl.when(step == 0)
    def _():
        add(weights[1], accs[1], outs[1])
        add(weights[2], accs[2], outs[2])


def partial_projection(places, slot, parts, weights, accs):
    features = parts[0][0].shape[1]
    rows = sum(part[0].shape[0] for part in parts)
    arrivals = [array for part in parts for array in part]
    widths = [weight.shape[1] for weight in weights]
    tile = 512
    column = lambda height: pl.BlockSpec((height, tile), lambda i, p: (0, i))
    per_array = lambda height: [column(height), whole(height, widths[1]), whole(height, widths[2])]
    block = lambda width: pl.BlockSpec((features, width), lambda i, p: (p[slot], 0))
    in_specs = [whole(*array.shape) for array in arrivals]
    in_specs.append(pl.BlockSpec((features, tile), lambda i, p: (p[slot], i)))
    in_specs += [block(widths[1]), block(widths[2])]
    operands = [*arrivals, *weights]
    if accs is not None:
        in_specs += per_array(rows)
        operands += accs
    return pl.pallas_call(
        functools.partial(partial_kernel, [len(part) for part in parts], accs is not None),
        grid_spec=pltpu.PrefetchScalarGridSpec(
            num_scalar_prefetch=1,
            grid=(widths[0] // tile,),
            in_specs=in_specs,
            out_specs=per_array(rows),
        ),
        out_shape=[jax.ShapeDtypeStruct((rows, width), jnp.float32) for width in widths],
        compiler_params=params(20),
        cost_estimate=cost(1),
        name="partial_projection",
    )(places, *operands)


def keys_values_kernel(count, n_before, places_ref, *refs):
    before, refs = refs[:n_before], refs[n_before:]
    hidden = summed(refs[:count])
    wk_ref, wv_ref, acck_ref, accv_ref, gain_ref, cos_ref, sin_ref = refs[count : count + 7]
    refs = refs[count + 7 :]
    head = gain_ref.shape[1]
    out_ref = refs[0] if n_before == 0 else refs[1]
    keys = acck_ref[...] + jnp.dot(hidden, wk_ref[...], preferred_element_type=jnp.float32)
    values = accv_ref[...] + jnp.dot(hidden, wv_ref[...], preferred_element_type=jnp.float32)
    keys = norm_rope(keys, gain_ref[...], cos_ref[...], sin_ref[...])
    out_ref[:, :head] = keys.astype(jnp.bfloat16)
    out_ref[:, head:] = values.astype(jnp.bfloat16)
    if n_before:
        pos_ref, summary_ref = refs[0], refs[2]
        picks = pos_ref.shape[1]
        picked, start = None, 0
        for ref in (*before, out_ref):
            rows = ref.shape[0]
            row = lax.broadcasted_iota(jnp.int32, (rows, picks), 0) + start
            chosen = jnp.where(row == pos_ref[...], 1.0, 0.0).astype(jnp.bfloat16)
            found = lax.dot_general(
                chosen, ref[...], (((0,), (0,)), ((), ())), preferred_element_type=jnp.float32
            )
            picked = found if picked is None else picked + found
            start += rows
        summary_ref[...] = picked.astype(jnp.bfloat16)


def keys_values(places, hidden, part, weights, accs, gain, cosine, sine, before=(), positions=None):
    rows, features = hidden[0].shape
    head = gain.shape[1]
    row_part = pl.BlockSpec((rows, head), lambda i, p: (part, 0))
    block = pl.BlockSpec((features, head), lambda i, p: (p[LAST], 0))
    in_specs = [whole(*array.shape) for array in (*before, *hidden)]
    in_specs += [block, block, row_part, row_part, whole(1, head), row_part, row_part]
    operands = [*before, *hidden, *weights, *accs, gain, cosine, sine]
    out_shape = [jax.ShapeDtypeStruct((rows, 2 * head), jnp.bfloat16)]
    if before:
        in_specs.append(whole(*positions.shape))
        operands.append(positions)
        out_shape.append(jax.ShapeDtypeStruct((positions.shape[1], 2 * head), jnp.bfloat16))
    return pl.pallas_call(
        functools.partial(keys_values_kernel, len(hidden), len(before)),
        grid_spec=pltpu.PrefetchScalarGridSpec(
            num_scalar_prefetch=1,
            grid=(1,),
            in_specs=in_specs,
            out_specs=[whole(*shape.shape) for shape in out_shape],
        ),
        out_shape=out_shape,
        compiler_params=params(12),
        cost_estimate=cost(1),
        name="keys_values",
    )(places, *operands)


def queries_kernel(count, places_ref, *refs):
    hidden = summed(refs[:count])
    w_ref, acc_ref, gain_ref, cos_ref, sin_ref, q_ref = refs[count:]
    head = gain_ref.shape[1]
    proj = acc_ref[...] + jnp.dot(hidden, w_ref[...], preferred_element_type=jnp.float32)
    for start in range(0, proj.shape[1], head):
        one = norm_rope(proj[:, start : start + head], gain_ref[...], cos_ref[...], sin_ref[...])
        q_ref[:, start : start + head] = one.astype(jnp.bfloat16)


def queries_of(places, hidden, part, weights, acc, gain, cosine, sine):
    rows, features = hidden[0].shape
    head = gain.shape[1]
    width = weights.shape[1]
    tile = 4 * head
    row_part = pl.BlockSpec((rows, head), lambda i, p: (part, 0))
    return pl.pallas_call(
        functools.partial(queries_kernel, len(hidden)),
        grid_spec=pltpu.PrefetchScalarGridSpec(
            num_scalar_prefetch=1,
            grid=(width // tile,),
            in_specs=[whole(rows, features) for _ in hidden]
            + [
                pl.BlockSpec((features, tile), lambda i, p: (p[LAST], i)),
                pl.BlockSpec((rows, tile), lambda i, p: (part, i)),
                whole(1, head),
                row_part,
                row_part,
            ],
            out_specs=pl.BlockSpec((rows, tile), lambda i, p: (0, i)),
        ),
        out_shape=jax.ShapeDtypeStruct((rows, width), jnp.bfloat16),
        compiler_params=params(12),
        cost_estimate=cost(1),
        name="queries",
    )(places, *hidden, weights, acc, gain, cosine, sine)


def attention_kernel(slots, n_parts, n_others, stack, places_ref, length_ref, *refs):
    q_parts, refs = refs[:n_parts], refs[n_parts:]
    own_parts, refs = refs[:n_parts], refs[n_parts:]
    others, refs = refs[:n_others], refs[n_others:]
    o_refs, (keys_all, values_all) = refs[:-2], refs[-2:]
    part_rows, width = own_parts[0].shape
    head = width // 2
    picks = others[0].shape[0]
    cross = n_others * picks
    rows = o_refs[0].shape[0]

    start = 0
    for ref in (*others, *own_parts):
        stop = start + ref.shape[0]
        keys_all[start:stop, :] = ref[:, :head]
        values_all[start:stop, :] = ref[:, head:]
        start = stop

    scale = head ** (-0.5) * LOG2E
    own_rows = n_parts * part_rows
    for slot, o_ref in zip(slots, o_refs):
        first = places_ref[slot] * rows
        offset = pl.multiple_of(lax.rem(first, part_rows), rows)
        row = lax.broadcasted_iota(jnp.int32, (rows, own_rows), 0) + first
        column = lax.broadcasted_iota(jnp.int32, (rows, own_rows), 1)
        allowed = jnp.concatenate([column <= row] * stack, axis=0)
        position = lax.broadcasted_iota(jnp.int32, (rows, head), 0) + first
        kept = jnp.concatenate([position < length_ref[0]] * stack, axis=0)
        for left in range(0, o_ref.shape[1], stack * head):
            lanes = [slice(left + i * head, left + (i + 1) * head) for i in range(stack)]
            queries = [q_parts[0][pl.ds(offset, rows), lane] for lane in lanes]
            for part in range(1, n_parts):
                here = first >= part * part_rows
                queries = [
                    jnp.where(here, q_parts[part][pl.ds(offset, rows), lane], query)
                    for lane, query in zip(lanes, queries)
                ]
            scores = lax.dot_general(
                jnp.concatenate(queries, axis=0),
                keys_all[...],
                (((1,), (1,)), ((), ())),
                preferred_element_type=jnp.float32,
            )
            own = jnp.where(allowed, scores[:, cross:], -1e30)
            free = scores[:, :cross]
            largest = jnp.maximum(
                jnp.max(free, axis=1, keepdims=True), jnp.max(own, axis=1, keepdims=True)
            )
            free = jnp.exp2((free - largest) * scale)
            own = jnp.exp2((own - largest) * scale)
            total = jnp.sum(free, axis=1, keepdims=True) + jnp.sum(own, axis=1, keepdims=True)
            mixed = jnp.dot(
                free.astype(jnp.bfloat16), values_all[:cross, :], preferred_element_type=jnp.float32
            ) + jnp.dot(
                own.astype(jnp.bfloat16), values_all[cross:, :], preferred_element_type=jnp.float32
            )
            mixed = jnp.where(kept, mixed / total, 0.0).astype(jnp.bfloat16)
            for index, lane in enumerate(lanes):
                o_ref[:, lane] = mixed[index * rows : (index + 1) * rows, :]


def attention(places, slots, rows, lengths, queries, own, others):
    n_parts = len(own)
    part_rows, width = queries[0].shape
    head = own[0].shape[1] // 2
    picks = others[0].shape[0]
    reach = n_parts * part_rows + len(others) * picks
    return pl.pallas_call(
        functools.partial(attention_kernel, slots, n_parts, len(others), 512 // rows),
        grid_spec=pltpu.PrefetchScalarGridSpec(
            num_scalar_prefetch=2,
            grid=(1,),
            in_specs=[whole(*array.shape) for array in (*queries, *own, *others)],
            out_specs=[whole(rows, width) for _ in slots],
            scratch_shapes=[
                pltpu.VMEM((reach, head), jnp.bfloat16),
                pltpu.VMEM((reach, head), jnp.bfloat16),
            ],
        ),
        out_shape=[jax.ShapeDtypeStruct((rows, width), jnp.bfloat16) for _ in slots],
        compiler_params=params(24 if reach <= 2048 else 56),
        cost_estimate=cost(1),
        name="attention",
    )(places, lengths, *queries, *own, *others)


def mix_kernel(rows_ref, w_ref, out_ref):
    total = jnp.dot(rows_ref[...], w_ref[...], preferred_element_type=jnp.float32)
    out_ref[...] = total.astype(out_ref.dtype)


def mix(attended, w_out, which):
    rows, depth = attended.shape
    width = w_out.shape[1] // 2
    tiles = 5
    tile = width // tiles
    return pl.pallas_call(
        mix_kernel,
        grid=(tiles,),
        in_specs=[
            whole(rows, depth),
            pl.BlockSpec((depth, tile), lambda i: (0, i + which * tiles)),
        ],
        out_specs=pl.BlockSpec((rows, tile), lambda i: (0, i)),
        out_shape=jax.ShapeDtypeStruct((rows, width), jnp.bfloat16),
        compiler_params=params(8),
        cost_estimate=cost(1),
        name="mix",
    )(attended, w_out)


def add_kernel(count, *refs):
    total = refs[0][...].astype(jnp.float32)
    for ref in refs[1:count]:
        total = total + ref[...].astype(jnp.float32)
    refs[-1][...] = total.astype(jnp.bfloat16)


def added(*arrays, half=None, into=None):
    rows, width = arrays[0].shape
    wide = 1 if half is None else 2
    at = half or 0
    operands = list(arrays)
    in_specs = [whole(rows, width) for _ in arrays]
    aliases = {}
    if into is not None:
        operands.append(into)
        in_specs.append(pl.BlockSpec(memory_space=pl.ANY))
        aliases = {len(arrays): 0}
    return pl.pallas_call(
        functools.partial(add_kernel, len(arrays)),
        grid=(1,),
        in_specs=in_specs,
        out_specs=pl.BlockSpec((rows, width), lambda i: (0, at)),
        out_shape=jax.ShapeDtypeStruct((rows, wide * width), jnp.bfloat16),
        input_output_aliases=aliases,
        compiler_params=params(8),
        cost_estimate=cost(1),
        name="added",
    )(*operands)


def shards(hidden_in, lengths, summary_pos, w_query, w_key, w_value, w_out, q_gain, k_gain):
    rows_here = hidden_in.shape[0]
    head_width = q_gain.shape[0]
    place = lax.axis_index("tensor")
    n_cand = lax.axis_size("cand")
    assert lax.axis_size("tensor") == 4 and w_key.shape[1] == head_width

    def swap(array):
        return lax.ppermute(array, "tensor", [(0, 1), (1, 0), (2, 3), (3, 2)])

    def across(array):
        return lax.ppermute(array, "tensor", [(1, 2), (2, 1)])

    def outward(array):
        return lax.ppermute(array, "tensor", [(1, 0), (2, 3)])

    def inward(array):
        return lax.ppermute(array, "tensor", [(0, 1), (3, 2)])

    def between(array, offset):
        return lax.ppermute(array, "cand", [(i, i ^ offset) for i in range(n_cand)])

    low = place < 2
    near = jnp.bitwise_xor(place, 1)
    places = jnp.stack([place, near, jnp.where(low, 2, 1), jnp.where(low, 3, 0)])
    places = places.astype(jnp.int32)
    tables = rope_tables(rows_here, head_width)
    k_gain, q_gain = k_gain[None], q_gain[None]
    weights = [w_query, w_key, w_value]
    half = rows_here // 2

    mine = [lax.slice_in_dim(hidden_in, i * half, (i + 1) * half) for i in (0, 1)]
    from_near, from_mid = [], []
    for array in mine:
        from_near.append(swap(array))
        from_mid.append(across(array))
    accs = partial_projection(places, OWN, [[hidden_in]], weights, None)
    to_inner = [across(array) for array in from_near]
    to_outer = [outward(array) for array in from_mid]
    from_near[1], accs = lax.optimization_barrier((from_near[1], accs))
    accs = partial_projection(places, NEAR, [[a] for a in from_near], weights, accs)
    to_inner[0], accs = lax.optimization_barrier((to_inner[0], accs))
    end = [outward(array) for array in to_inner]
    accs = partial_projection(
        places, THIRD, [[a, b] for a, b in zip(from_mid, to_outer)], weights, accs
    )

    final = [[a, b] for a, b in zip(to_inner, end)]
    (own_first,) = keys_values(places, final[0], 0, weights[1:], accs[1:], k_gain, *tables)
    first_queries = queries_of(places, final[0], 0, w_query, accs[0], q_gain, *tables)
    own_second, summary = keys_values(
        places,
        final[1],
        1,
        weights[1:],
        after(accs[1:], first_queries),
        k_gain,
        *tables,
        [own_first],
        summary_pos,
    )
    own = [own_first, own_second]
    others = [between(summary, offset) for offset in range(1, n_cand)]
    second_queries = queries_of(places, final[1], 1, w_query, accs[0], q_gain, *tables)
    queries = [first_queries, second_queries]

    def attend(slots):
        return attention(places, slots, rows_here // 4, lengths, queries, own, others)

    def mixed(rows):
        return [mix(rows, w_out, which) for which in (0, 1)]

    (far_rows,) = attend((LAST,))
    far = mixed(far_rows)
    places = after(places, far)
    third_rows, near_rows, own_rows = attend((THIRD, NEAR, OWN))
    mid = mixed(third_rows)
    far_in = [inward(array) for array in far]
    mid_in = [inward(array) for array in mid]
    far_sum = [added(far[0], after(far_in[0], mid))]
    near_part = mixed(after(near_rows, far_sum[0]))
    far_sum.append(added(far[1], after(far_in[1], near_part)))
    kept = mixed(after(own_rows, far_sum[1]))
    far_sum = [across(array) for array in far_sum]
    near_sum, mid_sum = [None, None], [None, None]
    cue = kept
    for i in (0, 1):
        near_sum[i] = added(near_part[i], after(far_sum[i], cue))
        mid_sum[i] = added(mid[i], after(mid_in[i], near_sum[i]))
        cue = mid_sum[i]
    near_sum = [swap(array) for array in near_sum]
    mid_sum = [across(array) for array in mid_sum]
    result = added(kept[0], near_sum[0], mid_sum[0], half=0)
    return added(kept[1], near_sum[1], mid_sum[1], half=1, into=result)


def solution(mesh):
    return jax.shard_map(
        shards,
        mesh=mesh,
        in_specs=(
            P("cand", "tensor"),
            P("cand"),
            P("cand", None),
            P(None, "tensor"),
            P(None, "tensor"),
            P(None, "tensor"),
            P("tensor", None),
            P(),
            P(),
        ),
        out_specs=P(("cand", "tensor"), None),
        check_vma=False,
    )
```

```python
import functools

import jax
import jax.numpy as jnp
import numpy as np
from jax import lax
from jax.experimental import pallas as pl
from jax.experimental.pallas import tpu as pltpu
from jax.sharding import PartitionSpec as P

MIB = 1024 * 1024
LOG2E = 1.4426950408889634
OWN, NEAR, THIRD, LAST = range(4)


def rope_tables(rows, width):
    half_width = width // 2
    frequency = (1000000.0 ** (-(np.arange(half_width) * 2.0 / width))).astype(np.float32)
    angle = np.arange(rows, dtype=np.float32)[:, None] * frequency[None, :]
    angle = angle.astype(np.float64)
    cosine, sine = np.cos(angle), np.sin(angle)
    return (
        jnp.asarray(np.concatenate([cosine, cosine], axis=1).astype(np.float32)),
        jnp.asarray(np.concatenate([-sine, sine], axis=1).astype(np.float32)),
    )


def norm_rope(vectors, gain, cosine, sine):
    scale = lax.rsqrt(jnp.mean(vectors * vectors, axis=-1, keepdims=True) + 1e-06)
    vectors = vectors * scale * gain
    return vectors * cosine + pltpu.roll(vectors, vectors.shape[-1] // 2, 1) * sine


def params(mebibytes):
    return pltpu.CompilerParams(vmem_limit_bytes=mebibytes * MIB)


def cost(flops):
    return pl.CostEstimate(flops=flops, bytes_accessed=1, transcendentals=0)


def after(array, cue):
    return lax.optimization_barrier((array, cue))[0]


def whole(*shape):
    return pl.BlockSpec(shape, lambda *_: (0,) * len(shape))


def summed(refs):
    total = refs[0][...]
    for ref in refs[1:]:
        total = total + ref[...]
    return total


def partial_kernel(counts, with_acc, places_ref, *refs):
    rows = []
    for count in counts:
        rows.append(summed(refs[:count]))
        refs = refs[count:]
    hidden = jnp.concatenate(rows, axis=0) if len(rows) > 1 else rows[0]
    weights, outs = refs[:3], refs[-3:]
    accs = refs[3:6] if with_acc else (None,) * 3
    step = pl.program_id(0)

    def add(w_ref, acc_ref, out_ref):
        product = jnp.dot(hidden, w_ref[...], preferred_element_type=jnp.float32)
        out_ref[...] = product if acc_ref is None else product + acc_ref[...]

    add(weights[0], accs[0], outs[0])

    @pl.when(step == 0)
    def _():
        add(weights[1], accs[1], outs[1])
        add(weights[2], accs[2], outs[2])


def partial_projection(places, slot, parts, weights, accs):
    features = parts[0][0].shape[1]
    rows = sum(part[0].shape[0] for part in parts)
    arrivals = [array for part in parts for array in part]
    widths = [weight.shape[1] for weight in weights]
    tile = 512
    column = lambda height: pl.BlockSpec((height, tile), lambda i, p: (0, i))
    per_array = lambda height: [column(height), whole(height, widths[1]), whole(height, widths[2])]
    block = lambda width: pl.BlockSpec((features, width), lambda i, p: (p[slot], 0))
    in_specs = [whole(*array.shape) for array in arrivals]
    in_specs.append(pl.BlockSpec((features, tile), lambda i, p: (p[slot], i)))
    in_specs += [block(widths[1]), block(widths[2])]
    operands = [*arrivals, *weights]
    if accs is not None:
        in_specs += per_array(rows)
        operands += accs
    return pl.pallas_call(
        functools.partial(partial_kernel, [len(part) for part in parts], accs is not None),
        grid_spec=pltpu.PrefetchScalarGridSpec(
            num_scalar_prefetch=1,
            grid=(widths[0] // tile,),
            in_specs=in_specs,
            out_specs=per_array(rows),
        ),
        out_shape=[jax.ShapeDtypeStruct((rows, width), jnp.float32) for width in widths],
        compiler_params=params(20),
        cost_estimate=cost(1),
        name="partial_projection",
    )(places, *operands)


def keys_values_kernel(count, n_before, places_ref, *refs):
    before, refs = refs[:n_before], refs[n_before:]
    hidden = summed(refs[:count])
    wk_ref, wv_ref, acck_ref, accv_ref, gain_ref, cos_ref, sin_ref = refs[count : count + 7]
    refs = refs[count + 7 :]
    head = gain_ref.shape[1]
    out_ref = refs[0] if n_before == 0 else refs[1]
    keys = acck_ref[...] + jnp.dot(hidden, wk_ref[...], preferred_element_type=jnp.float32)
    values = accv_ref[...] + jnp.dot(hidden, wv_ref[...], preferred_element_type=jnp.float32)
    keys = norm_rope(keys, gain_ref[...], cos_ref[...], sin_ref[...])
    out_ref[:, :head] = keys.astype(jnp.bfloat16)
    out_ref[:, head:] = values.astype(jnp.bfloat16)
    if n_before:
        pos_ref, summary_ref = refs[0], refs[2]
        picks = pos_ref.shape[1]
        picked, start = None, 0
        for ref in (*before, out_ref):
            rows = ref.shape[0]
            row = lax.broadcasted_iota(jnp.int32, (rows, picks), 0) + start
            chosen = jnp.where(row == pos_ref[...], 1.0, 0.0).astype(jnp.bfloat16)
            found = lax.dot_general(
                chosen, ref[...], (((0,), (0,)), ((), ())), preferred_element_type=jnp.float32
            )
            picked = found if picked is None else picked + found
            start += rows
        summary_ref[...] = picked.astype(jnp.bfloat16)


def keys_values(places, hidden, part, weights, accs, gain, cosine, sine, before=(), positions=None):
    rows, features = hidden[0].shape
    head = gain.shape[1]
    row_part = pl.BlockSpec((rows, head), lambda i, p: (part, 0))
    block = pl.BlockSpec((features, head), lambda i, p: (p[LAST], 0))
    in_specs = [whole(*array.shape) for array in (*before, *hidden)]
    in_specs += [block, block, row_part, row_part, whole(1, head), row_part, row_part]
    operands = [*before, *hidden, *weights, *accs, gain, cosine, sine]
    out_shape = [jax.ShapeDtypeStruct((rows, 2 * head), jnp.bfloat16)]
    if before:
        in_specs.append(whole(*positions.shape))
        operands.append(positions)
        out_shape.append(jax.ShapeDtypeStruct((positions.shape[1], 2 * head), jnp.bfloat16))
    return pl.pallas_call(
        functools.partial(keys_values_kernel, len(hidden), len(before)),
        grid_spec=pltpu.PrefetchScalarGridSpec(
            num_scalar_prefetch=1,
            grid=(1,),
            in_specs=in_specs,
            out_specs=[whole(*shape.shape) for shape in out_shape],
        ),
        out_shape=out_shape,
        compiler_params=params(12),
        cost_estimate=cost(1),
        name="keys_values",
    )(places, *operands)


def queries_kernel(count, places_ref, *refs):
    hidden = summed(refs[:count])
    w_ref, acc_ref, gain_ref, cos_ref, sin_ref, q_ref = refs[count:]
    head = gain_ref.shape[1]
    proj = acc_ref[...] + jnp.dot(hidden, w_ref[...], preferred_element_type=jnp.float32)
    for start in range(0, proj.shape[1], head):
        one = norm_rope(proj[:, start : start + head], gain_ref[...], cos_ref[...], sin_ref[...])
        q_ref[:, start : start + head] = one.astype(jnp.bfloat16)


def queries_of(places, hidden, part, weights, acc, gain, cosine, sine):
    rows, features = hidden[0].shape
    head = gain.shape[1]
    width = weights.shape[1]
    tile = 4 * head
    row_part = pl.BlockSpec((rows, head), lambda i, p: (part, 0))
    return pl.pallas_call(
        functools.partial(queries_kernel, len(hidden)),
        grid_spec=pltpu.PrefetchScalarGridSpec(
            num_scalar_prefetch=1,
            grid=(width // tile,),
            in_specs=[whole(rows, features) for _ in hidden]
            + [
                pl.BlockSpec((features, tile), lambda i, p: (p[LAST], i)),
                pl.BlockSpec((rows, tile), lambda i, p: (part, i)),
                whole(1, head),
                row_part,
                row_part,
            ],
            out_specs=pl.BlockSpec((rows, tile), lambda i, p: (0, i)),
        ),
        out_shape=jax.ShapeDtypeStruct((rows, width), jnp.bfloat16),
        compiler_params=params(12),
        cost_estimate=cost(1),
        name="queries",
    )(places, *hidden, weights, acc, gain, cosine, sine)


def attention_kernel(slots, n_parts, n_others, stack, places_ref, length_ref, *refs):
    q_parts, refs = refs[:n_parts], refs[n_parts:]
    own_parts, refs = refs[:n_parts], refs[n_parts:]
    others, refs = refs[:n_others], refs[n_others:]
    o_refs, (keys_all, values_all) = refs[:-2], refs[-2:]
    part_rows, width = own_parts[0].shape
    head = width // 2
    picks = others[0].shape[0]
    cross = n_others * picks
    rows = o_refs[0].shape[0]

    start = 0
    for ref in (*others, *own_parts):
        stop = start + ref.shape[0]
        keys_all[start:stop, :] = ref[:, :head]
        values_all[start:stop, :] = ref[:, head:]
        start = stop

    scale = head ** (-0.5) * LOG2E
    own_rows = n_parts * part_rows
    for slot, o_ref in zip(slots, o_refs):
        first = places_ref[slot] * rows
        offset = pl.multiple_of(lax.rem(first, part_rows), rows)
        row = lax.broadcasted_iota(jnp.int32, (rows, own_rows), 0) + first
        column = lax.broadcasted_iota(jnp.int32, (rows, own_rows), 1)
        allowed = jnp.concatenate([column <= row] * stack, axis=0)
        position = lax.broadcasted_iota(jnp.int32, (rows, head), 0) + first
        kept = jnp.concatenate([position < length_ref[0]] * stack, axis=0)
        for left in range(0, o_ref.shape[1], stack * head):
            lanes = [slice(left + i * head, left + (i + 1) * head) for i in range(stack)]
            queries = [q_parts[0][pl.ds(offset, rows), lane] for lane in lanes]
            for part in range(1, n_parts):
                here = first >= part * part_rows
                queries = [
                    jnp.where(here, q_parts[part][pl.ds(offset, rows), lane], query)
                    for lane, query in zip(lanes, queries)
                ]
            scores = lax.dot_general(
                jnp.concatenate(queries, axis=0),
                keys_all[...],
                (((1,), (1,)), ((), ())),
                preferred_element_type=jnp.float32,
            )
            own = jnp.where(allowed, scores[:, cross:], -1e30)
            free = scores[:, :cross]
            largest = jnp.maximum(
                jnp.max(free, axis=1, keepdims=True), jnp.max(own, axis=1, keepdims=True)
            )
            free = jnp.exp2((free - largest) * scale)
            own = jnp.exp2((own - largest) * scale)
            total = jnp.sum(free, axis=1, keepdims=True) + jnp.sum(own, axis=1, keepdims=True)
            mixed = jnp.dot(
                free.astype(jnp.bfloat16), values_all[:cross, :], preferred_element_type=jnp.float32
            ) + jnp.dot(
                own.astype(jnp.bfloat16), values_all[cross:, :], preferred_element_type=jnp.float32
            )
            mixed = jnp.where(kept, mixed / total, 0.0).astype(jnp.bfloat16)
            for index, lane in enumerate(lanes):
                o_ref[:, lane] = mixed[index * rows : (index + 1) * rows, :]


def attention(places, slots, rows, lengths, queries, own, others):
    n_parts = len(own)
    part_rows, width = queries[0].shape
    head = own[0].shape[1] // 2
    picks = others[0].shape[0]
    reach = n_parts * part_rows + len(others) * picks
    return pl.pallas_call(
        functools.partial(attention_kernel, slots, n_parts, len(others), 512 // rows),
        grid_spec=pltpu.PrefetchScalarGridSpec(
            num_scalar_prefetch=2,
            grid=(1,),
            in_specs=[whole(*array.shape) for array in (*queries, *own, *others)],
            out_specs=[whole(rows, width) for _ in slots],
            scratch_shapes=[
                pltpu.VMEM((reach, head), jnp.bfloat16),
                pltpu.VMEM((reach, head), jnp.bfloat16),
            ],
        ),
        out_shape=[jax.ShapeDtypeStruct((rows, width), jnp.bfloat16) for _ in slots],
        compiler_params=params(24 if reach <= 2048 else 56),
        cost_estimate=cost(1),
        name="attention",
    )(places, lengths, *queries, *own, *others)


def mix_kernel(rows_ref, w_ref, out_ref):
    total = jnp.dot(rows_ref[...], w_ref[...], preferred_element_type=jnp.float32)
    out_ref[...] = total.astype(out_ref.dtype)


def mix(attended, w_out, which):
    rows, depth = attended.shape
    width = w_out.shape[1] // 2
    tiles = 5
    tile = width // tiles
    return pl.pallas_call(
        mix_kernel,
        grid=(tiles,),
        in_specs=[
            whole(rows, depth),
            pl.BlockSpec((depth, tile), lambda i: (0, i + which * tiles)),
        ],
        out_specs=pl.BlockSpec((rows, tile), lambda i: (0, i)),
        out_shape=jax.ShapeDtypeStruct((rows, width), jnp.bfloat16),
        compiler_params=params(8),
        cost_estimate=cost(1),
        name="mix",
    )(attended, w_out)


def add_kernel(count, *refs):
    total = refs[0][...].astype(jnp.float32)
    for ref in refs[1:count]:
        total = total + ref[...].astype(jnp.float32)
    refs[-1][...] = total.astype(jnp.bfloat16)


def added(*arrays, half=None, into=None):
    rows, width = arrays[0].shape
    wide = 1 if half is None else 2
    at = half or 0
    operands = list(arrays)
    in_specs = [whole(rows, width) for _ in arrays]
    aliases = {}
    if into is not None:
        operands.append(into)
        in_specs.append(pl.BlockSpec(memory_space=pl.ANY))
        aliases = {len(arrays): 0}
    return pl.pallas_call(
        functools.partial(add_kernel, len(arrays)),
        grid=(1,),
        in_specs=in_specs,
        out_specs=pl.BlockSpec((rows, width), lambda i: (0, at)),
        out_shape=jax.ShapeDtypeStruct((rows, wide * width), jnp.bfloat16),
        input_output_aliases=aliases,
        compiler_params=params(8),
        cost_estimate=cost(1),
        name="added",
    )(*operands)


def shards(hidden_in, lengths, summary_pos, w_query, w_key, w_value, w_out, q_gain, k_gain):
    rows_here = hidden_in.shape[0]
    head_width = q_gain.shape[0]
    place = lax.axis_index("tensor")
    n_cand = lax.axis_size("cand")
    assert lax.axis_size("tensor") == 4 and w_key.shape[1] == head_width

    def swap(array):
        return lax.ppermute(array, "tensor", [(0, 1), (1, 0), (2, 3), (3, 2)])

    def across(array):
        return lax.ppermute(array, "tensor", [(1, 2), (2, 1)])

    def outward(array):
        return lax.ppermute(array, "tensor", [(1, 0), (2, 3)])

    def inward(array):
        return lax.ppermute(array, "tensor", [(0, 1), (3, 2)])

    def between(array, offset):
        return lax.ppermute(array, "cand", [(i, i ^ offset) for i in range(n_cand)])

    low = place < 2
    near = jnp.bitwise_xor(place, 1)
    places = jnp.stack([place, near, jnp.where(low, 2, 1), jnp.where(low, 3, 0)])
    places = places.astype(jnp.int32)
    tables = rope_tables(rows_here, head_width)
    k_gain, q_gain = k_gain[None], q_gain[None]
    weights = [w_query, w_key, w_value]
    half = rows_here // 2

    mine = [lax.slice_in_dim(hidden_in, i * half, (i + 1) * half) for i in (0, 1)]
    from_near, from_mid = [], []
    for array in mine:
        from_near.append(swap(array))
        from_mid.append(across(array))
    cue = (from_near[0], from_mid[0])
    accs = partial_projection(after(places, cue), OWN, [[hidden_in]], weights, None)
    from_near[1], from_mid[1], accs = lax.optimization_barrier((from_near[1], from_mid[1], accs))
    to_inner = [across(array) for array in from_near]
    to_outer = [outward(array) for array in from_mid]
    cue = (from_near[1], from_mid[1])
    accs = partial_projection(
        after(places, cue), NEAR, [[a] for a in from_near], weights, accs
    )
    to_inner[1], accs = lax.optimization_barrier((to_inner[1], accs))
    end = [outward(array) for array in to_inner]
    cue = tuple(to_inner)
    accs = partial_projection(
        after(places, cue), THIRD, [[a, b] for a, b in zip(from_mid, to_outer)], weights, accs
    )

    final = [[a, b] for a, b in zip(to_inner, end)]
    (own_first,) = keys_values(places, final[0], 0, weights[1:], accs[1:], k_gain, *tables)
    first_queries = queries_of(places, final[0], 0, w_query, accs[0], q_gain, *tables)
    own_second, summary = keys_values(
        places,
        final[1],
        1,
        weights[1:],
        after(accs[1:], first_queries),
        k_gain,
        *tables,
        [own_first],
        summary_pos,
    )
    own = [own_first, own_second]
    others = [between(summary, offset) for offset in range(1, n_cand)]
    second_queries = queries_of(places, final[1], 1, w_query, accs[0], q_gain, *tables)
    queries = [first_queries, second_queries]

    def attend(slots):
        return attention(places, slots, rows_here // 4, lengths, queries, own, others)

    def mixed(rows):
        return [mix(rows, w_out, which) for which in (0, 1)]

    (far_rows,) = attend((LAST,))
    far = mixed(far_rows)
    places = after(places, far)
    third_rows, near_rows, own_rows = attend((THIRD, NEAR, OWN))
    mid = mixed(third_rows)
    far_in = [inward(array) for array in far]
    mid_in = [inward(array) for array in mid]
    far_sum = [added(far[0], after(far_in[0], mid))]
    near_part = mixed(after(near_rows, far_sum[0]))
    far_sum.append(added(far[1], after(far_in[1], near_part)))
    kept = mixed(after(own_rows, far_sum[1]))
    far_sum = [across(array) for array in far_sum]
    near_sum, mid_sum = [None, None], [None, None]
    cue = kept
    for i in (0, 1):
        near_sum[i] = added(near_part[i], after(far_sum[i], cue))
        mid_sum[i] = added(mid[i], after(mid_in[i], near_sum[i]))
        cue = mid_sum[i]
    near_sum = [swap(array) for array in near_sum]
    mid_sum = [across(array) for array in mid_sum]
    result = added(kept[0], near_sum[0], mid_sum[0], half=0)
    return added(kept[1], near_sum[1], mid_sum[1], half=1, into=result)


def solution(mesh):
    return jax.shard_map(
        shards,
        mesh=mesh,
        in_specs=(
            P("cand", "tensor"),
            P("cand"),
            P("cand", None),
            P(None, "tensor"),
            P(None, "tensor"),
            P(None, "tensor"),
            P("tensor", None),
            P(),
            P(),
        ),
        out_specs=P(("cand", "tensor"), None),
        check_vma=False,
    )
```

```python
import functools

import jax
import jax.numpy as jnp
import numpy as np
from jax import lax
from jax.experimental import pallas as pl
from jax.experimental.pallas import tpu as pltpu
from jax.sharding import PartitionSpec as P

MIB = 1024 * 1024
LOG2E = 1.4426950408889634
OWN, NEAR, THIRD, LAST, EIGHTHS = range(5)
OFFSETS = (0, 6, 2, 4, 1, 7, 3, 5)


def rope_tables(rows, width):
    half_width = width // 2
    frequency = (1000000.0 ** (-(np.arange(half_width) * 2.0 / width))).astype(np.float32)
    angle = np.arange(rows, dtype=np.float32)[:, None] * frequency[None, :]
    angle = angle.astype(np.float64)
    cosine, sine = np.cos(angle), np.sin(angle)
    return (
        jnp.asarray(np.concatenate([cosine, cosine], axis=1).astype(np.float32)),
        jnp.asarray(np.concatenate([-sine, sine], axis=1).astype(np.float32)),
    )


def norm_rope(vectors, gain, cosine, sine):
    scale = lax.rsqrt(jnp.mean(vectors * vectors, axis=-1, keepdims=True) + 1e-06)
    vectors = vectors * scale * gain
    return vectors * cosine + pltpu.roll(vectors, vectors.shape[-1] // 2, 1) * sine


def params(mebibytes):
    return pltpu.CompilerParams(vmem_limit_bytes=mebibytes * MIB)


def cost(flops):
    return pl.CostEstimate(flops=flops, bytes_accessed=1, transcendentals=0)


def after(array, cue):
    return lax.optimization_barrier((array, cue))[0]


def whole(*shape):
    return pl.BlockSpec(shape, lambda *_: (0,) * len(shape))


def summed(refs):
    total = refs[0][...]
    for ref in refs[1:]:
        total = total + ref[...]
    return total


def partial_kernel(counts, with_acc, places_ref, *refs):
    rows = []
    for count in counts:
        rows.append(summed(refs[:count]))
        refs = refs[count:]
    hidden = jnp.concatenate(rows, axis=0) if len(rows) > 1 else rows[0]
    weights, outs = refs[:3], refs[-3:]
    accs = refs[3:6] if with_acc else (None,) * 3
    step = pl.program_id(0)

    def add(w_ref, acc_ref, out_ref):
        product = jnp.dot(hidden, w_ref[...], preferred_element_type=jnp.float32)
        out_ref[...] = product if acc_ref is None else product + acc_ref[...]

    add(weights[0], accs[0], outs[0])

    @pl.when(step == 0)
    def _():
        add(weights[1], accs[1], outs[1])
        add(weights[2], accs[2], outs[2])


def partial_projection(places, slot, parts, weights, accs):
    features = parts[0][0].shape[1]
    rows = sum(part[0].shape[0] for part in parts)
    arrivals = [array for part in parts for array in part]
    widths = [weight.shape[1] for weight in weights]
    tile = 512
    column = lambda height: pl.BlockSpec((height, tile), lambda i, p: (0, i))
    per_array = lambda height: [column(height), whole(height, widths[1]), whole(height, widths[2])]
    block = lambda width: pl.BlockSpec((features, width), lambda i, p: (p[slot], 0))
    in_specs = [whole(*array.shape) for array in arrivals]
    in_specs.append(pl.BlockSpec((features, tile), lambda i, p: (p[slot], i)))
    in_specs += [block(widths[1]), block(widths[2])]
    operands = [*arrivals, *weights]
    if accs is not None:
        in_specs += per_array(rows)
        operands += accs
    return pl.pallas_call(
        functools.partial(partial_kernel, [len(part) for part in parts], accs is not None),
        grid_spec=pltpu.PrefetchScalarGridSpec(
            num_scalar_prefetch=1,
            grid=(widths[0] // tile,),
            in_specs=in_specs,
            out_specs=per_array(rows),
        ),
        out_shape=[jax.ShapeDtypeStruct((rows, width), jnp.float32) for width in widths],
        compiler_params=params(20),
        cost_estimate=cost(1),
        name="partial_projection",
    )(places, *operands)


def keys_values_kernel(count, n_before, places_ref, *refs):
    before, refs = refs[:n_before], refs[n_before:]
    hidden = summed(refs[:count])
    wk_ref, wv_ref, acck_ref, accv_ref, gain_ref, cos_ref, sin_ref = refs[count : count + 7]
    refs = refs[count + 7 :]
    head = gain_ref.shape[1]
    out_ref = refs[0] if n_before == 0 else refs[1]
    keys = acck_ref[...] + jnp.dot(hidden, wk_ref[...], preferred_element_type=jnp.float32)
    values = accv_ref[...] + jnp.dot(hidden, wv_ref[...], preferred_element_type=jnp.float32)
    keys = norm_rope(keys, gain_ref[...], cos_ref[...], sin_ref[...])
    out_ref[:, :head] = keys.astype(jnp.bfloat16)
    out_ref[:, head:] = values.astype(jnp.bfloat16)
    if n_before:
        pos_ref, summary_ref = refs[0], refs[2]
        picks = pos_ref.shape[1]
        picked, start = None, 0
        for ref in (*before, out_ref):
            rows = ref.shape[0]
            row = lax.broadcasted_iota(jnp.int32, (rows, picks), 0) + start
            chosen = jnp.where(row == pos_ref[...], 1.0, 0.0).astype(jnp.bfloat16)
            found = lax.dot_general(
                chosen, ref[...], (((0,), (0,)), ((), ())), preferred_element_type=jnp.float32
            )
            picked = found if picked is None else picked + found
            start += rows
        summary_ref[...] = picked.astype(jnp.bfloat16)


def keys_values(places, hidden, part, weights, accs, gain, cosine, sine, before=(), positions=None):
    rows, features = hidden[0].shape
    head = gain.shape[1]
    row_part = pl.BlockSpec((rows, head), lambda i, p: (part, 0))
    block = pl.BlockSpec((features, head), lambda i, p: (p[LAST], 0))
    in_specs = [whole(*array.shape) for array in (*before, *hidden)]
    in_specs += [block, block, row_part, row_part, whole(1, head), row_part, row_part]
    operands = [*before, *hidden, *weights, *accs, gain, cosine, sine]
    out_shape = [jax.ShapeDtypeStruct((rows, 2 * head), jnp.bfloat16)]
    if before:
        in_specs.append(whole(*positions.shape))
        operands.append(positions)
        out_shape.append(jax.ShapeDtypeStruct((positions.shape[1], 2 * head), jnp.bfloat16))
    return pl.pallas_call(
        functools.partial(keys_values_kernel, len(hidden), len(before)),
        grid_spec=pltpu.PrefetchScalarGridSpec(
            num_scalar_prefetch=1,
            grid=(1,),
            in_specs=in_specs,
            out_specs=[whole(*shape.shape) for shape in out_shape],
        ),
        out_shape=out_shape,
        compiler_params=params(12),
        cost_estimate=cost(1),
        name="keys_values",
    )(places, *operands)


def queries_kernel(count, places_ref, *refs):
    hidden = summed(refs[:count])
    w_ref, acc_ref, gain_ref, cos_ref, sin_ref, q_ref = refs[count:]
    head = gain_ref.shape[1]
    proj = acc_ref[...] + jnp.dot(hidden, w_ref[...], preferred_element_type=jnp.float32)
    for start in range(0, proj.shape[1], head):
        one = norm_rope(proj[:, start : start + head], gain_ref[...], cos_ref[...], sin_ref[...])
        q_ref[:, start : start + head] = one.astype(jnp.bfloat16)


def queries_of(places, hidden, part, weights, acc, gain, cosine, sine):
    rows, features = hidden[0].shape
    head = gain.shape[1]
    width = weights.shape[1]
    tile = 4 * head
    row_part = pl.BlockSpec((rows, head), lambda i, p: (part, 0))
    return pl.pallas_call(
        functools.partial(queries_kernel, len(hidden)),
        grid_spec=pltpu.PrefetchScalarGridSpec(
            num_scalar_prefetch=1,
            grid=(width // tile,),
            in_specs=[whole(rows, features) for _ in hidden]
            + [
                pl.BlockSpec((features, tile), lambda i, p: (p[LAST], i)),
                pl.BlockSpec((rows, tile), lambda i, p: (part, i)),
                whole(1, head),
                row_part,
                row_part,
            ],
            out_specs=pl.BlockSpec((rows, tile), lambda i, p: (0, i)),
        ),
        out_shape=jax.ShapeDtypeStruct((rows, width), jnp.bfloat16),
        compiler_params=params(12),
        cost_estimate=cost(1),
        name="queries",
    )(places, *hidden, weights, acc, gain, cosine, sine)


def attention_kernel(slots, n_parts, n_others, stack, places_ref, length_ref, *refs):
    q_parts, refs = refs[:n_parts], refs[n_parts:]
    own_parts, refs = refs[:n_parts], refs[n_parts:]
    others, refs = refs[:n_others], refs[n_others:]
    o_refs, (keys_all, values_all) = refs[:-2], refs[-2:]
    part_rows, width = own_parts[0].shape
    head = width // 2
    picks = others[0].shape[0]
    cross = n_others * picks
    rows = o_refs[0].shape[0]

    start = 0
    for ref in (*others, *own_parts):
        stop = start + ref.shape[0]
        keys_all[start:stop, :] = ref[:, :head]
        values_all[start:stop, :] = ref[:, head:]
        start = stop

    scale = head ** (-0.5) * LOG2E
    own_rows = n_parts * part_rows
    for slot, o_ref in zip(slots, o_refs):
        first = places_ref[slot] * rows
        offset = pl.multiple_of(lax.rem(first, part_rows), rows)
        row = lax.broadcasted_iota(jnp.int32, (rows, own_rows), 0) + first
        column = lax.broadcasted_iota(jnp.int32, (rows, own_rows), 1)
        allowed = jnp.concatenate([column <= row] * stack, axis=0)
        position = lax.broadcasted_iota(jnp.int32, (rows, head), 0) + first
        kept = jnp.concatenate([position < length_ref[0]] * stack, axis=0)
        for left in range(0, o_ref.shape[1], stack * head):
            lanes = [slice(left + i * head, left + (i + 1) * head) for i in range(stack)]
            queries = [q_parts[0][pl.ds(offset, rows), lane] for lane in lanes]
            for part in range(1, n_parts):
                here = first >= part * part_rows
                queries = [
                    jnp.where(here, q_parts[part][pl.ds(offset, rows), lane], query)
                    for lane, query in zip(lanes, queries)
                ]
            scores = lax.dot_general(
                jnp.concatenate(queries, axis=0),
                keys_all[...],
                (((1,), (1,)), ((), ())),
                preferred_element_type=jnp.float32,
            )
            own = jnp.where(allowed, scores[:, cross:], -1e30)
            free = scores[:, :cross]
            largest = jnp.maximum(
                jnp.max(free, axis=1, keepdims=True), jnp.max(own, axis=1, keepdims=True)
            )
            free = jnp.exp2((free - largest) * scale)
            own = jnp.exp2((own - largest) * scale)
            total = jnp.sum(free, axis=1, keepdims=True) + jnp.sum(own, axis=1, keepdims=True)
            mixed = jnp.dot(
                free.astype(jnp.bfloat16), values_all[:cross, :], preferred_element_type=jnp.float32
            ) + jnp.dot(
                own.astype(jnp.bfloat16), values_all[cross:, :], preferred_element_type=jnp.float32
            )
            mixed = jnp.where(kept, mixed / total, 0.0).astype(jnp.bfloat16)
            for index, lane in enumerate(lanes):
                o_ref[:, lane] = mixed[index * rows : (index + 1) * rows, :]


def attention(places, slots, rows, lengths, queries, own, others):
    n_parts = len(own)
    part_rows, width = queries[0].shape
    head = own[0].shape[1] // 2
    picks = others[0].shape[0]
    reach = n_parts * part_rows + len(others) * picks
    return pl.pallas_call(
        functools.partial(attention_kernel, slots, n_parts, len(others), 512 // rows),
        grid_spec=pltpu.PrefetchScalarGridSpec(
            num_scalar_prefetch=2,
            grid=(1,),
            in_specs=[whole(*array.shape) for array in (*queries, *own, *others)],
            out_specs=[whole(rows, width) for _ in slots],
            scratch_shapes=[
                pltpu.VMEM((reach, head), jnp.bfloat16),
                pltpu.VMEM((reach, head), jnp.bfloat16),
            ],
        ),
        out_shape=[jax.ShapeDtypeStruct((rows, width), jnp.bfloat16) for _ in slots],
        compiler_params=params(24 if reach <= 2048 else 56),
        cost_estimate=cost(1),
        name="attention",
    )(places, lengths, *queries, *own, *others)


def mix_kernel(rows_ref, w_ref, out_ref):
    total = jnp.dot(rows_ref[...], w_ref[...], preferred_element_type=jnp.float32)
    out_ref[...] = total.astype(out_ref.dtype)


def mix(attended, w_out, which):
    rows, depth = attended.shape
    width = w_out.shape[1] // 2
    tiles = 5
    tile = width // tiles
    return pl.pallas_call(
        mix_kernel,
        grid=(tiles,),
        in_specs=[
            whole(rows, depth),
            pl.BlockSpec((depth, tile), lambda i: (0, i + which * tiles)),
        ],
        out_specs=pl.BlockSpec((rows, tile), lambda i: (0, i)),
        out_shape=jax.ShapeDtypeStruct((rows, width), jnp.bfloat16),
        compiler_params=params(8),
        cost_estimate=cost(1),
        name="mix",
    )(attended, w_out)


def eighths_kernel(places_ref, w_ref, out_ref):
    out_ref[...] = w_ref[...]


def eighths(places, w_out, share):
    width = w_out.shape[1] // 2
    return pl.pallas_call(
        eighths_kernel,
        grid_spec=pltpu.PrefetchScalarGridSpec(
            num_scalar_prefetch=1,
            grid=(2,),
            in_specs=[pl.BlockSpec((share, width), lambda i, p: (p[EIGHTHS + i], 1))],
            out_specs=pl.BlockSpec((share, width), lambda i, p: (i, 0)),
        ),
        out_shape=jax.ShapeDtypeStruct((2 * share, width), w_out.dtype),
        compiler_params=params(8),
        cost_estimate=cost(1),
        name="eighths",
    )(places, w_out)


def mix_sent_kernel(places_ref, rows_ref, *refs):
    pieces, out_ref = refs[:-1], refs[-1]
    share = rows_ref.shape[1] // len(OFFSETS)
    rows = []
    for index in range(len(OFFSETS)):
        start = pl.multiple_of(places_ref[EIGHTHS + index] * share, share)
        rows.append(rows_ref[:, pl.ds(start, share)])
    total = jnp.dot(
        jnp.concatenate(rows, axis=1),
        jnp.concatenate([piece[...] for piece in pieces], axis=0),
        preferred_element_type=jnp.float32,
    )
    out_ref[...] = total.astype(out_ref.dtype)


def mix_sent(places, attended, pieces):
    rows, depth = attended.shape
    width = pieces[0].shape[1]
    tile = width // 5
    column = lambda height: pl.BlockSpec((height, tile), lambda i, p: (0, i))
    return pl.pallas_call(
        mix_sent_kernel,
        grid_spec=pltpu.PrefetchScalarGridSpec(
            num_scalar_prefetch=1,
            grid=(width // tile,),
            in_specs=[whole(rows, depth)] + [column(piece.shape[0]) for piece in pieces],
            out_specs=column(rows),
        ),
        out_shape=jax.ShapeDtypeStruct((rows, width), jnp.bfloat16),
        compiler_params=params(8),
        cost_estimate=cost(1),
        name="mix_sent",
    )(places, attended, *pieces)


def add_kernel(count, *refs):
    total = refs[0][...].astype(jnp.float32)
    for ref in refs[1:count]:
        total = total + ref[...].astype(jnp.float32)
    refs[-1][...] = total.astype(jnp.bfloat16)


def added(*arrays, half=None, into=None):
    rows, width = arrays[0].shape
    wide = 1 if half is None else 2
    at = half or 0
    operands = list(arrays)
    in_specs = [whole(rows, width) for _ in arrays]
    aliases = {}
    if into is not None:
        operands.append(into)
        in_specs.append(pl.BlockSpec(memory_space=pl.ANY))
        aliases = {len(arrays): 0}
    return pl.pallas_call(
        functools.partial(add_kernel, len(arrays)),
        grid=(1,),
        in_specs=in_specs,
        out_specs=pl.BlockSpec((rows, width), lambda i: (0, at)),
        out_shape=jax.ShapeDtypeStruct((rows, wide * width), jnp.bfloat16),
        input_output_aliases=aliases,
        compiler_params=params(8),
        cost_estimate=cost(1),
        name="added",
    )(*operands)


def shards(hidden_in, lengths, summary_pos, w_query, w_key, w_value, w_out, q_gain, k_gain):
    rows_here = hidden_in.shape[0]
    head_width = q_gain.shape[0]
    place = lax.axis_index("tensor")
    n_cand = lax.axis_size("cand")
    assert lax.axis_size("tensor") == 4 and w_key.shape[1] == head_width

    def swap(array):
        return lax.ppermute(array, "tensor", [(0, 1), (1, 0), (2, 3), (3, 2)])

    def across(array):
        return lax.ppermute(array, "tensor", [(1, 2), (2, 1)])

    def outward(array):
        return lax.ppermute(array, "tensor", [(1, 0), (2, 3)])

    def inward(array):
        return lax.ppermute(array, "tensor", [(0, 1), (3, 2)])

    def between(array, offset):
        return lax.ppermute(array, "cand", [(i, i ^ offset) for i in range(n_cand)])

    low = place < 2
    near = jnp.bitwise_xor(place, 1)
    places = [place, near, jnp.where(low, 2, 1), jnp.where(low, 3, 0)]
    places += [jnp.bitwise_xor(lax.axis_index("cand"), offset) for offset in OFFSETS]
    places = jnp.stack(places).astype(jnp.int32)
    share = w_out.shape[0] // n_cand
    spread = n_cand == len(OFFSETS) and share % 128 == 0
    tables = rope_tables(rows_here, head_width)
    k_gain, q_gain = k_gain[None], q_gain[None]
    weights = [w_query, w_key, w_value]
    half = rows_here // 2

    mine = [lax.slice_in_dim(hidden_in, i * half, (i + 1) * half) for i in (0, 1)]
    from_near, from_mid = [], []
    for array in mine:
        from_near.append(swap(array))
        from_mid.append(across(array))
    to_outer = [outward(array) for array in from_mid]
    to_inner = [across(from_near[0])]
    cue = (from_near[0], from_mid[0])
    accs = partial_projection(after(places, cue), OWN, [[hidden_in]], weights, None)
    pieces = []
    if spread:
        pieces.append(inward(after(eighths(places, w_out, share), from_near[0])))
    from_near[1], accs = lax.optimization_barrier((from_near[1], accs))
    to_inner.append(across(after(from_near[1], to_outer[0])))
    cue = (from_near[1], from_mid[1])
    accs = partial_projection(
        after(places, cue), NEAR, [[a] for a in from_near], weights, accs
    )
    end = [outward(to_inner[0]), outward(after(to_inner[1], (to_outer[1], accs)))]
    if spread:
        pieces.append(between(pieces[0], OFFSETS[2]))
    cue = (to_inner, accs)
    accs = partial_projection(
        after(places, cue), THIRD, [[a, b] for a, b in zip(from_mid, to_outer)], weights, accs
    )

    final = [[a, b] for a, b in zip(to_inner, end)]
    (own_first,) = keys_values(places, final[0], 0, weights[1:], accs[1:], k_gain, *tables)
    first_queries = queries_of(places, final[0], 0, w_query, accs[0], q_gain, *tables)
    own_second, summary = keys_values(
        places,
        final[1],
        1,
        weights[1:],
        after(accs[1:], first_queries),
        k_gain,
        *tables,
        [own_first],
        summary_pos,
    )
    own = [own_first, own_second]
    others = [between(summary, offset) for offset in range(1, n_cand)]
    second_queries = queries_of(places, final[1], 1, w_query, accs[0], q_gain, *tables)
    queries = [first_queries, second_queries]

    def attend(slots):
        return attention(places, slots, rows_here // 4, lengths, queries, own, others)

    def mixed(rows):
        return [mix(rows, w_out, which) for which in (0, 1)]

    places, pieces = lax.optimization_barrier((places, pieces))
    (far_rows,) = attend((LAST,))
    far = mixed(far_rows)
    places = after(places, far)
    third_rows, near_rows, own_rows = attend((THIRD, NEAR, OWN))
    mid = mixed(third_rows)
    far_in = [inward(array) for array in far]
    mid_in = [inward(array) for array in mid]

    far_sum = added(far[0], after(far_in[0], mid))
    near_part = mixed(after(near_rows, far_sum))
    far_sum = [far_sum, added(far[1], after(far_in[1], near_part))]
    kept = mixed(after(own_rows, far_sum[1]))
    far_sum = [across(array) for array in far_sum]
    near_sum, mid_sum = [None, None], [None, None]
    cue = kept
    for i in (0, 1):
        near_sum[i] = added(near_part[i], after(far_sum[i], cue))
        mid_sum[i] = added(mid[i], after(mid_in[i], near_sum[i]))
        cue = mid_sum[i]
    mid_sum = [across(array) for array in mid_sum]
    if spread:
        kept[0] = added(kept[0], mid_sum[0])
        near_in = inward(near_rows)
        pieces += [between(after(piece, cue), 1) for piece in pieces]
        near_in, near_sum[0], _ = lax.optimization_barrier((near_in, near_sum[0], (cue, kept[0])))
        near_sum = [swap(near_sum[0]), outward(near_sum[1])]
        kept[1] = added(kept[1], mix_sent(places, near_in, pieces))
        result = added(kept[0], near_sum[0], half=0)
    else:
        near_sum = [swap(array) for array in near_sum]
        result = added(kept[0], near_sum[0], mid_sum[0], half=0)
    return added(kept[1], near_sum[1], mid_sum[1], half=1, into=result)


def solution(mesh):
    return jax.shard_map(
        shards,
        mesh=mesh,
        in_specs=(
            P("cand", "tensor"),
            P("cand"),
            P("cand", None),
            P(None, "tensor"),
            P(None, "tensor"),
            P(None, "tensor"),
            P("tensor", None),
            P(),
            P(),
        ),
        out_specs=P(("cand", "tensor"), None),
        check_vma=False,
    )
```

```python
import functools

import jax
import jax.numpy as jnp
import numpy as np
from jax import lax
from jax.experimental import pallas as pl
from jax.experimental.pallas import tpu as pltpu
from jax.sharding import PartitionSpec as P

MIB = 1024 * 1024
LOG2E = 1.4426950408889634
OWN, NEAR, THIRD, LAST, EIGHTHS = range(5)
OFFSETS = (0, 6, 2, 4, 1, 7, 3, 5)


def rope_tables(rows, width):
    half_width = width // 2
    frequency = (1000000.0 ** (-(np.arange(half_width) * 2.0 / width))).astype(np.float32)
    angle = np.arange(rows, dtype=np.float32)[:, None] * frequency[None, :]
    angle = angle.astype(np.float64)
    cosine, sine = np.cos(angle), np.sin(angle)
    return (
        jnp.asarray(np.concatenate([cosine, cosine], axis=1).astype(np.float32)),
        jnp.asarray(np.concatenate([-sine, sine], axis=1).astype(np.float32)),
    )


def norm_rope(vectors, gain, cosine, sine):
    scale = lax.rsqrt(jnp.mean(vectors * vectors, axis=-1, keepdims=True) + 1e-06)
    vectors = vectors * scale * gain
    return vectors * cosine + pltpu.roll(vectors, vectors.shape[-1] // 2, 1) * sine


def params(mebibytes):
    return pltpu.CompilerParams(vmem_limit_bytes=mebibytes * MIB)


def cost(flops):
    return pl.CostEstimate(flops=flops, bytes_accessed=1, transcendentals=0)


def after(array, cue):
    return lax.optimization_barrier((array, cue))[0]


def whole(*shape):
    return pl.BlockSpec(shape, lambda *_: (0,) * len(shape))


def summed(refs):
    total = refs[0][...]
    for ref in refs[1:]:
        total = total + ref[...]
    return total


def partial_kernel(counts, with_acc, places_ref, *refs):
    rows = []
    for count in counts:
        rows.append(summed(refs[:count]))
        refs = refs[count:]
    hidden = jnp.concatenate(rows, axis=0) if len(rows) > 1 else rows[0]
    weights, outs = refs[:3], refs[-3:]
    accs = refs[3:6] if with_acc else (None,) * 3
    step = pl.program_id(0)

    def add(w_ref, acc_ref, out_ref):
        product = jnp.dot(hidden, w_ref[...], preferred_element_type=jnp.float32)
        out_ref[...] = product if acc_ref is None else product + acc_ref[...]

    add(weights[0], accs[0], outs[0])

    @pl.when(step == 0)
    def _():
        add(weights[1], accs[1], outs[1])
        add(weights[2], accs[2], outs[2])


def partial_projection(places, slot, parts, weights, accs):
    features = parts[0][0].shape[1]
    rows = sum(part[0].shape[0] for part in parts)
    arrivals = [array for part in parts for array in part]
    widths = [weight.shape[1] for weight in weights]
    tile = 512
    column = lambda height: pl.BlockSpec((height, tile), lambda i, p: (0, i))
    per_array = lambda height: [column(height), whole(height, widths[1]), whole(height, widths[2])]
    block = lambda width: pl.BlockSpec((features, width), lambda i, p: (p[slot], 0))
    in_specs = [whole(*array.shape) for array in arrivals]
    in_specs.append(pl.BlockSpec((features, tile), lambda i, p: (p[slot], i)))
    in_specs += [block(widths[1]), block(widths[2])]
    operands = [*arrivals, *weights]
    if accs is not None:
        in_specs += per_array(rows)
        operands += accs
    return pl.pallas_call(
        functools.partial(partial_kernel, [len(part) for part in parts], accs is not None),
        grid_spec=pltpu.PrefetchScalarGridSpec(
            num_scalar_prefetch=1,
            grid=(widths[0] // tile,),
            in_specs=in_specs,
            out_specs=per_array(rows),
        ),
        out_shape=[jax.ShapeDtypeStruct((rows, width), jnp.float32) for width in widths],
        compiler_params=params(20),
        cost_estimate=cost(1),
        name="partial_projection",
    )(places, *operands)


def keys_values_kernel(count, n_before, places_ref, *refs):
    before, refs = refs[:n_before], refs[n_before:]
    hidden = summed(refs[:count])
    wk_ref, wv_ref, acck_ref, accv_ref, gain_ref, cos_ref, sin_ref = refs[count : count + 7]
    refs = refs[count + 7 :]
    head = gain_ref.shape[1]
    out_ref = refs[0] if n_before == 0 else refs[1]
    keys = acck_ref[...] + jnp.dot(hidden, wk_ref[...], preferred_element_type=jnp.float32)
    values = accv_ref[...] + jnp.dot(hidden, wv_ref[...], preferred_element_type=jnp.float32)
    keys = norm_rope(keys, gain_ref[...], cos_ref[...], sin_ref[...])
    out_ref[:, :head] = keys.astype(jnp.bfloat16)
    out_ref[:, head:] = values.astype(jnp.bfloat16)
    if n_before:
        pos_ref, summary_ref = refs[0], refs[2]
        picks = pos_ref.shape[1]
        picked, start = None, 0
        for ref in (*before, out_ref):
            rows = ref.shape[0]
            row = lax.broadcasted_iota(jnp.int32, (rows, picks), 0) + start
            chosen = jnp.where(row == pos_ref[...], 1.0, 0.0).astype(jnp.bfloat16)
            found = lax.dot_general(
                chosen, ref[...], (((0,), (0,)), ((), ())), preferred_element_type=jnp.float32
            )
            picked = found if picked is None else picked + found
            start += rows
        summary_ref[...] = picked.astype(jnp.bfloat16)


def keys_values(places, hidden, part, weights, accs, gain, cosine, sine, before=(), positions=None):
    rows, features = hidden[0].shape
    head = gain.shape[1]
    row_part = pl.BlockSpec((rows, head), lambda i, p: (part, 0))
    block = pl.BlockSpec((features, head), lambda i, p: (p[LAST], 0))
    in_specs = [whole(*array.shape) for array in (*before, *hidden)]
    in_specs += [block, block, row_part, row_part, whole(1, head), row_part, row_part]
    operands = [*before, *hidden, *weights, *accs, gain, cosine, sine]
    out_shape = [jax.ShapeDtypeStruct((rows, 2 * head), jnp.bfloat16)]
    if before:
        in_specs.append(whole(*positions.shape))
        operands.append(positions)
        out_shape.append(jax.ShapeDtypeStruct((positions.shape[1], 2 * head), jnp.bfloat16))
    return pl.pallas_call(
        functools.partial(keys_values_kernel, len(hidden), len(before)),
        grid_spec=pltpu.PrefetchScalarGridSpec(
            num_scalar_prefetch=1,
            grid=(1,),
            in_specs=in_specs,
            out_specs=[whole(*shape.shape) for shape in out_shape],
        ),
        out_shape=out_shape,
        compiler_params=params(12),
        cost_estimate=cost(1),
        name="keys_values",
    )(places, *operands)


def queries_kernel(count, places_ref, *refs):
    hidden = summed(refs[:count])
    w_ref, acc_ref, gain_ref, cos_ref, sin_ref, q_ref = refs[count:]
    head = gain_ref.shape[1]
    proj = acc_ref[...] + jnp.dot(hidden, w_ref[...], preferred_element_type=jnp.float32)
    for start in range(0, proj.shape[1], head):
        one = norm_rope(proj[:, start : start + head], gain_ref[...], cos_ref[...], sin_ref[...])
        q_ref[:, start : start + head] = one.astype(jnp.bfloat16)


def queries_of(places, hidden, part, weights, acc, gain, cosine, sine):
    rows, features = hidden[0].shape
    head = gain.shape[1]
    width = weights.shape[1]
    tile = 4 * head
    row_part = pl.BlockSpec((rows, head), lambda i, p: (part, 0))
    return pl.pallas_call(
        functools.partial(queries_kernel, len(hidden)),
        grid_spec=pltpu.PrefetchScalarGridSpec(
            num_scalar_prefetch=1,
            grid=(width // tile,),
            in_specs=[whole(rows, features) for _ in hidden]
            + [
                pl.BlockSpec((features, tile), lambda i, p: (p[LAST], i)),
                pl.BlockSpec((rows, tile), lambda i, p: (part, i)),
                whole(1, head),
                row_part,
                row_part,
            ],
            out_specs=pl.BlockSpec((rows, tile), lambda i, p: (0, i)),
        ),
        out_shape=jax.ShapeDtypeStruct((rows, width), jnp.bfloat16),
        compiler_params=params(12),
        cost_estimate=cost(1),
        name="queries",
    )(places, *hidden, weights, acc, gain, cosine, sine)


def attention_kernel(slots, n_parts, n_others, stack, places_ref, length_ref, *refs):
    q_parts, refs = refs[:n_parts], refs[n_parts:]
    own_parts, refs = refs[:n_parts], refs[n_parts:]
    others, refs = refs[:n_others], refs[n_others:]
    o_refs, (keys_all, values_all) = refs[:-2], refs[-2:]
    part_rows, width = own_parts[0].shape
    head = width // 2
    picks = others[0].shape[0]
    cross = n_others * picks
    rows = o_refs[0].shape[0]

    start = 0
    for ref in (*others, *own_parts):
        stop = start + ref.shape[0]
        keys_all[start:stop, :] = ref[:, :head]
        values_all[start:stop, :] = ref[:, head:]
        start = stop

    scale = head ** (-0.5) * LOG2E
    own_rows = n_parts * part_rows
    for slot, o_ref in zip(slots, o_refs):
        first = places_ref[slot] * rows
        offset = pl.multiple_of(lax.rem(first, part_rows), rows)
        row = lax.broadcasted_iota(jnp.int32, (rows, own_rows), 0) + first
        column = lax.broadcasted_iota(jnp.int32, (rows, own_rows), 1)
        allowed = jnp.concatenate([column <= row] * stack, axis=0)
        position = lax.broadcasted_iota(jnp.int32, (rows, head), 0) + first
        kept = jnp.concatenate([position < length_ref[0]] * stack, axis=0)
        for left in range(0, o_ref.shape[1], stack * head):
            lanes = [slice(left + i * head, left + (i + 1) * head) for i in range(stack)]
            queries = [q_parts[0][pl.ds(offset, rows), lane] for lane in lanes]
            for part in range(1, n_parts):
                here = first >= part * part_rows
                queries = [
                    jnp.where(here, q_parts[part][pl.ds(offset, rows), lane], query)
                    for lane, query in zip(lanes, queries)
                ]
            scores = lax.dot_general(
                jnp.concatenate(queries, axis=0),
                keys_all[...],
                (((1,), (1,)), ((), ())),
                preferred_element_type=jnp.float32,
            )
            own = jnp.where(allowed, scores[:, cross:], -1e30)
            free = scores[:, :cross]
            largest = jnp.maximum(
                jnp.max(free, axis=1, keepdims=True), jnp.max(own, axis=1, keepdims=True)
            )
            free = jnp.exp2((free - largest) * scale)
            own = jnp.exp2((own - largest) * scale)
            total = jnp.sum(free, axis=1, keepdims=True) + jnp.sum(own, axis=1, keepdims=True)
            mixed = jnp.dot(
                free.astype(jnp.bfloat16), values_all[:cross, :], preferred_element_type=jnp.float32
            ) + jnp.dot(
                own.astype(jnp.bfloat16), values_all[cross:, :], preferred_element_type=jnp.float32
            )
            mixed = jnp.where(kept, mixed / total, 0.0).astype(jnp.bfloat16)
            for index, lane in enumerate(lanes):
                o_ref[:, lane] = mixed[index * rows : (index + 1) * rows, :]


def attention(places, slots, rows, lengths, queries, own, others):
    n_parts = len(own)
    part_rows, width = queries[0].shape
    head = own[0].shape[1] // 2
    picks = others[0].shape[0]
    reach = n_parts * part_rows + len(others) * picks
    return pl.pallas_call(
        functools.partial(attention_kernel, slots, n_parts, len(others), 512 // rows),
        grid_spec=pltpu.PrefetchScalarGridSpec(
            num_scalar_prefetch=2,
            grid=(1,),
            in_specs=[whole(*array.shape) for array in (*queries, *own, *others)],
            out_specs=[whole(rows, width) for _ in slots],
            scratch_shapes=[
                pltpu.VMEM((reach, head), jnp.bfloat16),
                pltpu.VMEM((reach, head), jnp.bfloat16),
            ],
        ),
        out_shape=[jax.ShapeDtypeStruct((rows, width), jnp.bfloat16) for _ in slots],
        compiler_params=params(24 if reach <= 2048 else 56),
        cost_estimate=cost(1),
        name="attention",
    )(places, lengths, *queries, *own, *others)


def mix_kernel(rows_ref, w_ref, out_ref):
    total = jnp.dot(rows_ref[...], w_ref[...], preferred_element_type=jnp.float32)
    out_ref[...] = total.astype(out_ref.dtype)


def mix(attended, w_out, which):
    rows, depth = attended.shape
    width = w_out.shape[1] // 2
    tiles = 5
    tile = width // tiles
    return pl.pallas_call(
        mix_kernel,
        grid=(tiles,),
        in_specs=[
            whole(rows, depth),
            pl.BlockSpec((depth, tile), lambda i: (0, i + which * tiles)),
        ],
        out_specs=pl.BlockSpec((rows, tile), lambda i: (0, i)),
        out_shape=jax.ShapeDtypeStruct((rows, width), jnp.bfloat16),
        compiler_params=params(8),
        cost_estimate=cost(1),
        name="mix",
    )(attended, w_out)


def eighths_kernel(places_ref, w_ref, out_ref):
    out_ref[...] = w_ref[...]


def eighths(places, w_out, share):
    width = w_out.shape[1] // 2
    return pl.pallas_call(
        eighths_kernel,
        grid_spec=pltpu.PrefetchScalarGridSpec(
            num_scalar_prefetch=1,
            grid=(2,),
            in_specs=[pl.BlockSpec((share, width), lambda i, p: (p[EIGHTHS + i], 1))],
            out_specs=pl.BlockSpec((share, width), lambda i, p: (i, 0)),
        ),
        out_shape=jax.ShapeDtypeStruct((2 * share, width), w_out.dtype),
        compiler_params=params(8),
        cost_estimate=cost(1),
        name="eighths",
    )(places, w_out)


def mix_sent_kernel(places_ref, rows_ref, *refs):
    pieces, out_ref = refs[:-1], refs[-1]
    share = rows_ref.shape[1] // len(OFFSETS)
    rows = []
    for index in range(len(OFFSETS)):
        start = pl.multiple_of(places_ref[EIGHTHS + index] * share, share)
        rows.append(rows_ref[:, pl.ds(start, share)])
    total = jnp.dot(
        jnp.concatenate(rows, axis=1),
        jnp.concatenate([piece[...] for piece in pieces], axis=0),
        preferred_element_type=jnp.float32,
    )
    out_ref[...] = total.astype(out_ref.dtype)


def mix_sent(places, attended, pieces):
    rows, depth = attended.shape
    width = pieces[0].shape[1]
    tile = width // 5
    column = lambda height: pl.BlockSpec((height, tile), lambda i, p: (0, i))
    return pl.pallas_call(
        mix_sent_kernel,
        grid_spec=pltpu.PrefetchScalarGridSpec(
            num_scalar_prefetch=1,
            grid=(width // tile,),
            in_specs=[whole(rows, depth)] + [column(piece.shape[0]) for piece in pieces],
            out_specs=column(rows),
        ),
        out_shape=jax.ShapeDtypeStruct((rows, width), jnp.bfloat16),
        compiler_params=params(8),
        cost_estimate=cost(1),
        name="mix_sent",
    )(places, attended, *pieces)


def add_kernel(count, *refs):
    total = refs[0][...].astype(jnp.float32)
    for ref in refs[1:count]:
        total = total + ref[...].astype(jnp.float32)
    refs[-1][...] = total.astype(jnp.bfloat16)


def added(*arrays, half=None, into=None):
    rows, width = arrays[0].shape
    wide = 1 if half is None else 2
    at = half or 0
    operands = list(arrays)
    in_specs = [whole(rows, width) for _ in arrays]
    aliases = {}
    if into is not None:
        operands.append(into)
        in_specs.append(pl.BlockSpec(memory_space=pl.ANY))
        aliases = {len(arrays): 0}
    return pl.pallas_call(
        functools.partial(add_kernel, len(arrays)),
        grid=(1,),
        in_specs=in_specs,
        out_specs=pl.BlockSpec((rows, width), lambda i: (0, at)),
        out_shape=jax.ShapeDtypeStruct((rows, wide * width), jnp.bfloat16),
        input_output_aliases=aliases,
        compiler_params=params(8),
        cost_estimate=cost(1),
        name="added",
    )(*operands)


def shards(hidden_in, lengths, summary_pos, w_query, w_key, w_value, w_out, q_gain, k_gain):
    rows_here = hidden_in.shape[0]
    head_width = q_gain.shape[0]
    place = lax.axis_index("tensor")
    n_cand = lax.axis_size("cand")
    assert lax.axis_size("tensor") == 4 and w_key.shape[1] == head_width

    def swap(array):
        return lax.ppermute(array, "tensor", [(0, 1), (1, 0), (2, 3), (3, 2)])

    def across(array):
        return lax.ppermute(array, "tensor", [(1, 2), (2, 1)])

    def outward(array):
        return lax.ppermute(array, "tensor", [(1, 0), (2, 3)])

    def inward(array):
        return lax.ppermute(array, "tensor", [(0, 1), (3, 2)])

    def between(array, offset):
        return lax.ppermute(array, "cand", [(i, i ^ offset) for i in range(n_cand)])

    low = place < 2
    near = jnp.bitwise_xor(place, 1)
    places = [place, near, jnp.where(low, 2, 1), jnp.where(low, 3, 0)]
    places += [jnp.bitwise_xor(lax.axis_index("cand"), offset) for offset in OFFSETS]
    places = jnp.stack(places).astype(jnp.int32)
    share = w_out.shape[0] // n_cand
    spread = n_cand == len(OFFSETS) and share % 128 == 0
    tables = rope_tables(rows_here, head_width)
    k_gain, q_gain = k_gain[None], q_gain[None]
    weights = [w_query, w_key, w_value]
    half = rows_here // 2

    mine = [lax.slice_in_dim(hidden_in, i * half, (i + 1) * half) for i in (0, 1)]
    from_near, from_mid = [], []
    for array in mine:
        from_near.append(swap(array))
        from_mid.append(across(array))
    accs = partial_projection(places, OWN, [[hidden_in]], weights, None)
    from_near[0], from_mid[0], accs = lax.optimization_barrier((from_near[0], from_mid[0], accs))
    to_outer = [outward(array) for array in from_mid]
    to_inner = [across(from_near[0])]
    to_inner.append(across(after(from_near[1], (to_outer[0], from_mid[1]))))
    pieces = []
    if spread:
        pieces.append(inward(after(eighths(places, w_out, share), from_near)))
    cue = (from_near[1], from_mid[1])
    accs = partial_projection(
        after(places, cue), NEAR, [[a] for a in from_near], weights, accs
    )
    end = [outward(to_inner[0]), outward(after(to_inner[1], (to_outer[1], accs)))]
    if spread:
        pieces.append(between(after(pieces[0], to_inner[1]), OFFSETS[2]))
        pieces.append(between(after(pieces[0], end[0]), 1))
    cue = (to_inner, accs)
    accs = partial_projection(
        after(places, cue), THIRD, [[a, b] for a, b in zip(from_mid, to_outer)], weights, accs
    )

    final = [[a, b] for a, b in zip(to_inner, end)]
    (own_first,) = keys_values(places, final[0], 0, weights[1:], accs[1:], k_gain, *tables)
    first_queries = queries_of(places, final[0], 0, w_query, accs[0], q_gain, *tables)
    own_second, summary = keys_values(
        places,
        final[1],
        1,
        weights[1:],
        after(accs[1:], (first_queries, pieces)),
        k_gain,
        *tables,
        [own_first],
        summary_pos,
    )
    own = [own_first, own_second]
    others = [between(summary, offset) for offset in range(1, n_cand)]
    second_queries = queries_of(places, final[1], 1, w_query, accs[0], q_gain, *tables)
    queries = [first_queries, second_queries]

    def attend(slots):
        return attention(places, slots, rows_here // 4, lengths, queries, own, others)

    def mixed(rows):
        return [mix(rows, w_out, which) for which in (0, 1)]

    if spread:
        pieces.append(between(after(pieces[1], others), 1))
    (far_rows,) = attend((LAST,))
    far = mixed(far_rows)
    places = after(places, (far, pieces))
    third_rows, near_rows, own_rows = attend((THIRD, NEAR, OWN))
    mid = mixed(third_rows)
    far_in = [inward(array) for array in far]
    mid_in = [inward(array) for array in mid]

    far_sum = added(far[0], after(far_in[0], mid))
    near_part = mixed(after(near_rows, far_sum))
    far_sum = [far_sum, added(far[1], after(far_in[1], near_part))]
    kept = mixed(after(own_rows, far_sum[1]))
    far_sum = [across(array) for array in far_sum]
    out_sum, mid_sum = [None, None], [None, None]
    out_sum[0] = added(near_part[0], after(far_sum[0], kept))
    mid_sum[0] = added(mid[0], after(mid_in[0], out_sum[0]))
    out_sum[1] = added(near_part[1], after(far_sum[1], mid_sum[0]))
    from_inner = [outward(array) for array in out_sum]
    kept[0] = added(kept[0], after(from_inner[0], out_sum[1]))
    mid_sum[1] = added(mid[1], after(mid_in[1], kept[0]))
    cue = mid_sum[1]
    mid_sum = [across(array) for array in mid_sum]
    if spread:
        near_in = inward(after(near_rows, out_sum[0]))
        sent = mix_sent(places, after(near_in, cue), pieces)
    else:
        sent = inward(near_part[1])
    near_in = inward(after(near_part[0], near_in if spread else out_sum[1]))
    kept[1] = added(kept[1], from_inner[1], sent)
    kept[0] = added(kept[0], after(mid_sum[0], kept[1]))
    result = added(kept[1], after(mid_sum[1], kept[0]), half=1)
    return added(kept[0], near_in, half=0, into=result)


def solution(mesh):
    return jax.shard_map(
        shards,
        mesh=mesh,
        in_specs=(
            P("cand", "tensor"),
            P("cand"),
            P("cand", None),
            P(None, "tensor"),
            P(None, "tensor"),
            P(None, "tensor"),
            P("tensor", None),
            P(),
            P(),
        ),
        out_specs=P(("cand", "tensor"), None),
        check_vma=False,
    )
```

```python
import functools

import jax
import jax.numpy as jnp
import numpy as np
from jax import lax
from jax.experimental import pallas as pl
from jax.experimental.pallas import tpu as pltpu
from jax.sharding import PartitionSpec as P

MIB = 1024 * 1024
LOG2E = 1.4426950408889634
OWN, NEAR, THIRD, LAST, EIGHTHS = range(5)
OFFSETS = (0, 6, 2, 4, 1, 7, 3, 5)


def rope_tables(rows, width):
    half_width = width // 2
    frequency = (1000000.0 ** (-(np.arange(half_width) * 2.0 / width))).astype(np.float32)
    angle = np.arange(rows, dtype=np.float32)[:, None] * frequency[None, :]
    angle = angle.astype(np.float64)
    cosine, sine = np.cos(angle), np.sin(angle)
    return (
        jnp.asarray(np.concatenate([cosine, cosine], axis=1).astype(np.float32)),
        jnp.asarray(np.concatenate([-sine, sine], axis=1).astype(np.float32)),
    )


def norm_rope(vectors, gain, cosine, sine):
    scale = lax.rsqrt(jnp.mean(vectors * vectors, axis=-1, keepdims=True) + 1e-06)
    vectors = vectors * scale * gain
    return vectors * cosine + pltpu.roll(vectors, vectors.shape[-1] // 2, 1) * sine


def params(mebibytes):
    return pltpu.CompilerParams(vmem_limit_bytes=mebibytes * MIB)


def cost(flops):
    return pl.CostEstimate(flops=flops, bytes_accessed=1, transcendentals=0)


def after(array, cue):
    return lax.optimization_barrier((array, cue))[0]


def whole(*shape):
    return pl.BlockSpec(shape, lambda *_: (0,) * len(shape))


def summed(refs):
    total = refs[0][...]
    for ref in refs[1:]:
        total = total + ref[...]
    return total


def partial_kernel(counts, with_acc, places_ref, *refs):
    rows = []
    for count in counts:
        rows.append(summed(refs[:count]))
        refs = refs[count:]
    hidden = jnp.concatenate(rows, axis=0) if len(rows) > 1 else rows[0]
    weights, outs = refs[:3], refs[-3:]
    accs = refs[3:6] if with_acc else (None,) * 3
    step = pl.program_id(0)

    def add(w_ref, acc_ref, out_ref):
        product = jnp.dot(hidden, w_ref[...], preferred_element_type=jnp.float32)
        out_ref[...] = product if acc_ref is None else product + acc_ref[...]

    add(weights[0], accs[0], outs[0])

    @pl.when(step == 0)
    def _():
        add(weights[1], accs[1], outs[1])
        add(weights[2], accs[2], outs[2])


def partial_projection(places, slot, parts, weights, accs):
    features = parts[0][0].shape[1]
    rows = sum(part[0].shape[0] for part in parts)
    arrivals = [array for part in parts for array in part]
    widths = [weight.shape[1] for weight in weights]
    tile = 512
    column = lambda height: pl.BlockSpec((height, tile), lambda i, p: (0, i))
    per_array = lambda height: [column(height), whole(height, widths[1]), whole(height, widths[2])]
    block = lambda width: pl.BlockSpec((features, width), lambda i, p: (p[slot], 0))
    in_specs = [whole(*array.shape) for array in arrivals]
    in_specs.append(pl.BlockSpec((features, tile), lambda i, p: (p[slot], i)))
    in_specs += [block(widths[1]), block(widths[2])]
    operands = [*arrivals, *weights]
    if accs is not None:
        in_specs += per_array(rows)
        operands += accs
    return pl.pallas_call(
        functools.partial(partial_kernel, [len(part) for part in parts], accs is not None),
        grid_spec=pltpu.PrefetchScalarGridSpec(
            num_scalar_prefetch=1,
            grid=(widths[0] // tile,),
            in_specs=in_specs,
            out_specs=per_array(rows),
        ),
        out_shape=[jax.ShapeDtypeStruct((rows, width), jnp.float32) for width in widths],
        compiler_params=params(20),
        cost_estimate=cost(1),
        name="partial_projection",
    )(places, *operands)


def keys_values_kernel(count, n_before, places_ref, *refs):
    before, refs = refs[:n_before], refs[n_before:]
    hidden = summed(refs[:count])
    wk_ref, wv_ref, acck_ref, accv_ref, gain_ref, cos_ref, sin_ref = refs[count : count + 7]
    refs = refs[count + 7 :]
    head = gain_ref.shape[1]
    out_ref = refs[0] if n_before == 0 else refs[1]
    keys = acck_ref[...] + jnp.dot(hidden, wk_ref[...], preferred_element_type=jnp.float32)
    values = accv_ref[...] + jnp.dot(hidden, wv_ref[...], preferred_element_type=jnp.float32)
    keys = norm_rope(keys, gain_ref[...], cos_ref[...], sin_ref[...])
    out_ref[:, :head] = keys.astype(jnp.bfloat16)
    out_ref[:, head:] = values.astype(jnp.bfloat16)
    if n_before:
        pos_ref, summary_ref = refs[0], refs[2]
        picks = pos_ref.shape[1]
        picked, start = None, 0
        for ref in (*before, out_ref):
            rows = ref.shape[0]
            row = lax.broadcasted_iota(jnp.int32, (rows, picks), 0) + start
            chosen = jnp.where(row == pos_ref[...], 1.0, 0.0).astype(jnp.bfloat16)
            found = lax.dot_general(
                chosen, ref[...], (((0,), (0,)), ((), ())), preferred_element_type=jnp.float32
            )
            picked = found if picked is None else picked + found
            start += rows
        summary_ref[...] = picked.astype(jnp.bfloat16)


def keys_values(places, hidden, part, weights, accs, gain, cosine, sine, before=(), positions=None):
    rows, features = hidden[0].shape
    head = gain.shape[1]
    row_part = pl.BlockSpec((rows, head), lambda i, p: (part, 0))
    block = pl.BlockSpec((features, head), lambda i, p: (p[LAST], 0))
    in_specs = [whole(*array.shape) for array in (*before, *hidden)]
    in_specs += [block, block, row_part, row_part, whole(1, head), row_part, row_part]
    operands = [*before, *hidden, *weights, *accs, gain, cosine, sine]
    out_shape = [jax.ShapeDtypeStruct((rows, 2 * head), jnp.bfloat16)]
    if before:
        in_specs.append(whole(*positions.shape))
        operands.append(positions)
        out_shape.append(jax.ShapeDtypeStruct((positions.shape[1], 2 * head), jnp.bfloat16))
    return pl.pallas_call(
        functools.partial(keys_values_kernel, len(hidden), len(before)),
        grid_spec=pltpu.PrefetchScalarGridSpec(
            num_scalar_prefetch=1,
            grid=(1,),
            in_specs=in_specs,
            out_specs=[whole(*shape.shape) for shape in out_shape],
        ),
        out_shape=out_shape,
        compiler_params=params(12),
        cost_estimate=cost(1),
        name="keys_values",
    )(places, *operands)


def queries_kernel(count, places_ref, *refs):
    hidden = summed(refs[:count])
    w_ref, acc_ref, gain_ref, cos_ref, sin_ref, q_ref = refs[count:]
    head = gain_ref.shape[1]
    proj = acc_ref[...] + jnp.dot(hidden, w_ref[...], preferred_element_type=jnp.float32)
    for start in range(0, proj.shape[1], head):
        one = norm_rope(proj[:, start : start + head], gain_ref[...], cos_ref[...], sin_ref[...])
        q_ref[:, start : start + head] = one.astype(jnp.bfloat16)


def queries_of(places, hidden, part, weights, acc, gain, cosine, sine):
    rows, features = hidden[0].shape
    head = gain.shape[1]
    width = weights.shape[1]
    tile = 4 * head
    row_part = pl.BlockSpec((rows, head), lambda i, p: (part, 0))
    return pl.pallas_call(
        functools.partial(queries_kernel, len(hidden)),
        grid_spec=pltpu.PrefetchScalarGridSpec(
            num_scalar_prefetch=1,
            grid=(width // tile,),
            in_specs=[whole(rows, features) for _ in hidden]
            + [
                pl.BlockSpec((features, tile), lambda i, p: (p[LAST], i)),
                pl.BlockSpec((rows, tile), lambda i, p: (part, i)),
                whole(1, head),
                row_part,
                row_part,
            ],
            out_specs=pl.BlockSpec((rows, tile), lambda i, p: (0, i)),
        ),
        out_shape=jax.ShapeDtypeStruct((rows, width), jnp.bfloat16),
        compiler_params=params(12),
        cost_estimate=cost(1),
        name="queries",
    )(places, *hidden, weights, acc, gain, cosine, sine)


def attention_kernel(slots, n_parts, n_others, stack, places_ref, length_ref, *refs):
    q_parts, refs = refs[:n_parts], refs[n_parts:]
    own_parts, refs = refs[:n_parts], refs[n_parts:]
    others, refs = refs[:n_others], refs[n_others:]
    o_refs, (keys_all, values_all) = refs[:-2], refs[-2:]
    part_rows, width = own_parts[0].shape
    head = width // 2
    picks = others[0].shape[0]
    cross = n_others * picks
    rows = o_refs[0].shape[0]

    start = 0
    for ref in (*others, *own_parts):
        stop = start + ref.shape[0]
        keys_all[start:stop, :] = ref[:, :head]
        values_all[start:stop, :] = ref[:, head:]
        start = stop

    scale = head ** (-0.5) * LOG2E
    own_rows = n_parts * part_rows
    for slot, o_ref in zip(slots, o_refs):
        first = places_ref[slot] * rows
        offset = pl.multiple_of(lax.rem(first, part_rows), rows)
        row = lax.broadcasted_iota(jnp.int32, (rows, own_rows), 0) + first
        column = lax.broadcasted_iota(jnp.int32, (rows, own_rows), 1)
        allowed = jnp.concatenate([column <= row] * stack, axis=0)
        position = lax.broadcasted_iota(jnp.int32, (rows, head), 0) + first
        kept = jnp.concatenate([position < length_ref[0]] * stack, axis=0)
        for left in range(0, o_ref.shape[1], stack * head):
            lanes = [slice(left + i * head, left + (i + 1) * head) for i in range(stack)]
            queries = [q_parts[0][pl.ds(offset, rows), lane] for lane in lanes]
            for part in range(1, n_parts):
                here = first >= part * part_rows
                queries = [
                    jnp.where(here, q_parts[part][pl.ds(offset, rows), lane], query)
                    for lane, query in zip(lanes, queries)
                ]
            scores = lax.dot_general(
                jnp.concatenate(queries, axis=0),
                keys_all[...],
                (((1,), (1,)), ((), ())),
                preferred_element_type=jnp.float32,
            )
            own = jnp.where(allowed, scores[:, cross:], -1e30)
            free = scores[:, :cross]
            largest = jnp.maximum(
                jnp.max(free, axis=1, keepdims=True), jnp.max(own, axis=1, keepdims=True)
            )
            free = jnp.exp2((free - largest) * scale)
            own = jnp.exp2((own - largest) * scale)
            total = jnp.sum(free, axis=1, keepdims=True) + jnp.sum(own, axis=1, keepdims=True)
            mixed = jnp.dot(
                free.astype(jnp.bfloat16), values_all[:cross, :], preferred_element_type=jnp.float32
            ) + jnp.dot(
                own.astype(jnp.bfloat16), values_all[cross:, :], preferred_element_type=jnp.float32
            )
            mixed = jnp.where(kept, mixed / total, 0.0).astype(jnp.bfloat16)
            for index, lane in enumerate(lanes):
                o_ref[:, lane] = mixed[index * rows : (index + 1) * rows, :]


def attention(places, slots, rows, lengths, queries, own, others):
    n_parts = len(own)
    part_rows, width = queries[0].shape
    head = own[0].shape[1] // 2
    picks = others[0].shape[0]
    reach = n_parts * part_rows + len(others) * picks
    return pl.pallas_call(
        functools.partial(attention_kernel, slots, n_parts, len(others), 512 // rows),
        grid_spec=pltpu.PrefetchScalarGridSpec(
            num_scalar_prefetch=2,
            grid=(1,),
            in_specs=[whole(*array.shape) for array in (*queries, *own, *others)],
            out_specs=[whole(rows, width) for _ in slots],
            scratch_shapes=[
                pltpu.VMEM((reach, head), jnp.bfloat16),
                pltpu.VMEM((reach, head), jnp.bfloat16),
            ],
        ),
        out_shape=[jax.ShapeDtypeStruct((rows, width), jnp.bfloat16) for _ in slots],
        compiler_params=params(24 if reach <= 2048 else 56),
        cost_estimate=cost(1),
        name="attention",
    )(places, lengths, *queries, *own, *others)


def mix_kernel(rows_ref, w_ref, out_ref):
    total = jnp.dot(rows_ref[...], w_ref[...], preferred_element_type=jnp.float32)
    out_ref[...] = total.astype(out_ref.dtype)


def mix(attended, w_out, which):
    rows, depth = attended.shape
    width = w_out.shape[1] // 2
    tiles = 5
    tile = width // tiles
    return pl.pallas_call(
        mix_kernel,
        grid=(tiles,),
        in_specs=[
            whole(rows, depth),
            pl.BlockSpec((depth, tile), lambda i: (0, i + which * tiles)),
        ],
        out_specs=pl.BlockSpec((rows, tile), lambda i: (0, i)),
        out_shape=jax.ShapeDtypeStruct((rows, width), jnp.bfloat16),
        compiler_params=params(8),
        cost_estimate=cost(1),
        name="mix",
    )(attended, w_out)


def eighth_kernel(places_ref, w_ref, out_ref):
    out_ref[...] = w_ref[...]


def eighth(places, which, w_out, share):
    width = w_out.shape[1] // 2
    return pl.pallas_call(
        eighth_kernel,
        grid_spec=pltpu.PrefetchScalarGridSpec(
            num_scalar_prefetch=1,
            grid=(1,),
            in_specs=[pl.BlockSpec((share, width), lambda i, p: (p[EIGHTHS + which], 1))],
            out_specs=whole(share, width),
        ),
        out_shape=jax.ShapeDtypeStruct((share, width), w_out.dtype),
        compiler_params=params(8),
        cost_estimate=cost(1),
        name="eighth",
    )(places, w_out)


def mix_sent_kernel(places_ref, rows_ref, *refs):
    pieces, out_ref = refs[:-1], refs[-1]
    share = rows_ref.shape[1] // len(OFFSETS)
    rows = []
    for index in range(len(OFFSETS)):
        start = pl.multiple_of(places_ref[EIGHTHS + index] * share, share)
        rows.append(rows_ref[:, pl.ds(start, share)])
    total = jnp.dot(
        jnp.concatenate(rows, axis=1),
        jnp.concatenate([piece[...] for piece in pieces], axis=0),
        preferred_element_type=jnp.float32,
    )
    out_ref[...] = total.astype(out_ref.dtype)


def mix_sent(places, attended, pieces):
    rows, depth = attended.shape
    width = pieces[0].shape[1]
    tile = width // 5
    column = lambda height: pl.BlockSpec((height, tile), lambda i, p: (0, i))
    return pl.pallas_call(
        mix_sent_kernel,
        grid_spec=pltpu.PrefetchScalarGridSpec(
            num_scalar_prefetch=1,
            grid=(width // tile,),
            in_specs=[whole(rows, depth)] + [column(piece.shape[0]) for piece in pieces],
            out_specs=column(rows),
        ),
        out_shape=jax.ShapeDtypeStruct((rows, width), jnp.bfloat16),
        compiler_params=params(8),
        cost_estimate=cost(1),
        name="mix_sent",
    )(places, attended, *pieces)


def add_kernel(count, *refs):
    total = refs[0][...].astype(jnp.float32)
    for ref in refs[1:count]:
        total = total + ref[...].astype(jnp.float32)
    refs[-1][...] = total.astype(jnp.bfloat16)


def added(*arrays, half=None, into=None):
    rows, width = arrays[0].shape
    wide = 1 if half is None else 2
    at = half or 0
    operands = list(arrays)
    in_specs = [whole(rows, width) for _ in arrays]
    aliases = {}
    if into is not None:
        operands.append(into)
        in_specs.append(pl.BlockSpec(memory_space=pl.ANY))
        aliases = {len(arrays): 0}
    return pl.pallas_call(
        functools.partial(add_kernel, len(arrays)),
        grid=(1,),
        in_specs=in_specs,
        out_specs=pl.BlockSpec((rows, width), lambda i: (0, at)),
        out_shape=jax.ShapeDtypeStruct((rows, wide * width), jnp.bfloat16),
        input_output_aliases=aliases,
        compiler_params=params(8),
        cost_estimate=cost(1),
        name="added",
    )(*operands)


def shards(hidden_in, lengths, summary_pos, w_query, w_key, w_value, w_out, q_gain, k_gain):
    rows_here = hidden_in.shape[0]
    head_width = q_gain.shape[0]
    place = lax.axis_index("tensor")
    n_cand = lax.axis_size("cand")
    assert lax.axis_size("tensor") == 4 and w_key.shape[1] == head_width

    def swap(array):
        return lax.ppermute(array, "tensor", [(0, 1), (1, 0), (2, 3), (3, 2)])

    def across(array):
        return lax.ppermute(array, "tensor", [(1, 2), (2, 1)])

    def outward(array):
        return lax.ppermute(array, "tensor", [(1, 0), (2, 3)])

    def inward(array):
        return lax.ppermute(array, "tensor", [(0, 1), (3, 2)])

    def between(array, offset):
        return lax.ppermute(array, "cand", [(i, i ^ offset) for i in range(n_cand)])

    low = place < 2
    near = jnp.bitwise_xor(place, 1)
    places = [place, near, jnp.where(low, 2, 1), jnp.where(low, 3, 0)]
    places += [jnp.bitwise_xor(lax.axis_index("cand"), offset) for offset in OFFSETS]
    places = jnp.stack(places).astype(jnp.int32)
    share = w_out.shape[0] // n_cand
    spread = n_cand == len(OFFSETS) and share % 128 == 0
    tables = rope_tables(rows_here, head_width)
    k_gain, q_gain = k_gain[None], q_gain[None]
    weights = [w_query, w_key, w_value]
    half = rows_here // 2

    mine = [lax.slice_in_dim(hidden_in, i * half, (i + 1) * half) for i in (0, 1)]
    from_near, from_mid = [], []
    for array in mine:
        from_near.append(swap(array))
        from_mid.append(across(array))
    accs = partial_projection(places, OWN, [[hidden_in]], weights, None)
    from_near[0], from_mid[0], accs = lax.optimization_barrier((from_near[0], from_mid[0], accs))
    to_outer = [outward(array) for array in from_mid]
    cue = (from_near[1], from_mid[1])
    accs = partial_projection(
        after(places, cue), NEAR, [[a] for a in from_near], weights, accs
    )
    to_inner = [across(from_near[0])]
    to_inner.append(across(after(from_near[1], (to_outer[0], accs))))
    end = [outward(array) for array in to_inner]
    pieces = {}
    if spread:
        first, second = (eighth(places, i, w_out, share) for i in (0, 1))
        pieces[0] = inward(after(first, to_outer[0]))
        cue = (to_inner[1], to_outer[1])
        pieces[6] = inward(after(second, cue))
        first = after(pieces[0], cue)
        pieces[2], pieces[4] = between(first, 2), between(first, 4)
    cue = (to_inner, accs)
    accs = partial_projection(
        after(places, cue), THIRD, [[a, b] for a, b in zip(from_mid, to_outer)], weights, accs
    )

    final = [[a, b] for a, b in zip(to_inner, end)]
    (own_first,) = keys_values(places, final[0], 0, weights[1:], accs[1:], k_gain, *tables)
    first_queries = queries_of(places, final[0], 0, w_query, accs[0], q_gain, *tables)
    own_second, summary = keys_values(
        places,
        final[1],
        1,
        weights[1:],
        after(accs[1:], (first_queries, pieces)),
        k_gain,
        *tables,
        [own_first],
        summary_pos,
    )
    own = [own_first, own_second]
    others = [between(summary, offset) for offset in range(1, n_cand)]
    second_queries = queries_of(places, final[1], 1, w_query, accs[0], q_gain, *tables)
    queries = [first_queries, second_queries]

    if spread:
        cue = (others, second_queries)
        for offset in (0, 6, 2, 4):
            pieces[offset ^ 1] = between(after(pieces[offset], cue), 1)

    def attend(slots):
        return attention(places, slots, rows_here // 4, lengths, queries, own, others)

    def send(rows, part):
        return inward(rows if spread else part)

    def share_of(arrived):
        if not spread:
            return arrived
        return mix_sent(places, arrived, [pieces[offset] for offset in OFFSETS])

    def mixed(rows):
        return [mix(rows, w_out, which) for which in (0, 1)]

    (far_rows,) = attend((LAST,))
    far = mixed(far_rows)
    far_sent = send(far_rows, far[1])
    places = after(places, far)
    (third_rows,) = attend((THIRD,))
    far_sent = after(far_sent, third_rows)
    far_in = inward(after(far[0], far_sent))
    far_right = added(far[1], share_of(far_sent))
    third = mixed(after(third_rows, far_right))
    third_sent = send(third_rows, third[1])
    far_right = across(far_right)
    places = after(places, third)
    near_rows, own_rows = attend((NEAR, OWN))
    far_left = added(far[0], after(far_in, near_rows))
    third_sent = after(third_sent, far_left)
    far_left = across(far_left)
    third_in = inward(after(third[0], third_sent))
    third_right = added(third[1], share_of(third_sent))
    near = mixed(after(near_rows, third_right))
    near_sent = send(near_rows, near[1])
    third_right = across(third_right)
    out_right = added(near[1], after(far_right, near))
    kept = mixed(after(own_rows, (out_right, far_left)))
    near_sent = after(near_sent, kept)
    near_in = inward(after(near[0], near_sent))
    near_sent = share_of(near_sent)
    third_left = added(third[0], after(third_in, near_sent))
    arrived = after((outward(out_right), third_right), third_left)
    result = added(kept[1], near_sent, *arrived, half=1)
    third_left = across(third_left)
    out_left = outward(added(near[0], after(far_left, result)))
    return added(kept[0], near_in, out_left, third_left, half=0, into=result)


def solution(mesh):
    return jax.shard_map(
        shards,
        mesh=mesh,
        in_specs=(
            P("cand", "tensor"),
            P("cand"),
            P("cand", None),
            P(None, "tensor"),
            P(None, "tensor"),
            P(None, "tensor"),
            P("tensor", None),
            P(),
            P(),
        ),
        out_specs=P(("cand", "tensor"), None),
        check_vma=False,
    )
```

```python
import functools

import jax
import jax.numpy as jnp
import numpy as np
from jax import lax
from jax.experimental import pallas as pl
from jax.experimental.pallas import tpu as pltpu
from jax.sharding import PartitionSpec as P

MIB = 1024 * 1024
LOG2E = 1.4426950408889634
OWN, NEAR, THIRD, LAST, EIGHTHS = range(5)
OFFSETS = (0, 6, 2, 4, 1, 7, 3, 5)


def rope_tables(rows, width):
    half_width = width // 2
    frequency = (1000000.0 ** (-(np.arange(half_width) * 2.0 / width))).astype(np.float32)
    angle = np.arange(rows, dtype=np.float32)[:, None] * frequency[None, :]
    angle = angle.astype(np.float64)
    cosine, sine = np.cos(angle), np.sin(angle)
    return (
        jnp.asarray(np.concatenate([cosine, cosine], axis=1).astype(np.float32)),
        jnp.asarray(np.concatenate([-sine, sine], axis=1).astype(np.float32)),
    )


def norm_rope(vectors, gain, cosine, sine):
    scale = lax.rsqrt(jnp.mean(vectors * vectors, axis=-1, keepdims=True) + 1e-06)
    vectors = vectors * scale * gain
    return vectors * cosine + pltpu.roll(vectors, vectors.shape[-1] // 2, 1) * sine


def params(mebibytes):
    return pltpu.CompilerParams(vmem_limit_bytes=mebibytes * MIB)


def cost(flops):
    return pl.CostEstimate(flops=flops, bytes_accessed=1, transcendentals=0)


def after(array, cue):
    return lax.optimization_barrier((array, cue))[0]


def whole(*shape):
    return pl.BlockSpec(shape, lambda *_: (0,) * len(shape))


def summed(refs):
    total = refs[0][...]
    for ref in refs[1:]:
        total = total + ref[...]
    return total


def partial_kernel(counts, with_acc, places_ref, *refs):
    rows = []
    for count in counts:
        rows.append(summed(refs[:count]))
        refs = refs[count:]
    hidden = jnp.concatenate(rows, axis=0) if len(rows) > 1 else rows[0]
    weights, outs = refs[:3], refs[-3:]
    accs = refs[3:6] if with_acc else (None,) * 3
    step = pl.program_id(0)

    def add(w_ref, acc_ref, out_ref):
        product = jnp.dot(hidden, w_ref[...], preferred_element_type=jnp.float32)
        out_ref[...] = product if acc_ref is None else product + acc_ref[...]

    add(weights[0], accs[0], outs[0])

    @pl.when(step == 0)
    def _():
        add(weights[1], accs[1], outs[1])
        add(weights[2], accs[2], outs[2])


def partial_projection(places, slot, parts, weights, accs):
    features = parts[0][0].shape[1]
    rows = sum(part[0].shape[0] for part in parts)
    arrivals = [array for part in parts for array in part]
    widths = [weight.shape[1] for weight in weights]
    tile = 512
    column = lambda height: pl.BlockSpec((height, tile), lambda i, p: (0, i))
    per_array = lambda height: [column(height), whole(height, widths[1]), whole(height, widths[2])]
    block = lambda width: pl.BlockSpec((features, width), lambda i, p: (p[slot], 0))
    in_specs = [whole(*array.shape) for array in arrivals]
    in_specs.append(pl.BlockSpec((features, tile), lambda i, p: (p[slot], i)))
    in_specs += [block(widths[1]), block(widths[2])]
    operands = [*arrivals, *weights]
    if accs is not None:
        in_specs += per_array(rows)
        operands += accs
    return pl.pallas_call(
        functools.partial(partial_kernel, [len(part) for part in parts], accs is not None),
        grid_spec=pltpu.PrefetchScalarGridSpec(
            num_scalar_prefetch=1,
            grid=(widths[0] // tile,),
            in_specs=in_specs,
            out_specs=per_array(rows),
        ),
        out_shape=[jax.ShapeDtypeStruct((rows, width), jnp.float32) for width in widths],
        compiler_params=params(20),
        cost_estimate=cost(1),
        name="partial_projection",
    )(places, *operands)


def keys_values_kernel(count, n_before, places_ref, *refs):
    before, refs = refs[:n_before], refs[n_before:]
    hidden = summed(refs[:count])
    wk_ref, wv_ref, acck_ref, accv_ref, gain_ref, cos_ref, sin_ref = refs[count : count + 7]
    refs = refs[count + 7 :]
    head = gain_ref.shape[1]
    out_ref = refs[0] if n_before == 0 else refs[1]
    keys = acck_ref[...] + jnp.dot(hidden, wk_ref[...], preferred_element_type=jnp.float32)
    values = accv_ref[...] + jnp.dot(hidden, wv_ref[...], preferred_element_type=jnp.float32)
    keys = norm_rope(keys, gain_ref[...], cos_ref[...], sin_ref[...])
    out_ref[:, :head] = keys.astype(jnp.bfloat16)
    out_ref[:, head:] = values.astype(jnp.bfloat16)
    if n_before:
        pos_ref, summary_ref = refs[0], refs[2]
        picks = pos_ref.shape[1]
        picked, start = None, 0
        for ref in (*before, out_ref):
            rows = ref.shape[0]
            row = lax.broadcasted_iota(jnp.int32, (rows, picks), 0) + start
            chosen = jnp.where(row == pos_ref[...], 1.0, 0.0).astype(jnp.bfloat16)
            found = lax.dot_general(
                chosen, ref[...], (((0,), (0,)), ((), ())), preferred_element_type=jnp.float32
            )
            picked = found if picked is None else picked + found
            start += rows
        summary_ref[...] = picked.astype(jnp.bfloat16)


def keys_values(places, hidden, part, weights, accs, gain, cosine, sine, before=(), positions=None):
    rows, features = hidden[0].shape
    head = gain.shape[1]
    row_part = pl.BlockSpec((rows, head), lambda i, p: (part, 0))
    block = pl.BlockSpec((features, head), lambda i, p: (p[LAST], 0))
    in_specs = [whole(*array.shape) for array in (*before, *hidden)]
    in_specs += [block, block, row_part, row_part, whole(1, head), row_part, row_part]
    operands = [*before, *hidden, *weights, *accs, gain, cosine, sine]
    out_shape = [jax.ShapeDtypeStruct((rows, 2 * head), jnp.bfloat16)]
    if before:
        in_specs.append(whole(*positions.shape))
        operands.append(positions)
        out_shape.append(jax.ShapeDtypeStruct((positions.shape[1], 2 * head), jnp.bfloat16))
    return pl.pallas_call(
        functools.partial(keys_values_kernel, len(hidden), len(before)),
        grid_spec=pltpu.PrefetchScalarGridSpec(
            num_scalar_prefetch=1,
            grid=(1,),
            in_specs=in_specs,
            out_specs=[whole(*shape.shape) for shape in out_shape],
        ),
        out_shape=out_shape,
        compiler_params=params(12),
        cost_estimate=cost(1),
        name="keys_values",
    )(places, *operands)


def queries_kernel(count, places_ref, *refs):
    hidden = summed(refs[:count])
    w_ref, acc_ref, gain_ref, cos_ref, sin_ref, q_ref = refs[count:]
    head = gain_ref.shape[1]
    proj = acc_ref[...] + jnp.dot(hidden, w_ref[...], preferred_element_type=jnp.float32)
    for start in range(0, proj.shape[1], head):
        one = norm_rope(proj[:, start : start + head], gain_ref[...], cos_ref[...], sin_ref[...])
        q_ref[:, start : start + head] = one.astype(jnp.bfloat16)


def queries_of(places, hidden, part, weights, acc, gain, cosine, sine):
    rows, features = hidden[0].shape
    head = gain.shape[1]
    width = weights.shape[1]
    tile = 4 * head
    row_part = pl.BlockSpec((rows, head), lambda i, p: (part, 0))
    return pl.pallas_call(
        functools.partial(queries_kernel, len(hidden)),
        grid_spec=pltpu.PrefetchScalarGridSpec(
            num_scalar_prefetch=1,
            grid=(width // tile,),
            in_specs=[whole(rows, features) for _ in hidden]
            + [
                pl.BlockSpec((features, tile), lambda i, p: (p[LAST], i)),
                pl.BlockSpec((rows, tile), lambda i, p: (part, i)),
                whole(1, head),
                row_part,
                row_part,
            ],
            out_specs=pl.BlockSpec((rows, tile), lambda i, p: (0, i)),
        ),
        out_shape=jax.ShapeDtypeStruct((rows, width), jnp.bfloat16),
        compiler_params=params(12),
        cost_estimate=cost(1),
        name="queries",
    )(places, *hidden, weights, acc, gain, cosine, sine)


def attention_kernel(slots, n_parts, n_others, stack, places_ref, length_ref, *refs):
    q_parts, refs = refs[:n_parts], refs[n_parts:]
    own_parts, refs = refs[:n_parts], refs[n_parts:]
    others, refs = refs[:n_others], refs[n_others:]
    o_refs, (keys_all, values_all) = refs[:-2], refs[-2:]
    part_rows, width = own_parts[0].shape
    head = width // 2
    picks = others[0].shape[0]
    cross = n_others * picks
    rows = o_refs[0].shape[0]

    start = 0
    for ref in (*others, *own_parts):
        stop = start + ref.shape[0]
        keys_all[start:stop, :] = ref[:, :head]
        values_all[start:stop, :] = ref[:, head:]
        start = stop

    scale = head ** (-0.5) * LOG2E
    own_rows = n_parts * part_rows
    for slot, o_ref in zip(slots, o_refs):
        first = places_ref[slot] * rows
        offset = pl.multiple_of(lax.rem(first, part_rows), rows)
        row = lax.broadcasted_iota(jnp.int32, (rows, own_rows), 0) + first
        column = lax.broadcasted_iota(jnp.int32, (rows, own_rows), 1)
        allowed = jnp.concatenate([column <= row] * stack, axis=0)
        position = lax.broadcasted_iota(jnp.int32, (rows, head), 0) + first
        kept = jnp.concatenate([position < length_ref[0]] * stack, axis=0)
        for left in range(0, o_ref.shape[1], stack * head):
            lanes = [slice(left + i * head, left + (i + 1) * head) for i in range(stack)]
            queries = [q_parts[0][pl.ds(offset, rows), lane] for lane in lanes]
            for part in range(1, n_parts):
                here = first >= part * part_rows
                queries = [
                    jnp.where(here, q_parts[part][pl.ds(offset, rows), lane], query)
                    for lane, query in zip(lanes, queries)
                ]
            scores = lax.dot_general(
                jnp.concatenate(queries, axis=0),
                keys_all[...],
                (((1,), (1,)), ((), ())),
                preferred_element_type=jnp.float32,
            )
            own = jnp.where(allowed, scores[:, cross:], -1e30)
            free = scores[:, :cross]
            largest = jnp.maximum(
                jnp.max(free, axis=1, keepdims=True), jnp.max(own, axis=1, keepdims=True)
            )
            free = jnp.exp2((free - largest) * scale)
            own = jnp.exp2((own - largest) * scale)
            total = jnp.sum(free, axis=1, keepdims=True) + jnp.sum(own, axis=1, keepdims=True)
            mixed = jnp.dot(
                free.astype(jnp.bfloat16), values_all[:cross, :], preferred_element_type=jnp.float32
            ) + jnp.dot(
                own.astype(jnp.bfloat16), values_all[cross:, :], preferred_element_type=jnp.float32
            )
            mixed = jnp.where(kept, mixed / total, 0.0).astype(jnp.bfloat16)
            for index, lane in enumerate(lanes):
                o_ref[:, lane] = mixed[index * rows : (index + 1) * rows, :]


def attention(places, slots, rows, lengths, queries, own, others):
    n_parts = len(own)
    part_rows, width = queries[0].shape
    head = own[0].shape[1] // 2
    picks = others[0].shape[0]
    reach = n_parts * part_rows + len(others) * picks
    return pl.pallas_call(
        functools.partial(attention_kernel, slots, n_parts, len(others), 512 // rows),
        grid_spec=pltpu.PrefetchScalarGridSpec(
            num_scalar_prefetch=2,
            grid=(1,),
            in_specs=[whole(*array.shape) for array in (*queries, *own, *others)],
            out_specs=[whole(rows, width) for _ in slots],
            scratch_shapes=[
                pltpu.VMEM((reach, head), jnp.bfloat16),
                pltpu.VMEM((reach, head), jnp.bfloat16),
            ],
        ),
        out_shape=[jax.ShapeDtypeStruct((rows, width), jnp.bfloat16) for _ in slots],
        compiler_params=params(24 if reach <= 2048 else 56),
        cost_estimate=cost(1),
        name="attention",
    )(places, lengths, *queries, *own, *others)


def mix_kernel(rows_ref, w_ref, out_ref):
    total = jnp.dot(rows_ref[...], w_ref[...], preferred_element_type=jnp.float32)
    out_ref[...] = total.astype(out_ref.dtype)


def mix(attended, w_out, which):
    rows, depth = attended.shape
    width = w_out.shape[1] // 2
    tiles = 5
    tile = width // tiles
    return pl.pallas_call(
        mix_kernel,
        grid=(tiles,),
        in_specs=[
            whole(rows, depth),
            pl.BlockSpec((depth, tile), lambda i: (0, i + which * tiles)),
        ],
        out_specs=pl.BlockSpec((rows, tile), lambda i: (0, i)),
        out_shape=jax.ShapeDtypeStruct((rows, width), jnp.bfloat16),
        compiler_params=params(8),
        cost_estimate=cost(1),
        name="mix",
    )(attended, w_out)


def eighth_kernel(places_ref, w_ref, out_ref):
    out_ref[...] = w_ref[...]


def eighth(places, which, w_out, share):
    width = w_out.shape[1] // 2
    return pl.pallas_call(
        eighth_kernel,
        grid_spec=pltpu.PrefetchScalarGridSpec(
            num_scalar_prefetch=1,
            grid=(1,),
            in_specs=[pl.BlockSpec((share, width), lambda i, p: (p[EIGHTHS + which], 1))],
            out_specs=whole(share, width),
        ),
        out_shape=jax.ShapeDtypeStruct((share, width), w_out.dtype),
        compiler_params=params(8),
        cost_estimate=cost(1),
        name="eighth",
    )(places, w_out)


def mix_sent_kernel(places_ref, rows_ref, *refs):
    pieces, out_ref = refs[:-1], refs[-1]
    share = rows_ref.shape[1] // len(OFFSETS)
    rows = []
    for index in range(len(OFFSETS)):
        start = pl.multiple_of(places_ref[EIGHTHS + index] * share, share)
        rows.append(rows_ref[:, pl.ds(start, share)])
    total = jnp.dot(
        jnp.concatenate(rows, axis=1),
        jnp.concatenate([piece[...] for piece in pieces], axis=0),
        preferred_element_type=jnp.float32,
    )
    out_ref[...] = total.astype(out_ref.dtype)


def mix_sent(places, attended, pieces):
    rows, depth = attended.shape
    width = pieces[0].shape[1]
    tile = width // 5
    column = lambda height: pl.BlockSpec((height, tile), lambda i, p: (0, i))
    return pl.pallas_call(
        mix_sent_kernel,
        grid_spec=pltpu.PrefetchScalarGridSpec(
            num_scalar_prefetch=1,
            grid=(width // tile,),
            in_specs=[whole(rows, depth)] + [column(piece.shape[0]) for piece in pieces],
            out_specs=column(rows),
        ),
        out_shape=jax.ShapeDtypeStruct((rows, width), jnp.bfloat16),
        compiler_params=params(8),
        cost_estimate=cost(1),
        name="mix_sent",
    )(places, attended, *pieces)


def halves_kernel(ref, first_ref, second_ref):
    half = first_ref.shape[0]
    first_ref[...] = ref[:half, :]
    second_ref[...] = ref[half:, :]


def halves(array):
    rows, width = array.shape
    half = jax.ShapeDtypeStruct((rows // 2, width), array.dtype)
    return pl.pallas_call(
        halves_kernel,
        grid=(1,),
        in_specs=[whole(rows, width)],
        out_specs=[whole(rows // 2, width)] * 2,
        out_shape=[half, half],
        compiler_params=params(8),
        cost_estimate=cost(1),
        name="halves",
    )(array)


def add_kernel(count, *refs):
    total = refs[0][...].astype(jnp.float32)
    for ref in refs[1:count]:
        total = total + ref[...].astype(jnp.float32)
    refs[-1][...] = total.astype(jnp.bfloat16)


def added(*arrays, half=None, into=None):
    rows, width = arrays[0].shape
    wide = 1 if half is None else 2
    at = half or 0
    operands = list(arrays)
    in_specs = [whole(rows, width) for _ in arrays]
    aliases = {}
    if into is not None:
        operands.append(into)
        in_specs.append(pl.BlockSpec(memory_space=pl.ANY))
        aliases = {len(arrays): 0}
    return pl.pallas_call(
        functools.partial(add_kernel, len(arrays)),
        grid=(1,),
        in_specs=in_specs,
        out_specs=pl.BlockSpec((rows, width), lambda i: (0, at)),
        out_shape=jax.ShapeDtypeStruct((rows, wide * width), jnp.bfloat16),
        input_output_aliases=aliases,
        compiler_params=params(8),
        cost_estimate=cost(1),
        name="added",
    )(*operands)


def shards(hidden_in, lengths, summary_pos, w_query, w_key, w_value, w_out, q_gain, k_gain):
    rows_here = hidden_in.shape[0]
    head_width = q_gain.shape[0]
    place = lax.axis_index("tensor")
    n_cand = lax.axis_size("cand")
    assert lax.axis_size("tensor") == 4 and w_key.shape[1] == head_width

    def swap(array):
        return lax.ppermute(array, "tensor", [(0, 1), (1, 0), (2, 3), (3, 2)])

    def across(array):
        return lax.ppermute(array, "tensor", [(1, 2), (2, 1)])

    def outward(array):
        return lax.ppermute(array, "tensor", [(1, 0), (2, 3)])

    def inward(array):
        return lax.ppermute(array, "tensor", [(0, 1), (3, 2)])

    def between(array, offset):
        return lax.ppermute(array, "cand", [(i, i ^ offset) for i in range(n_cand)])

    low = place < 2
    near = jnp.bitwise_xor(place, 1)
    places = [place, near, jnp.where(low, 2, 1), jnp.where(low, 3, 0)]
    places += [jnp.bitwise_xor(lax.axis_index("cand"), offset) for offset in OFFSETS]
    places = jnp.stack(places).astype(jnp.int32)
    share = w_out.shape[0] // n_cand
    spread = n_cand == len(OFFSETS) and share % 128 == 0
    tables = rope_tables(rows_here, head_width)
    k_gain, q_gain = k_gain[None], q_gain[None]
    weights = [w_query, w_key, w_value]
    half = rows_here // 2

    from_near = swap(hidden_in)
    from_mid = [across(array) for array in halves(hidden_in)]
    accs = partial_projection(places, OWN, [[hidden_in]], weights, None)
    from_mid[0], accs = lax.optimization_barrier((from_mid[0], accs))
    to_outer = [outward(array) for array in from_mid]
    accs = partial_projection(after(places, from_mid[1]), NEAR, [[from_near]], weights, accs)
    from_near = halves(from_near)
    to_inner = [across(from_near[0])]
    to_inner.append(across(after(from_near[1], (to_outer[0], accs))))
    end = [outward(array) for array in to_inner]
    pieces = {}
    if spread:
        first, second = (eighth(places, i, w_out, share) for i in (0, 1))
        pieces[0] = inward(after(first, to_outer[0]))
        cue = (to_inner[1], to_outer[1])
        pieces[6] = inward(after(second, cue))
        first = after(pieces[0], cue)
        pieces[2], pieces[4] = between(first, 2), between(first, 4)
    cue = (to_inner, accs)
    accs = partial_projection(
        after(places, cue), THIRD, [[a, b] for a, b in zip(from_mid, to_outer)], weights, accs
    )

    final = [[a, b] for a, b in zip(to_inner, end)]
    (own_first,) = keys_values(places, final[0], 0, weights[1:], accs[1:], k_gain, *tables)
    first_queries = queries_of(places, final[0], 0, w_query, accs[0], q_gain, *tables)
    own_second, summary = keys_values(
        places,
        final[1],
        1,
        weights[1:],
        after(accs[1:], (first_queries, pieces)),
        k_gain,
        *tables,
        [own_first],
        summary_pos,
    )
    own = [own_first, own_second]
    others = [between(summary, offset) for offset in range(1, n_cand)]
    second_queries = queries_of(places, final[1], 1, w_query, accs[0], q_gain, *tables)
    queries = [first_queries, second_queries]

    if spread:
        cue = (others, second_queries)
        for offset in (0, 6, 2, 4):
            pieces[offset ^ 1] = between(after(pieces[offset], cue), 1)

    def attend(slots):
        return attention(places, slots, rows_here // 4, lengths, queries, own, others)

    def send(rows, part):
        return inward(rows if spread else part)

    def share_of(arrived):
        if not spread:
            return arrived
        return mix_sent(places, arrived, [pieces[offset] for offset in OFFSETS])

    def mixed(rows):
        return [mix(rows, w_out, which) for which in (0, 1)]

    (far_rows,) = attend((LAST,))
    far = mixed(far_rows)
    far_sent = send(far_rows, far[1])
    places = after(places, far)
    (third_rows,) = attend((THIRD,))
    far_sent = after(far_sent, third_rows)
    far_in = inward(after(far[0], far_sent))
    far_right = added(far[1], share_of(far_sent))
    third = mixed(after(third_rows, far_right))
    third_sent = send(third_rows, third[1])
    far_right = across(far_right)
    places = after(places, third)
    near_rows, own_rows = attend((NEAR, OWN))
    far_left = added(far[0], after(far_in, near_rows))
    third_sent = after(third_sent, far_left)
    far_left = across(far_left)
    third_in = inward(third[0])
    third_right = added(third[1], share_of(third_sent))
    near = mixed(after(near_rows, third_right))
    near_sent = send(near_rows, near[1])
    third_right = across(third_right)
    out_right = added(near[1], after(far_right, near))
    kept = mixed(after(own_rows, (out_right, far_left)))
    out_left = added(near[0], after(far_left, kept))
    third_left = added(third[0], after(third_in, out_left))
    near_sent = share_of(after(near_sent, third_left))
    result = added(kept[1], near_sent, outward(out_right), third_right, half=1)
    near_in = inward(after(near[0], third_left))
    out_left, third_left = outward(out_left), across(third_left)
    return added(kept[0], near_in, out_left, third_left, half=0, into=result)


def solution(mesh):
    return jax.shard_map(
        shards,
        mesh=mesh,
        in_specs=(
            P("cand", "tensor"),
            P("cand"),
            P("cand", None),
            P(None, "tensor"),
            P(None, "tensor"),
            P(None, "tensor"),
            P("tensor", None),
            P(),
            P(),
        ),
        out_specs=P(("cand", "tensor"), None),
        check_vma=False,
    )
```

```python
import functools

import jax
import jax.numpy as jnp
import numpy as np
from jax import lax
from jax.experimental import pallas as pl
from jax.experimental.pallas import tpu as pltpu
from jax.sharding import PartitionSpec as P

MIB = 1024 * 1024
LOG2E = 1.4426950408889634
OWN, NEAR, THIRD, LAST, EIGHTHS = range(5)
OFFSETS = (0, 6, 2, 4, 1, 7, 3, 5)


def rope_tables(rows, width):
    half_width = width // 2
    frequency = (1000000.0 ** (-(np.arange(half_width) * 2.0 / width))).astype(np.float32)
    angle = np.arange(rows, dtype=np.float32)[:, None] * frequency[None, :]
    angle = angle.astype(np.float64)
    cosine, sine = np.cos(angle), np.sin(angle)
    return (
        jnp.asarray(np.concatenate([cosine, cosine], axis=1).astype(np.float32)),
        jnp.asarray(np.concatenate([-sine, sine], axis=1).astype(np.float32)),
    )


def norm_rope(vectors, gain, cosine, sine):
    scale = lax.rsqrt(jnp.mean(vectors * vectors, axis=-1, keepdims=True) + 1e-06)
    vectors = vectors * scale * gain
    return vectors * cosine + pltpu.roll(vectors, vectors.shape[-1] // 2, 1) * sine


def params(mebibytes):
    return pltpu.CompilerParams(vmem_limit_bytes=mebibytes * MIB)


def cost(flops):
    return pl.CostEstimate(flops=flops, bytes_accessed=1, transcendentals=0)


def after(array, cue):
    return lax.optimization_barrier((array, cue))[0]


def whole(*shape):
    return pl.BlockSpec(shape, lambda *_: (0,) * len(shape))


def summed(refs):
    total = refs[0][...]
    for ref in refs[1:]:
        total = total + ref[...]
    return total


def partial_kernel(counts, with_acc, places_ref, *refs):
    rows = []
    for count in counts:
        rows.append(summed(refs[:count]))
        refs = refs[count:]
    hidden = jnp.concatenate(rows, axis=0) if len(rows) > 1 else rows[0]
    weights, outs = refs[:3], refs[-3:]
    accs = refs[3:6] if with_acc else (None,) * 3
    step = pl.program_id(0)

    def add(w_ref, acc_ref, out_ref):
        product = jnp.dot(hidden, w_ref[...], preferred_element_type=jnp.float32)
        out_ref[...] = product if acc_ref is None else product + acc_ref[...]

    add(weights[0], accs[0], outs[0])

    @pl.when(step == 0)
    def _():
        add(weights[1], accs[1], outs[1])
        add(weights[2], accs[2], outs[2])


def partial_projection(places, slot, parts, weights, accs):
    features = parts[0][0].shape[1]
    rows = sum(part[0].shape[0] for part in parts)
    arrivals = [array for part in parts for array in part]
    widths = [weight.shape[1] for weight in weights]
    tile = 512
    column = lambda height: pl.BlockSpec((height, tile), lambda i, p: (0, i))
    per_array = lambda height: [column(height), whole(height, widths[1]), whole(height, widths[2])]
    block = lambda width: pl.BlockSpec((features, width), lambda i, p: (p[slot], 0))
    in_specs = [whole(*array.shape) for array in arrivals]
    in_specs.append(pl.BlockSpec((features, tile), lambda i, p: (p[slot], i)))
    in_specs += [block(widths[1]), block(widths[2])]
    operands = [*arrivals, *weights]
    if accs is not None:
        in_specs += per_array(rows)
        operands += accs
    return pl.pallas_call(
        functools.partial(partial_kernel, [len(part) for part in parts], accs is not None),
        grid_spec=pltpu.PrefetchScalarGridSpec(
            num_scalar_prefetch=1,
            grid=(widths[0] // tile,),
            in_specs=in_specs,
            out_specs=per_array(rows),
        ),
        out_shape=[jax.ShapeDtypeStruct((rows, width), jnp.float32) for width in widths],
        compiler_params=params(20),
        cost_estimate=cost(1),
        name="partial_projection",
    )(places, *operands)


def keys_values_kernel(count, n_before, places_ref, *refs):
    before, refs = refs[:n_before], refs[n_before:]
    hidden = summed(refs[:count])
    wk_ref, wv_ref, acck_ref, accv_ref, gain_ref, cos_ref, sin_ref = refs[count : count + 7]
    refs = refs[count + 7 :]
    head = gain_ref.shape[1]
    out_ref = refs[0] if n_before == 0 else refs[1]
    keys = acck_ref[...] + jnp.dot(hidden, wk_ref[...], preferred_element_type=jnp.float32)
    values = accv_ref[...] + jnp.dot(hidden, wv_ref[...], preferred_element_type=jnp.float32)
    keys = norm_rope(keys, gain_ref[...], cos_ref[...], sin_ref[...])
    out_ref[:, :head] = keys.astype(jnp.bfloat16)
    out_ref[:, head:] = values.astype(jnp.bfloat16)
    if n_before:
        pos_ref, summary_ref = refs[0], refs[2]
        picks = pos_ref.shape[1]
        picked, start = None, 0
        for ref in (*before, out_ref):
            rows = ref.shape[0]
            row = lax.broadcasted_iota(jnp.int32, (rows, picks), 0) + start
            chosen = jnp.where(row == pos_ref[...], 1.0, 0.0).astype(jnp.bfloat16)
            found = lax.dot_general(
                chosen, ref[...], (((0,), (0,)), ((), ())), preferred_element_type=jnp.float32
            )
            picked = found if picked is None else picked + found
            start += rows
        summary_ref[...] = picked.astype(jnp.bfloat16)


def keys_values(places, hidden, part, weights, accs, gain, cosine, sine, before=(), positions=None):
    rows, features = hidden[0].shape
    head = gain.shape[1]
    row_part = pl.BlockSpec((rows, head), lambda i, p: (part, 0))
    block = pl.BlockSpec((features, head), lambda i, p: (p[LAST], 0))
    in_specs = [whole(*array.shape) for array in (*before, *hidden)]
    in_specs += [block, block, row_part, row_part, whole(1, head), row_part, row_part]
    operands = [*before, *hidden, *weights, *accs, gain, cosine, sine]
    out_shape = [jax.ShapeDtypeStruct((rows, 2 * head), jnp.bfloat16)]
    if before:
        in_specs.append(whole(*positions.shape))
        operands.append(positions)
        out_shape.append(jax.ShapeDtypeStruct((positions.shape[1], 2 * head), jnp.bfloat16))
    return pl.pallas_call(
        functools.partial(keys_values_kernel, len(hidden), len(before)),
        grid_spec=pltpu.PrefetchScalarGridSpec(
            num_scalar_prefetch=1,
            grid=(1,),
            in_specs=in_specs,
            out_specs=[whole(*shape.shape) for shape in out_shape],
        ),
        out_shape=out_shape,
        compiler_params=params(12),
        cost_estimate=cost(1),
        name="keys_values",
    )(places, *operands)


def queries_kernel(count, places_ref, *refs):
    hidden = summed(refs[:count])
    w_ref, acc_ref, gain_ref, cos_ref, sin_ref, q_ref = refs[count:]
    head = gain_ref.shape[1]
    proj = acc_ref[...] + jnp.dot(hidden, w_ref[...], preferred_element_type=jnp.float32)
    for start in range(0, proj.shape[1], head):
        one = norm_rope(proj[:, start : start + head], gain_ref[...], cos_ref[...], sin_ref[...])
        q_ref[:, start : start + head] = one.astype(jnp.bfloat16)


def queries_of(places, hidden, part, weights, acc, gain, cosine, sine):
    rows, features = hidden[0].shape
    head = gain.shape[1]
    width = weights.shape[1]
    tile = 4 * head
    row_part = pl.BlockSpec((rows, head), lambda i, p: (part, 0))
    return pl.pallas_call(
        functools.partial(queries_kernel, len(hidden)),
        grid_spec=pltpu.PrefetchScalarGridSpec(
            num_scalar_prefetch=1,
            grid=(width // tile,),
            in_specs=[whole(rows, features) for _ in hidden]
            + [
                pl.BlockSpec((features, tile), lambda i, p: (p[LAST], i)),
                pl.BlockSpec((rows, tile), lambda i, p: (part, i)),
                whole(1, head),
                row_part,
                row_part,
            ],
            out_specs=pl.BlockSpec((rows, tile), lambda i, p: (0, i)),
        ),
        out_shape=jax.ShapeDtypeStruct((rows, width), jnp.bfloat16),
        compiler_params=params(12),
        cost_estimate=cost(1),
        name="queries",
    )(places, *hidden, weights, acc, gain, cosine, sine)


def attention_kernel(slots, n_parts, n_others, stack, places_ref, length_ref, *refs):
    q_parts, refs = refs[:n_parts], refs[n_parts:]
    own_parts, refs = refs[:n_parts], refs[n_parts:]
    others, refs = refs[:n_others], refs[n_others:]
    o_refs, (keys_all, values_all) = refs[:-2], refs[-2:]
    part_rows, width = own_parts[0].shape
    head = width // 2
    picks = others[0].shape[0]
    cross = n_others * picks
    rows = o_refs[0].shape[0]

    start = 0
    for ref in (*others, *own_parts):
        stop = start + ref.shape[0]
        keys_all[start:stop, :] = ref[:, :head]
        values_all[start:stop, :] = ref[:, head:]
        start = stop

    scale = head ** (-0.5) * LOG2E
    own_rows = n_parts * part_rows
    for slot, o_ref in zip(slots, o_refs):
        first = places_ref[slot] * rows
        offset = pl.multiple_of(lax.rem(first, part_rows), rows)
        row = lax.broadcasted_iota(jnp.int32, (rows, own_rows), 0) + first
        column = lax.broadcasted_iota(jnp.int32, (rows, own_rows), 1)
        allowed = jnp.concatenate([column <= row] * stack, axis=0)
        position = lax.broadcasted_iota(jnp.int32, (rows, head), 0) + first
        kept = jnp.concatenate([position < length_ref[0]] * stack, axis=0)
        for left in range(0, o_ref.shape[1], stack * head):
            lanes = [slice(left + i * head, left + (i + 1) * head) for i in range(stack)]
            queries = [q_parts[0][pl.ds(offset, rows), lane] for lane in lanes]
            for part in range(1, n_parts):
                here = first >= part * part_rows
                queries = [
                    jnp.where(here, q_parts[part][pl.ds(offset, rows), lane], query)
                    for lane, query in zip(lanes, queries)
                ]
            scores = lax.dot_general(
                jnp.concatenate(queries, axis=0),
                keys_all[...],
                (((1,), (1,)), ((), ())),
                preferred_element_type=jnp.float32,
            )
            own = jnp.where(allowed, scores[:, cross:], -1e30)
            free = scores[:, :cross]
            largest = jnp.maximum(
                jnp.max(free, axis=1, keepdims=True), jnp.max(own, axis=1, keepdims=True)
            )
            free = jnp.exp2((free - largest) * scale)
            own = jnp.exp2((own - largest) * scale)
            total = jnp.sum(free, axis=1, keepdims=True) + jnp.sum(own, axis=1, keepdims=True)
            mixed = jnp.dot(
                free.astype(jnp.bfloat16), values_all[:cross, :], preferred_element_type=jnp.float32
            ) + jnp.dot(
                own.astype(jnp.bfloat16), values_all[cross:, :], preferred_element_type=jnp.float32
            )
            mixed = jnp.where(kept, mixed / total, 0.0).astype(jnp.bfloat16)
            for index, lane in enumerate(lanes):
                o_ref[:, lane] = mixed[index * rows : (index + 1) * rows, :]


def attention(places, slots, rows, lengths, queries, own, others):
    n_parts = len(own)
    part_rows, width = queries[0].shape
    head = own[0].shape[1] // 2
    picks = others[0].shape[0]
    reach = n_parts * part_rows + len(others) * picks
    return pl.pallas_call(
        functools.partial(attention_kernel, slots, n_parts, len(others), 512 // rows),
        grid_spec=pltpu.PrefetchScalarGridSpec(
            num_scalar_prefetch=2,
            grid=(1,),
            in_specs=[whole(*array.shape) for array in (*queries, *own, *others)],
            out_specs=[whole(rows, width) for _ in slots],
            scratch_shapes=[
                pltpu.VMEM((reach, head), jnp.bfloat16),
                pltpu.VMEM((reach, head), jnp.bfloat16),
            ],
        ),
        out_shape=[jax.ShapeDtypeStruct((rows, width), jnp.bfloat16) for _ in slots],
        compiler_params=params(24 if reach <= 2048 else 56),
        cost_estimate=cost(1),
        name="attention",
    )(places, lengths, *queries, *own, *others)


def mix_kernel(rows_ref, w_ref, out_ref):
    total = jnp.dot(rows_ref[...], w_ref[...], preferred_element_type=jnp.float32)
    out_ref[...] = total.astype(out_ref.dtype)


def mix(attended, w_out, which):
    rows, depth = attended.shape
    width = w_out.shape[1] // 2
    tiles = 5
    tile = width // tiles
    return pl.pallas_call(
        mix_kernel,
        grid=(tiles,),
        in_specs=[
            whole(rows, depth),
            pl.BlockSpec((depth, tile), lambda i: (0, i + which * tiles)),
        ],
        out_specs=pl.BlockSpec((rows, tile), lambda i: (0, i)),
        out_shape=jax.ShapeDtypeStruct((rows, width), jnp.bfloat16),
        compiler_params=params(8),
        cost_estimate=cost(1),
        name="mix",
    )(attended, w_out)


def eighth_kernel(places_ref, w_ref, out_ref):
    out_ref[...] = w_ref[...]


def eighth(places, which, w_out, share):
    width = w_out.shape[1] // 2
    return pl.pallas_call(
        eighth_kernel,
        grid_spec=pltpu.PrefetchScalarGridSpec(
            num_scalar_prefetch=1,
            grid=(1,),
            in_specs=[pl.BlockSpec((share, width), lambda i, p: (p[EIGHTHS + which], 1))],
            out_specs=whole(share, width),
        ),
        out_shape=jax.ShapeDtypeStruct((share, width), w_out.dtype),
        compiler_params=params(8),
        cost_estimate=cost(1),
        name="eighth",
    )(places, w_out)


def mix_sent_kernel(places_ref, rows_ref, *refs):
    pieces, out_ref = refs[:-1], refs[-1]
    share = rows_ref.shape[1] // len(OFFSETS)
    rows = []
    for index in range(len(OFFSETS)):
        start = pl.multiple_of(places_ref[EIGHTHS + index] * share, share)
        rows.append(rows_ref[:, pl.ds(start, share)])
    total = jnp.dot(
        jnp.concatenate(rows, axis=1),
        jnp.concatenate([piece[...] for piece in pieces], axis=0),
        preferred_element_type=jnp.float32,
    )
    out_ref[...] = total.astype(out_ref.dtype)


def mix_sent(places, attended, pieces):
    rows, depth = attended.shape
    width = pieces[0].shape[1]
    tile = width // 5
    column = lambda height: pl.BlockSpec((height, tile), lambda i, p: (0, i))
    return pl.pallas_call(
        mix_sent_kernel,
        grid_spec=pltpu.PrefetchScalarGridSpec(
            num_scalar_prefetch=1,
            grid=(width // tile,),
            in_specs=[whole(rows, depth)] + [column(piece.shape[0]) for piece in pieces],
            out_specs=column(rows),
        ),
        out_shape=jax.ShapeDtypeStruct((rows, width), jnp.bfloat16),
        compiler_params=params(8),
        cost_estimate=cost(1),
        name="mix_sent",
    )(places, attended, *pieces)


def halves_kernel(ref, first_ref, second_ref):
    half = first_ref.shape[0]
    first_ref[...] = ref[:half, :]
    second_ref[...] = ref[half:, :]


def halves(array):
    rows, width = array.shape
    half = jax.ShapeDtypeStruct((rows // 2, width), array.dtype)
    return pl.pallas_call(
        halves_kernel,
        grid=(1,),
        in_specs=[whole(rows, width)],
        out_specs=[whole(rows // 2, width)] * 2,
        out_shape=[half, half],
        compiler_params=params(8),
        cost_estimate=cost(1),
        name="halves",
    )(array)


def add_kernel(count, *refs):
    total = refs[0][...].astype(jnp.float32)
    for ref in refs[1:count]:
        total = total + ref[...].astype(jnp.float32)
    refs[-1][...] = total.astype(jnp.bfloat16)


def added(*arrays, half=None, into=None):
    rows, width = arrays[0].shape
    wide = 1 if half is None else 2
    at = half or 0
    operands = list(arrays)
    in_specs = [whole(rows, width) for _ in arrays]
    aliases = {}
    if into is not None:
        operands.append(into)
        in_specs.append(pl.BlockSpec(memory_space=pl.ANY))
        aliases = {len(arrays): 0}
    return pl.pallas_call(
        functools.partial(add_kernel, len(arrays)),
        grid=(1,),
        in_specs=in_specs,
        out_specs=pl.BlockSpec((rows, width), lambda i: (0, at)),
        out_shape=jax.ShapeDtypeStruct((rows, wide * width), jnp.bfloat16),
        input_output_aliases=aliases,
        compiler_params=params(8),
        cost_estimate=cost(1),
        name="added",
    )(*operands)


def shards(hidden_in, lengths, summary_pos, w_query, w_key, w_value, w_out, q_gain, k_gain):
    rows_here = hidden_in.shape[0]
    head_width = q_gain.shape[0]
    place = lax.axis_index("tensor")
    n_cand = lax.axis_size("cand")
    assert lax.axis_size("tensor") == 4 and w_key.shape[1] == head_width

    def swap(array):
        return lax.ppermute(array, "tensor", [(0, 1), (1, 0), (2, 3), (3, 2)])

    def across(array):
        return lax.ppermute(array, "tensor", [(1, 2), (2, 1)])

    def outward(array):
        return lax.ppermute(array, "tensor", [(1, 0), (2, 3)])

    def inward(array):
        return lax.ppermute(array, "tensor", [(0, 1), (3, 2)])

    def between(array, offset):
        return lax.ppermute(array, "cand", [(i, i ^ offset) for i in range(n_cand)])

    low = place < 2
    near = jnp.bitwise_xor(place, 1)
    places = [place, near, jnp.where(low, 2, 1), jnp.where(low, 3, 0)]
    places += [jnp.bitwise_xor(lax.axis_index("cand"), offset) for offset in OFFSETS]
    places = jnp.stack(places).astype(jnp.int32)
    share = w_out.shape[0] // n_cand
    spread = n_cand == len(OFFSETS) and share % 128 == 0
    tables = rope_tables(rows_here, head_width)
    k_gain, q_gain = k_gain[None], q_gain[None]
    weights = [w_query, w_key, w_value]
    half = rows_here // 2

    from_near = swap(hidden_in)
    from_mid = [across(array) for array in halves(hidden_in)]
    accs = partial_projection(places, OWN, [[hidden_in]], weights, None)
    from_mid[0], accs = lax.optimization_barrier((from_mid[0], accs))
    to_outer = [outward(array) for array in from_mid]
    accs = partial_projection(after(places, from_mid[1]), NEAR, [[from_near]], weights, accs)
    from_near = halves(from_near)
    to_inner = [across(from_near[0])]
    to_inner.append(across(after(from_near[1], (to_outer[0], accs))))
    end = [outward(array) for array in to_inner]
    pieces = {}
    if spread:
        first, second = (eighth(places, i, w_out, share) for i in (0, 1))
        pieces[0] = inward(after(first, to_outer[0]))
        cue = (to_inner[1], to_outer[1])
        pieces[6] = inward(after(second, cue))
        first = after(pieces[0], cue)
        pieces[2], pieces[4] = between(first, 2), between(first, 4)
    cue = (to_inner, accs)
    accs = partial_projection(
        after(places, cue), THIRD, [[a, b] for a, b in zip(from_mid, to_outer)], weights, accs
    )

    final = [[a, b] for a, b in zip(to_inner, end)]
    (own_first,) = keys_values(places, final[0], 0, weights[1:], accs[1:], k_gain, *tables)
    first_queries = queries_of(places, final[0], 0, w_query, accs[0], q_gain, *tables)
    own_second, summary = keys_values(
        places,
        final[1],
        1,
        weights[1:],
        after(accs[1:], (first_queries, pieces)),
        k_gain,
        *tables,
        [own_first],
        summary_pos,
    )
    own = [own_first, own_second]
    others = [between(summary, offset) for offset in range(1, n_cand)]
    second_queries = queries_of(places, final[1], 1, w_query, accs[0], q_gain, *tables)
    queries = [first_queries, second_queries]

    if spread:
        cue = (others, second_queries)
        for offset in (0, 6, 2, 4):
            pieces[offset ^ 1] = between(after(pieces[offset], cue), 1)

    def attend(slots):
        return attention(places, slots, rows_here // 4, lengths, queries, own, others)

    def send(rows, part):
        return inward(rows if spread else part)

    def share_of(arrived):
        if not spread:
            return arrived
        return mix_sent(places, arrived, [pieces[offset] for offset in OFFSETS])

    def mixed(rows):
        return [mix(rows, w_out, which) for which in (0, 1)]

    (far_rows,) = attend((LAST,))
    far = mixed(far_rows)
    far_sent = send(far_rows, far[1])
    places = after(places, far)
    (third_rows,) = attend((THIRD,))
    far_sent = after(far_sent, third_rows)
    far_in = inward(after(far[0], far_sent))
    far_right = added(far[1], share_of(far_sent))
    places = after(places, far_right)
    near_rows, own_rows = attend((NEAR, OWN))
    third = mixed(after(third_rows, near_rows))
    third_sent = send(third_rows, third[1])
    far_right = across(far_right)
    far_left = added(far[0], after(far_in, third))
    third_sent = after(third_sent, far_left)
    far_left = across(far_left)
    third_in = inward(after(third[0], third_sent))
    third_right = added(third[1], share_of(third_sent))
    near = mixed(after(near_rows, (third_right, far_right)))
    near_sent = send(near_rows, near[1])
    third_right = across(third_right)
    out_right = added(near[1], after(far_right, near))
    kept = mixed(after(own_rows, (out_right, far_left)))
    out_left = added(near[0], after(far_left, kept))
    third_left = added(third[0], after(third_in, out_left))
    near_sent = share_of(after(near_sent, third_left))
    result = added(kept[1], near_sent, outward(out_right), third_right, half=1)
    near_in = inward(after(near[0], third_left))
    out_left, third_left = outward(out_left), across(third_left)
    return added(kept[0], near_in, out_left, third_left, half=0, into=result)


def solution(mesh):
    return jax.shard_map(
        shards,
        mesh=mesh,
        in_specs=(
            P("cand", "tensor"),
            P("cand"),
            P("cand", None),
            P(None, "tensor"),
            P(None, "tensor"),
            P(None, "tensor"),
            P("tensor", None),
            P(),
            P(),
        ),
        out_specs=P(("cand", "tensor"), None),
        check_vma=False,
    )
```

```python
import functools

import jax
import jax.numpy as jnp
import numpy as np
from jax import lax
from jax.experimental import pallas as pl
from jax.experimental.pallas import tpu as pltpu
from jax.sharding import PartitionSpec as P

MIB = 1024 * 1024
LOG2E = 1.4426950408889634
OWN, NEAR, THIRD, LAST, EIGHTHS = range(5)
OFFSETS = (0, 6, 2, 4, 1, 7, 3, 5)


def rope_tables(rows, width):
    half_width = width // 2
    frequency = (1000000.0 ** (-(np.arange(half_width) * 2.0 / width))).astype(np.float32)
    angle = np.arange(rows, dtype=np.float32)[:, None] * frequency[None, :]
    angle = angle.astype(np.float64)
    cosine, sine = np.cos(angle), np.sin(angle)
    return (
        jnp.asarray(np.concatenate([cosine, cosine], axis=1).astype(np.float32)),
        jnp.asarray(np.concatenate([-sine, sine], axis=1).astype(np.float32)),
    )


def norm_rope(vectors, gain, cosine, sine):
    scale = lax.rsqrt(jnp.mean(vectors * vectors, axis=-1, keepdims=True) + 1e-06)
    vectors = vectors * scale * gain
    return vectors * cosine + pltpu.roll(vectors, vectors.shape[-1] // 2, 1) * sine


def params(mebibytes):
    return pltpu.CompilerParams(vmem_limit_bytes=mebibytes * MIB)


def cost(flops):
    return pl.CostEstimate(flops=flops, bytes_accessed=1, transcendentals=0)


def after(array, cue):
    return lax.optimization_barrier((array, cue))[0]


def whole(*shape):
    return pl.BlockSpec(shape, lambda *_: (0,) * len(shape))


def summed(refs):
    total = refs[0][...]
    for ref in refs[1:]:
        total = total + ref[...]
    return total


def partial_kernel(counts, with_acc, places_ref, *refs):
    rows = []
    for count in counts:
        rows.append(summed(refs[:count]))
        refs = refs[count:]
    hidden = jnp.concatenate(rows, axis=0) if len(rows) > 1 else rows[0]
    weights, outs = refs[:3], refs[-3:]
    accs = refs[3:6] if with_acc else (None,) * 3
    step = pl.program_id(0)

    def add(w_ref, acc_ref, out_ref):
        product = jnp.dot(hidden, w_ref[...], preferred_element_type=jnp.float32)
        out_ref[...] = product if acc_ref is None else product + acc_ref[...]

    add(weights[0], accs[0], outs[0])

    @pl.when(step == 0)
    def _():
        add(weights[1], accs[1], outs[1])
        add(weights[2], accs[2], outs[2])


def partial_projection(places, slot, parts, weights, accs):
    features = parts[0][0].shape[1]
    rows = sum(part[0].shape[0] for part in parts)
    arrivals = [array for part in parts for array in part]
    widths = [weight.shape[1] for weight in weights]
    tile = 512
    column = lambda height: pl.BlockSpec((height, tile), lambda i, p: (0, i))
    per_array = lambda height: [column(height), whole(height, widths[1]), whole(height, widths[2])]
    block = lambda width: pl.BlockSpec((features, width), lambda i, p: (p[slot], 0))
    in_specs = [whole(*array.shape) for array in arrivals]
    in_specs.append(pl.BlockSpec((features, tile), lambda i, p: (p[slot], i)))
    in_specs += [block(widths[1]), block(widths[2])]
    operands = [*arrivals, *weights]
    if accs is not None:
        in_specs += per_array(rows)
        operands += accs
    return pl.pallas_call(
        functools.partial(partial_kernel, [len(part) for part in parts], accs is not None),
        grid_spec=pltpu.PrefetchScalarGridSpec(
            num_scalar_prefetch=1,
            grid=(widths[0] // tile,),
            in_specs=in_specs,
            out_specs=per_array(rows),
        ),
        out_shape=[jax.ShapeDtypeStruct((rows, width), jnp.float32) for width in widths],
        compiler_params=params(20),
        cost_estimate=cost(1),
        name="partial_projection",
    )(places, *operands)


def keys_values_kernel(count, n_before, places_ref, *refs):
    before, refs = refs[:n_before], refs[n_before:]
    hidden = summed(refs[:count])
    wk_ref, wv_ref, acck_ref, accv_ref, gain_ref, cos_ref, sin_ref = refs[count : count + 7]
    refs = refs[count + 7 :]
    head = gain_ref.shape[1]
    out_ref = refs[0] if n_before == 0 else refs[1]
    keys = acck_ref[...] + jnp.dot(hidden, wk_ref[...], preferred_element_type=jnp.float32)
    values = accv_ref[...] + jnp.dot(hidden, wv_ref[...], preferred_element_type=jnp.float32)
    keys = norm_rope(keys, gain_ref[...], cos_ref[...], sin_ref[...])
    out_ref[:, :head] = keys.astype(jnp.bfloat16)
    out_ref[:, head:] = values.astype(jnp.bfloat16)
    if n_before:
        pos_ref, summary_ref = refs[0], refs[2]
        picks = pos_ref.shape[1]
        picked, start = None, 0
        for ref in (*before, out_ref):
            rows = ref.shape[0]
            row = lax.broadcasted_iota(jnp.int32, (rows, picks), 0) + start
            chosen = jnp.where(row == pos_ref[...], 1.0, 0.0).astype(jnp.bfloat16)
            found = lax.dot_general(
                chosen, ref[...], (((0,), (0,)), ((), ())), preferred_element_type=jnp.float32
            )
            picked = found if picked is None else picked + found
            start += rows
        summary_ref[...] = picked.astype(jnp.bfloat16)


def keys_values(places, hidden, part, weights, accs, gain, cosine, sine, before=(), positions=None):
    rows, features = hidden[0].shape
    head = gain.shape[1]
    row_part = pl.BlockSpec((rows, head), lambda i, p: (part, 0))
    block = pl.BlockSpec((features, head), lambda i, p: (p[LAST], 0))
    in_specs = [whole(*array.shape) for array in (*before, *hidden)]
    in_specs += [block, block, row_part, row_part, whole(1, head), row_part, row_part]
    operands = [*before, *hidden, *weights, *accs, gain, cosine, sine]
    out_shape = [jax.ShapeDtypeStruct((rows, 2 * head), jnp.bfloat16)]
    if before:
        in_specs.append(whole(*positions.shape))
        operands.append(positions)
        out_shape.append(jax.ShapeDtypeStruct((positions.shape[1], 2 * head), jnp.bfloat16))
    return pl.pallas_call(
        functools.partial(keys_values_kernel, len(hidden), len(before)),
        grid_spec=pltpu.PrefetchScalarGridSpec(
            num_scalar_prefetch=1,
            grid=(1,),
            in_specs=in_specs,
            out_specs=[whole(*shape.shape) for shape in out_shape],
        ),
        out_shape=out_shape,
        compiler_params=params(12),
        cost_estimate=cost(1),
        name="keys_values",
    )(places, *operands)


def queries_kernel(count, places_ref, *refs):
    hidden = summed(refs[:count])
    w_ref, acc_ref, gain_ref, cos_ref, sin_ref, q_ref = refs[count:]
    head = gain_ref.shape[1]
    proj = acc_ref[...] + jnp.dot(hidden, w_ref[...], preferred_element_type=jnp.float32)
    for start in range(0, proj.shape[1], head):
        one = norm_rope(proj[:, start : start + head], gain_ref[...], cos_ref[...], sin_ref[...])
        q_ref[:, start : start + head] = one.astype(jnp.bfloat16)


def queries_of(places, hidden, part, weights, acc, gain, cosine, sine):
    rows, features = hidden[0].shape
    head = gain.shape[1]
    width = weights.shape[1]
    tile = 4 * head
    row_part = pl.BlockSpec((rows, head), lambda i, p: (part, 0))
    return pl.pallas_call(
        functools.partial(queries_kernel, len(hidden)),
        grid_spec=pltpu.PrefetchScalarGridSpec(
            num_scalar_prefetch=1,
            grid=(width // tile,),
            in_specs=[whole(rows, features) for _ in hidden]
            + [
                pl.BlockSpec((features, tile), lambda i, p: (p[LAST], i)),
                pl.BlockSpec((rows, tile), lambda i, p: (part, i)),
                whole(1, head),
                row_part,
                row_part,
            ],
            out_specs=pl.BlockSpec((rows, tile), lambda i, p: (0, i)),
        ),
        out_shape=jax.ShapeDtypeStruct((rows, width), jnp.bfloat16),
        compiler_params=params(12),
        cost_estimate=cost(1),
        name="queries",
    )(places, *hidden, weights, acc, gain, cosine, sine)


def attention_kernel(slots, n_parts, n_others, stack, places_ref, length_ref, *refs):
    q_parts, refs = refs[:n_parts], refs[n_parts:]
    own_parts, refs = refs[:n_parts], refs[n_parts:]
    others, refs = refs[:n_others], refs[n_others:]
    o_refs, (keys_all, values_all) = refs[:-2], refs[-2:]
    part_rows, width = own_parts[0].shape
    head = width // 2
    picks = others[0].shape[0]
    cross = n_others * picks
    rows = o_refs[0].shape[0]

    start = 0
    for ref in (*others, *own_parts):
        stop = start + ref.shape[0]
        keys_all[start:stop, :] = ref[:, :head]
        values_all[start:stop, :] = ref[:, head:]
        start = stop

    scale = head ** (-0.5) * LOG2E
    own_rows = n_parts * part_rows
    for slot, o_ref in zip(slots, o_refs):
        first = places_ref[slot] * rows
        offset = pl.multiple_of(lax.rem(first, part_rows), rows)
        row = lax.broadcasted_iota(jnp.int32, (rows, own_rows), 0) + first
        column = lax.broadcasted_iota(jnp.int32, (rows, own_rows), 1)
        allowed = jnp.concatenate([column <= row] * stack, axis=0)
        position = lax.broadcasted_iota(jnp.int32, (rows, head), 0) + first
        kept = jnp.concatenate([position < length_ref[0]] * stack, axis=0)
        for left in range(0, o_ref.shape[1], stack * head):
            lanes = [slice(left + i * head, left + (i + 1) * head) for i in range(stack)]
            queries = [q_parts[0][pl.ds(offset, rows), lane] for lane in lanes]
            for part in range(1, n_parts):
                here = first >= part * part_rows
                queries = [
                    jnp.where(here, q_parts[part][pl.ds(offset, rows), lane], query)
                    for lane, query in zip(lanes, queries)
                ]
            scores = lax.dot_general(
                jnp.concatenate(queries, axis=0),
                keys_all[...],
                (((1,), (1,)), ((), ())),
                preferred_element_type=jnp.float32,
            )
            own = jnp.where(allowed, scores[:, cross:], -1e30)
            free = scores[:, :cross]
            largest = jnp.maximum(
                jnp.max(free, axis=1, keepdims=True), jnp.max(own, axis=1, keepdims=True)
            )
            free = jnp.exp2((free - largest) * scale)
            own = jnp.exp2((own - largest) * scale)
            total = jnp.sum(free, axis=1, keepdims=True) + jnp.sum(own, axis=1, keepdims=True)
            mixed = jnp.dot(
                free.astype(jnp.bfloat16), values_all[:cross, :], preferred_element_type=jnp.float32
            ) + jnp.dot(
                own.astype(jnp.bfloat16), values_all[cross:, :], preferred_element_type=jnp.float32
            )
            mixed = jnp.where(kept, mixed / total, 0.0).astype(jnp.bfloat16)
            for index, lane in enumerate(lanes):
                o_ref[:, lane] = mixed[index * rows : (index + 1) * rows, :]


def attention(places, slots, rows, lengths, queries, own, others):
    n_parts = len(own)
    part_rows, width = queries[0].shape
    head = own[0].shape[1] // 2
    picks = others[0].shape[0]
    reach = n_parts * part_rows + len(others) * picks
    return pl.pallas_call(
        functools.partial(attention_kernel, slots, n_parts, len(others), 512 // rows),
        grid_spec=pltpu.PrefetchScalarGridSpec(
            num_scalar_prefetch=2,
            grid=(1,),
            in_specs=[whole(*array.shape) for array in (*queries, *own, *others)],
            out_specs=[whole(rows, width) for _ in slots],
            scratch_shapes=[
                pltpu.VMEM((reach, head), jnp.bfloat16),
                pltpu.VMEM((reach, head), jnp.bfloat16),
            ],
        ),
        out_shape=[jax.ShapeDtypeStruct((rows, width), jnp.bfloat16) for _ in slots],
        compiler_params=params(24 if reach <= 2048 else 56),
        cost_estimate=cost(1),
        name="attention",
    )(places, lengths, *queries, *own, *others)


def mix_kernel(rows_ref, w_ref, out_ref):
    total = jnp.dot(rows_ref[...], w_ref[...], preferred_element_type=jnp.float32)
    out_ref[...] = total.astype(out_ref.dtype)


def mix(attended, w_out, which):
    rows, depth = attended.shape
    width = w_out.shape[1] // 2
    tiles = 5
    tile = width // tiles
    return pl.pallas_call(
        mix_kernel,
        grid=(tiles,),
        in_specs=[
            whole(rows, depth),
            pl.BlockSpec((depth, tile), lambda i: (0, i + which * tiles)),
        ],
        out_specs=pl.BlockSpec((rows, tile), lambda i: (0, i)),
        out_shape=jax.ShapeDtypeStruct((rows, width), jnp.bfloat16),
        compiler_params=params(8),
        cost_estimate=cost(1),
        name="mix",
    )(attended, w_out)


def eighth_kernel(places_ref, w_ref, out_ref):
    out_ref[...] = w_ref[...]


def eighth(places, which, w_out, share):
    width = w_out.shape[1] // 2
    return pl.pallas_call(
        eighth_kernel,
        grid_spec=pltpu.PrefetchScalarGridSpec(
            num_scalar_prefetch=1,
            grid=(1,),
            in_specs=[pl.BlockSpec((share, width), lambda i, p: (p[EIGHTHS + which], 1))],
            out_specs=whole(share, width),
        ),
        out_shape=jax.ShapeDtypeStruct((share, width), w_out.dtype),
        compiler_params=params(8),
        cost_estimate=cost(1),
        name="eighth",
    )(places, w_out)


def mix_sent_kernel(places_ref, rows_ref, *refs):
    pieces, out_ref = refs[:-1], refs[-1]
    share = rows_ref.shape[1] // len(OFFSETS)
    rows = []
    for index in range(len(OFFSETS)):
        start = pl.multiple_of(places_ref[EIGHTHS + index] * share, share)
        rows.append(rows_ref[:, pl.ds(start, share)])
    total = jnp.dot(
        jnp.concatenate(rows, axis=1),
        jnp.concatenate([piece[...] for piece in pieces], axis=0),
        preferred_element_type=jnp.float32,
    )
    out_ref[...] = total.astype(out_ref.dtype)


def mix_sent(places, attended, pieces):
    rows, depth = attended.shape
    width = pieces[0].shape[1]
    tile = width // 5
    column = lambda height: pl.BlockSpec((height, tile), lambda i, p: (0, i))
    return pl.pallas_call(
        mix_sent_kernel,
        grid_spec=pltpu.PrefetchScalarGridSpec(
            num_scalar_prefetch=1,
            grid=(width // tile,),
            in_specs=[whole(rows, depth)] + [column(piece.shape[0]) for piece in pieces],
            out_specs=column(rows),
        ),
        out_shape=jax.ShapeDtypeStruct((rows, width), jnp.bfloat16),
        compiler_params=params(8),
        cost_estimate=cost(1),
        name="mix_sent",
    )(places, attended, *pieces)


def halves_kernel(ref, first_ref, second_ref):
    half = first_ref.shape[0]
    first_ref[...] = ref[:half, :]
    second_ref[...] = ref[half:, :]


def halves(array):
    rows, width = array.shape
    half = jax.ShapeDtypeStruct((rows // 2, width), array.dtype)
    return pl.pallas_call(
        halves_kernel,
        grid=(1,),
        in_specs=[whole(rows, width)],
        out_specs=[whole(rows // 2, width)] * 2,
        out_shape=[half, half],
        compiler_params=params(8),
        cost_estimate=cost(1),
        name="halves",
    )(array)


def add_kernel(count, *refs):
    total = refs[0][...].astype(jnp.float32)
    for ref in refs[1:count]:
        total = total + ref[...].astype(jnp.float32)
    refs[-1][...] = total.astype(jnp.bfloat16)


def added(*arrays, half=None, into=None):
    rows, width = arrays[0].shape
    wide = 1 if half is None else 2
    at = half or 0
    operands = list(arrays)
    in_specs = [whole(rows, width) for _ in arrays]
    aliases = {}
    if into is not None:
        operands.append(into)
        in_specs.append(pl.BlockSpec(memory_space=pl.ANY))
        aliases = {len(arrays): 0}
    return pl.pallas_call(
        functools.partial(add_kernel, len(arrays)),
        grid=(1,),
        in_specs=in_specs,
        out_specs=pl.BlockSpec((rows, width), lambda i: (0, at)),
        out_shape=jax.ShapeDtypeStruct((rows, wide * width), jnp.bfloat16),
        input_output_aliases=aliases,
        compiler_params=params(8),
        cost_estimate=cost(1),
        name="added",
    )(*operands)


def shards(hidden_in, lengths, summary_pos, w_query, w_key, w_value, w_out, q_gain, k_gain):
    rows_here = hidden_in.shape[0]
    head_width = q_gain.shape[0]
    place = lax.axis_index("tensor")
    n_cand = lax.axis_size("cand")
    assert lax.axis_size("tensor") == 4 and w_key.shape[1] == head_width

    def swap(array):
        return lax.ppermute(array, "tensor", [(0, 1), (1, 0), (2, 3), (3, 2)])

    def across(array):
        return lax.ppermute(array, "tensor", [(1, 2), (2, 1)])

    def outward(array):
        return lax.ppermute(array, "tensor", [(1, 0), (2, 3)])

    def inward(array):
        return lax.ppermute(array, "tensor", [(0, 1), (3, 2)])

    def between(array, offset):
        return lax.ppermute(array, "cand", [(i, i ^ offset) for i in range(n_cand)])

    low = place < 2
    near = jnp.bitwise_xor(place, 1)
    places = [place, near, jnp.where(low, 2, 1), jnp.where(low, 3, 0)]
    places += [jnp.bitwise_xor(lax.axis_index("cand"), offset) for offset in OFFSETS]
    places = jnp.stack(places).astype(jnp.int32)
    share = w_out.shape[0] // n_cand
    spread = n_cand == len(OFFSETS) and share % 128 == 0
    tables = rope_tables(rows_here, head_width)
    k_gain, q_gain = k_gain[None], q_gain[None]
    weights = [w_query, w_key, w_value]
    half = rows_here // 2

    from_near = swap(hidden_in)
    from_mid = [across(array) for array in halves(hidden_in)]
    accs = partial_projection(places, OWN, [[hidden_in]], weights, None)
    from_mid[0], accs = lax.optimization_barrier((from_mid[0], accs))
    to_outer = [outward(array) for array in from_mid]
    accs = partial_projection(after(places, from_mid[1]), NEAR, [[from_near]], weights, accs)
    from_near = halves(from_near)
    to_inner = [across(from_near[0])]
    to_inner.append(across(after(from_near[1], (to_outer[0], accs))))
    end = [outward(array) for array in to_inner]
    pieces = {}
    if spread:
        first, second = (eighth(places, i, w_out, share) for i in (0, 1))
        pieces[0] = inward(after(first, to_outer[0]))
        cue = (to_inner[1], to_outer[1])
        pieces[6] = inward(after(second, cue))
        first = after(pieces[0], cue)
        pieces[2], pieces[4] = between(first, 2), between(first, 4)
    cue = (to_inner, accs)
    accs = partial_projection(
        after(places, cue), THIRD, [[a, b] for a, b in zip(from_mid, to_outer)], weights, accs
    )

    final = [[a, b] for a, b in zip(to_inner, end)]
    (own_first,) = keys_values(places, final[0], 0, weights[1:], accs[1:], k_gain, *tables)
    first_queries = queries_of(places, final[0], 0, w_query, accs[0], q_gain, *tables)
    own_second, summary = keys_values(
        places,
        final[1],
        1,
        weights[1:],
        after(accs[1:], (first_queries, pieces)),
        k_gain,
        *tables,
        [own_first],
        summary_pos,
    )
    own = [own_first, own_second]
    others = [between(summary, offset) for offset in range(1, n_cand)]
    second_queries = queries_of(places, final[1], 1, w_query, accs[0], q_gain, *tables)
    queries = [first_queries, second_queries]

    if spread:
        cue = (others, second_queries)
        for offset in (0, 6, 2, 4):
            pieces[offset ^ 1] = between(after(pieces[offset], cue), 1)

    def attend(slots):
        return attention(places, slots, rows_here // 4, lengths, queries, own, others)

    def send(rows, part):
        return inward(rows if spread else part)

    def share_of(arrived):
        if not spread:
            return arrived
        return mix_sent(places, arrived, [pieces[offset] for offset in OFFSETS])

    def mixed(rows):
        return [mix(rows, w_out, which) for which in (0, 1)]

    (far_rows,) = attend((LAST,))
    far = mixed(far_rows)
    far_sent = after(send(far_rows, far[1]), far)
    far_in = inward(after(far[0], far_sent))
    far_right = added(far[1], share_of(far_sent))
    places = after(places, far_right)
    (third_rows,) = attend((THIRD,))
    third = mixed(third_rows)
    third_sent = send(third_rows, third[1])
    far_right = across(far_right)
    far_left = added(far[0], after(far_in, third))
    places = after(places, far_left)
    near_rows, own_rows = attend((NEAR, OWN))
    far_left = across(far_left)
    third_sent = after(third_sent, near_rows)
    third_in = inward(after(third[0], third_sent))
    near = [None, mix(near_rows, w_out, 1)]
    near_sent = send(near_rows, near[1])
    out_right = added(near[1], far_right)
    third_sent = after(third_sent, out_right)
    out_right = outward(out_right)
    third_right = added(third[1], share_of(third_sent))
    near[0] = mix(after(near_rows, third_right), w_out, 0)
    third_right = across(third_right)
    out_left = added(near[0], far_left)
    third_left = added(third[0], after(third_in, out_left))
    out_left = outward(out_left)
    near_sent = after(near_sent, third_left)
    kept = mixed(after(own_rows, near_sent))
    near_in = inward(after(near[0], (out_right, near_sent)))
    near_sent = share_of(near_sent)
    result = added(kept[1], near_sent, out_right, third_right, half=1)
    third_left = across(third_left)
    return added(kept[0], near_in, out_left, third_left, half=0, into=result)


def solution(mesh):
    return jax.shard_map(
        shards,
        mesh=mesh,
        in_specs=(
            P("cand", "tensor"),
            P("cand"),
            P("cand", None),
            P(None, "tensor"),
            P(None, "tensor"),
            P(None, "tensor"),
            P("tensor", None),
            P(),
            P(),
        ),
        out_specs=P(("cand", "tensor"), None),
        check_vma=False,
    )
```

```python
import functools

import jax
import jax.numpy as jnp
import numpy as np
from jax import lax
from jax.experimental import pallas as pl
from jax.experimental.pallas import tpu as pltpu
from jax.sharding import PartitionSpec as P

MIB = 1024 * 1024
LOG2E = 1.4426950408889634
OWN, NEAR, THIRD, LAST, EIGHTHS = range(5)
OFFSETS = (0, 6, 2, 4, 1, 7, 3, 5)


def rope_tables(rows, width):
    half_width = width // 2
    frequency = (1000000.0 ** (-(np.arange(half_width) * 2.0 / width))).astype(np.float32)
    angle = np.arange(rows, dtype=np.float32)[:, None] * frequency[None, :]
    angle = angle.astype(np.float64)
    cosine, sine = np.cos(angle), np.sin(angle)
    return (
        jnp.asarray(np.concatenate([cosine, cosine], axis=1).astype(np.float32)),
        jnp.asarray(np.concatenate([-sine, sine], axis=1).astype(np.float32)),
    )


def norm_rope(vectors, gain, cosine, sine):
    scale = lax.rsqrt(jnp.mean(vectors * vectors, axis=-1, keepdims=True) + 1e-06)
    vectors = vectors * scale * gain
    return vectors * cosine + pltpu.roll(vectors, vectors.shape[-1] // 2, 1) * sine


def params(mebibytes):
    return pltpu.CompilerParams(vmem_limit_bytes=mebibytes * MIB)


def cost(flops):
    return pl.CostEstimate(flops=flops, bytes_accessed=1, transcendentals=0)


def after(array, cue):
    return lax.optimization_barrier((array, cue))[0]


def whole(*shape):
    return pl.BlockSpec(shape, lambda *_: (0,) * len(shape))


def summed(refs):
    total = refs[0][...]
    for ref in refs[1:]:
        total = total + ref[...]
    return total


def partial_kernel(counts, with_acc, places_ref, *refs):
    rows = []
    for count in counts:
        rows.append(summed(refs[:count]))
        refs = refs[count:]
    hidden = jnp.concatenate(rows, axis=0) if len(rows) > 1 else rows[0]
    weights, outs = refs[:3], refs[-3:]
    accs = refs[3:6] if with_acc else (None,) * 3
    step = pl.program_id(0)

    def add(w_ref, acc_ref, out_ref):
        product = jnp.dot(hidden, w_ref[...], preferred_element_type=jnp.float32)
        out_ref[...] = product if acc_ref is None else product + acc_ref[...]

    add(weights[0], accs[0], outs[0])

    @pl.when(step == 0)
    def _():
        add(weights[1], accs[1], outs[1])
        add(weights[2], accs[2], outs[2])


def partial_projection(places, slot, parts, weights, accs):
    features = parts[0][0].shape[1]
    rows = sum(part[0].shape[0] for part in parts)
    arrivals = [array for part in parts for array in part]
    widths = [weight.shape[1] for weight in weights]
    tile = 512
    column = lambda height: pl.BlockSpec((height, tile), lambda i, p: (0, i))
    per_array = lambda height: [column(height), whole(height, widths[1]), whole(height, widths[2])]
    block = lambda width: pl.BlockSpec((features, width), lambda i, p: (p[slot], 0))
    in_specs = [whole(*array.shape) for array in arrivals]
    in_specs.append(pl.BlockSpec((features, tile), lambda i, p: (p[slot], i)))
    in_specs += [block(widths[1]), block(widths[2])]
    operands = [*arrivals, *weights]
    if accs is not None:
        in_specs += per_array(rows)
        operands += accs
    return pl.pallas_call(
        functools.partial(partial_kernel, [len(part) for part in parts], accs is not None),
        grid_spec=pltpu.PrefetchScalarGridSpec(
            num_scalar_prefetch=1,
            grid=(widths[0] // tile,),
            in_specs=in_specs,
            out_specs=per_array(rows),
        ),
        out_shape=[jax.ShapeDtypeStruct((rows, width), jnp.float32) for width in widths],
        compiler_params=params(20),
        cost_estimate=cost(1),
        name="partial_projection",
    )(places, *operands)


def keys_values_kernel(count, n_before, places_ref, *refs):
    before, refs = refs[:n_before], refs[n_before:]
    hidden = summed(refs[:count])
    wk_ref, wv_ref, acck_ref, accv_ref, gain_ref, cos_ref, sin_ref = refs[count : count + 7]
    refs = refs[count + 7 :]
    head = gain_ref.shape[1]
    out_ref = refs[0] if n_before == 0 else refs[1]
    keys = acck_ref[...] + jnp.dot(hidden, wk_ref[...], preferred_element_type=jnp.float32)
    values = accv_ref[...] + jnp.dot(hidden, wv_ref[...], preferred_element_type=jnp.float32)
    keys = norm_rope(keys, gain_ref[...], cos_ref[...], sin_ref[...])
    out_ref[:, :head] = keys.astype(jnp.bfloat16)
    out_ref[:, head:] = values.astype(jnp.bfloat16)
    if n_before:
        pos_ref, summary_ref = refs[0], refs[2]
        picks = pos_ref.shape[1]
        picked, start = None, 0
        for ref in (*before, out_ref):
            rows = ref.shape[0]
            row = lax.broadcasted_iota(jnp.int32, (rows, picks), 0) + start
            chosen = jnp.where(row == pos_ref[...], 1.0, 0.0).astype(jnp.bfloat16)
            found = lax.dot_general(
                chosen, ref[...], (((0,), (0,)), ((), ())), preferred_element_type=jnp.float32
            )
            picked = found if picked is None else picked + found
            start += rows
        summary_ref[...] = picked.astype(jnp.bfloat16)


def keys_values(places, hidden, part, weights, accs, gain, cosine, sine, before=(), positions=None):
    rows, features = hidden[0].shape
    head = gain.shape[1]
    row_part = pl.BlockSpec((rows, head), lambda i, p: (part, 0))
    block = pl.BlockSpec((features, head), lambda i, p: (p[LAST], 0))
    in_specs = [whole(*array.shape) for array in (*before, *hidden)]
    in_specs += [block, block, row_part, row_part, whole(1, head), row_part, row_part]
    operands = [*before, *hidden, *weights, *accs, gain, cosine, sine]
    out_shape = [jax.ShapeDtypeStruct((rows, 2 * head), jnp.bfloat16)]
    if before:
        in_specs.append(whole(*positions.shape))
        operands.append(positions)
        out_shape.append(jax.ShapeDtypeStruct((positions.shape[1], 2 * head), jnp.bfloat16))
    return pl.pallas_call(
        functools.partial(keys_values_kernel, len(hidden), len(before)),
        grid_spec=pltpu.PrefetchScalarGridSpec(
            num_scalar_prefetch=1,
            grid=(1,),
            in_specs=in_specs,
            out_specs=[whole(*shape.shape) for shape in out_shape],
        ),
        out_shape=out_shape,
        compiler_params=params(12),
        cost_estimate=cost(1),
        name="keys_values",
    )(places, *operands)


def queries_kernel(count, places_ref, *refs):
    hidden = summed(refs[:count])
    w_ref, acc_ref, gain_ref, cos_ref, sin_ref, q_ref = refs[count:]
    head = gain_ref.shape[1]
    proj = acc_ref[...] + jnp.dot(hidden, w_ref[...], preferred_element_type=jnp.float32)
    for start in range(0, proj.shape[1], head):
        one = norm_rope(proj[:, start : start + head], gain_ref[...], cos_ref[...], sin_ref[...])
        q_ref[:, start : start + head] = one.astype(jnp.bfloat16)


def queries_of(places, hidden, part, weights, acc, gain, cosine, sine):
    rows, features = hidden[0].shape
    head = gain.shape[1]
    width = weights.shape[1]
    tile = 4 * head
    row_part = pl.BlockSpec((rows, head), lambda i, p: (part, 0))
    return pl.pallas_call(
        functools.partial(queries_kernel, len(hidden)),
        grid_spec=pltpu.PrefetchScalarGridSpec(
            num_scalar_prefetch=1,
            grid=(width // tile,),
            in_specs=[whole(rows, features) for _ in hidden]
            + [
                pl.BlockSpec((features, tile), lambda i, p: (p[LAST], i)),
                pl.BlockSpec((rows, tile), lambda i, p: (part, i)),
                whole(1, head),
                row_part,
                row_part,
            ],
            out_specs=pl.BlockSpec((rows, tile), lambda i, p: (0, i)),
        ),
        out_shape=jax.ShapeDtypeStruct((rows, width), jnp.bfloat16),
        compiler_params=params(12),
        cost_estimate=cost(1),
        name="queries",
    )(places, *hidden, weights, acc, gain, cosine, sine)


def attention_kernel(slots, n_parts, n_others, stack, places_ref, length_ref, *refs):
    q_parts, refs = refs[:n_parts], refs[n_parts:]
    own_parts, refs = refs[:n_parts], refs[n_parts:]
    others, refs = refs[:n_others], refs[n_others:]
    o_refs, (keys_all, values_all) = refs[:-2], refs[-2:]
    part_rows, width = own_parts[0].shape
    head = width // 2
    picks = others[0].shape[0]
    cross = n_others * picks
    rows = o_refs[0].shape[0]

    start = 0
    for ref in (*others, *own_parts):
        stop = start + ref.shape[0]
        keys_all[start:stop, :] = ref[:, :head]
        values_all[start:stop, :] = ref[:, head:]
        start = stop

    scale = head ** (-0.5) * LOG2E
    own_rows = n_parts * part_rows
    for slot, o_ref in zip(slots, o_refs):
        first = places_ref[slot] * rows
        offset = pl.multiple_of(lax.rem(first, part_rows), rows)
        row = lax.broadcasted_iota(jnp.int32, (rows, own_rows), 0) + first
        column = lax.broadcasted_iota(jnp.int32, (rows, own_rows), 1)
        allowed = jnp.concatenate([column <= row] * stack, axis=0)
        position = lax.broadcasted_iota(jnp.int32, (rows, head), 0) + first
        kept = jnp.concatenate([position < length_ref[0]] * stack, axis=0)
        for left in range(0, o_ref.shape[1], stack * head):
            lanes = [slice(left + i * head, left + (i + 1) * head) for i in range(stack)]
            queries = [q_parts[0][pl.ds(offset, rows), lane] for lane in lanes]
            for part in range(1, n_parts):
                here = first >= part * part_rows
                queries = [
                    jnp.where(here, q_parts[part][pl.ds(offset, rows), lane], query)
                    for lane, query in zip(lanes, queries)
                ]
            scores = lax.dot_general(
                jnp.concatenate(queries, axis=0),
                keys_all[...],
                (((1,), (1,)), ((), ())),
                preferred_element_type=jnp.float32,
            )
            own = jnp.where(allowed, scores[:, cross:], -1e30)
            free = scores[:, :cross]
            largest = jnp.maximum(
                jnp.max(free, axis=1, keepdims=True), jnp.max(own, axis=1, keepdims=True)
            )
            free = jnp.exp2((free - largest) * scale)
            own = jnp.exp2((own - largest) * scale)
            total = jnp.sum(free, axis=1, keepdims=True) + jnp.sum(own, axis=1, keepdims=True)
            mixed = jnp.dot(
                free.astype(jnp.bfloat16), values_all[:cross, :], preferred_element_type=jnp.float32
            ) + jnp.dot(
                own.astype(jnp.bfloat16), values_all[cross:, :], preferred_element_type=jnp.float32
            )
            mixed = jnp.where(kept, mixed / total, 0.0).astype(jnp.bfloat16)
            for index, lane in enumerate(lanes):
                o_ref[:, lane] = mixed[index * rows : (index + 1) * rows, :]


def attention(places, slots, rows, lengths, queries, own, others):
    n_parts = len(own)
    part_rows, width = queries[0].shape
    head = own[0].shape[1] // 2
    picks = others[0].shape[0]
    reach = n_parts * part_rows + len(others) * picks
    return pl.pallas_call(
        functools.partial(attention_kernel, slots, n_parts, len(others), 512 // rows),
        grid_spec=pltpu.PrefetchScalarGridSpec(
            num_scalar_prefetch=2,
            grid=(1,),
            in_specs=[whole(*array.shape) for array in (*queries, *own, *others)],
            out_specs=[whole(rows, width) for _ in slots],
            scratch_shapes=[
                pltpu.VMEM((reach, head), jnp.bfloat16),
                pltpu.VMEM((reach, head), jnp.bfloat16),
            ],
        ),
        out_shape=[jax.ShapeDtypeStruct((rows, width), jnp.bfloat16) for _ in slots],
        compiler_params=params(24 if reach <= 2048 else 56),
        cost_estimate=cost(1),
        name="attention",
    )(places, lengths, *queries, *own, *others)


def mix_kernel(rows_ref, w_ref, out_ref):
    total = jnp.dot(rows_ref[...], w_ref[...], preferred_element_type=jnp.float32)
    out_ref[...] = total.astype(out_ref.dtype)


def mix(attended, w_out, which):
    rows, depth = attended.shape
    width = w_out.shape[1] // 2
    tiles = 5
    tile = width // tiles
    return pl.pallas_call(
        mix_kernel,
        grid=(tiles,),
        in_specs=[
            whole(rows, depth),
            pl.BlockSpec((depth, tile), lambda i: (0, i + which * tiles)),
        ],
        out_specs=pl.BlockSpec((rows, tile), lambda i: (0, i)),
        out_shape=jax.ShapeDtypeStruct((rows, width), jnp.bfloat16),
        compiler_params=params(8),
        cost_estimate=cost(1),
        name="mix",
    )(attended, w_out)


def eighth_kernel(places_ref, w_ref, out_ref):
    out_ref[...] = w_ref[...]


def eighth(places, which, w_out, share):
    width = w_out.shape[1] // 2
    return pl.pallas_call(
        eighth_kernel,
        grid_spec=pltpu.PrefetchScalarGridSpec(
            num_scalar_prefetch=1,
            grid=(1,),
            in_specs=[pl.BlockSpec((share, width), lambda i, p: (p[EIGHTHS + which], 1))],
            out_specs=whole(share, width),
        ),
        out_shape=jax.ShapeDtypeStruct((share, width), w_out.dtype),
        compiler_params=params(8),
        cost_estimate=cost(1),
        name="eighth",
    )(places, w_out)


def mix_sent_kernel(places_ref, rows_ref, *refs):
    pieces, out_ref = refs[:-1], refs[-1]
    share = rows_ref.shape[1] // len(OFFSETS)
    rows = []
    for index in range(len(OFFSETS)):
        start = pl.multiple_of(places_ref[EIGHTHS + index] * share, share)
        rows.append(rows_ref[:, pl.ds(start, share)])
    total = jnp.dot(
        jnp.concatenate(rows, axis=1),
        jnp.concatenate([piece[...] for piece in pieces], axis=0),
        preferred_element_type=jnp.float32,
    )
    out_ref[...] = total.astype(out_ref.dtype)


def mix_sent(places, attended, pieces):
    rows, depth = attended.shape
    width = pieces[0].shape[1]
    tile = width // 5
    column = lambda height: pl.BlockSpec((height, tile), lambda i, p: (0, i))
    return pl.pallas_call(
        mix_sent_kernel,
        grid_spec=pltpu.PrefetchScalarGridSpec(
            num_scalar_prefetch=1,
            grid=(width // tile,),
            in_specs=[whole(rows, depth)] + [column(piece.shape[0]) for piece in pieces],
            out_specs=column(rows),
        ),
        out_shape=jax.ShapeDtypeStruct((rows, width), jnp.bfloat16),
        compiler_params=params(8),
        cost_estimate=cost(1),
        name="mix_sent",
    )(places, attended, *pieces)


def halves_kernel(ref, first_ref, second_ref):
    half = first_ref.shape[0]
    first_ref[...] = ref[:half, :]
    second_ref[...] = ref[half:, :]


def halves(array):
    rows, width = array.shape
    half = jax.ShapeDtypeStruct((rows // 2, width), array.dtype)
    return pl.pallas_call(
        halves_kernel,
        grid=(1,),
        in_specs=[whole(rows, width)],
        out_specs=[whole(rows // 2, width)] * 2,
        out_shape=[half, half],
        compiler_params=params(8),
        cost_estimate=cost(1),
        name="halves",
    )(array)


def add_kernel(count, *refs):
    total = refs[0][...].astype(jnp.float32)
    for ref in refs[1:count]:
        total = total + ref[...].astype(jnp.float32)
    refs[-1][...] = total.astype(jnp.bfloat16)


def added(*arrays, half=None, into=None):
    rows, width = arrays[0].shape
    wide = 1 if half is None else 2
    at = half or 0
    operands = list(arrays)
    in_specs = [whole(rows, width) for _ in arrays]
    aliases = {}
    if into is not None:
        operands.append(into)
        in_specs.append(pl.BlockSpec(memory_space=pl.ANY))
        aliases = {len(arrays): 0}
    return pl.pallas_call(
        functools.partial(add_kernel, len(arrays)),
        grid=(1,),
        in_specs=in_specs,
        out_specs=pl.BlockSpec((rows, width), lambda i: (0, at)),
        out_shape=jax.ShapeDtypeStruct((rows, wide * width), jnp.bfloat16),
        input_output_aliases=aliases,
        compiler_params=params(8),
        cost_estimate=cost(1),
        name="added",
    )(*operands)


def shards(hidden_in, lengths, summary_pos, w_query, w_key, w_value, w_out, q_gain, k_gain):
    rows_here = hidden_in.shape[0]
    head_width = q_gain.shape[0]
    place = lax.axis_index("tensor")
    n_cand = lax.axis_size("cand")
    assert lax.axis_size("tensor") == 4 and w_key.shape[1] == head_width

    def swap(array):
        return lax.ppermute(array, "tensor", [(0, 1), (1, 0), (2, 3), (3, 2)])

    def across(array):
        return lax.ppermute(array, "tensor", [(1, 2), (2, 1)])

    def outward(array):
        return lax.ppermute(array, "tensor", [(1, 0), (2, 3)])

    def inward(array):
        return lax.ppermute(array, "tensor", [(0, 1), (3, 2)])

    def between(array, offset):
        return lax.ppermute(array, "cand", [(i, i ^ offset) for i in range(n_cand)])

    low = place < 2
    near = jnp.bitwise_xor(place, 1)
    places = [place, near, jnp.where(low, 2, 1), jnp.where(low, 3, 0)]
    places += [jnp.bitwise_xor(lax.axis_index("cand"), offset) for offset in OFFSETS]
    places = jnp.stack(places).astype(jnp.int32)
    share = w_out.shape[0] // n_cand
    spread = n_cand == len(OFFSETS) and share % 128 == 0
    tables = rope_tables(rows_here, head_width)
    k_gain, q_gain = k_gain[None], q_gain[None]
    weights = [w_query, w_key, w_value]
    half = rows_here // 2

    from_near = swap(hidden_in)
    from_mid = [across(array) for array in halves(hidden_in)]
    accs = partial_projection(places, OWN, [[hidden_in]], weights, None)
    from_mid[0], accs = lax.optimization_barrier((from_mid[0], accs))
    to_outer = [outward(from_mid[0])]
    accs = partial_projection(after(places, from_mid[1]), NEAR, [[from_near]], weights, accs)
    from_near = halves(from_near)
    to_outer.append(outward(after(from_mid[1], from_near)))
    to_inner = [across(from_near[0])]
    to_inner.append(across(after(from_near[1], (to_outer[0], accs))))
    end = [outward(array) for array in to_inner]
    pieces = {}
    if spread:
        first, second = (eighth(places, i, w_out, share) for i in (0, 1))
        pieces[0] = inward(after(first, to_outer[0]))
        cue = to_outer[1]
        pieces[6] = inward(after(second, cue))
        first = after(pieces[0], cue)
        pieces[2], pieces[4] = between(first, 2), between(first, 4)
    cue = (to_inner, accs)
    accs = partial_projection(
        after(places, cue), THIRD, [[a, b] for a, b in zip(from_mid, to_outer)], weights, accs
    )

    final = [[a, b] for a, b in zip(to_inner, end)]
    (own_first,) = keys_values(places, final[0], 0, weights[1:], accs[1:], k_gain, *tables)
    first_queries = queries_of(places, final[0], 0, w_query, accs[0], q_gain, *tables)
    own_second, summary = keys_values(
        places,
        final[1],
        1,
        weights[1:],
        after(accs[1:], (first_queries, pieces)),
        k_gain,
        *tables,
        [own_first],
        summary_pos,
    )
    own = [own_first, own_second]
    others = [between(summary, offset) for offset in range(1, n_cand)]
    second_queries = queries_of(places, final[1], 1, w_query, accs[0], q_gain, *tables)
    queries = [first_queries, second_queries]

    if spread:
        cue = (others, second_queries)
        for offset in (0, 6, 2, 4):
            pieces[offset ^ 1] = between(after(pieces[offset], cue), 1)

    def attend(slots):
        return attention(places, slots, rows_here // 4, lengths, queries, own, others)

    def send(rows, part):
        return inward(rows if spread else part)

    def share_of(arrived):
        if not spread:
            return arrived
        return mix_sent(places, arrived, [pieces[offset] for offset in OFFSETS])

    def mixed(rows):
        return [mix(rows, w_out, which) for which in (0, 1)]

    (far_rows,) = attend((LAST,))
    far = mixed(far_rows)
    far_sent = send(far_rows, far[1])
    places = after(places, far)
    (third_rows,) = attend((THIRD,))
    far_sent = after(far_sent, third_rows)
    far_in = inward(after(far[0], far_sent))
    far_right = added(far[1], share_of(far_sent))
    places = after(places, far_right)
    near_rows, own_rows = attend((NEAR, OWN))
    third = mixed(after(third_rows, near_rows))
    third_sent = send(third_rows, third[1])
    far_right = across(far_right)
    far_left = added(far[0], after(far_in, third))
    third_sent = after(third_sent, far_left)
    far_left = across(far_left)
    third_in = inward(after(third[0], third_sent))
    third_right = added(third[1], share_of(third_sent))
    near = mixed(after(near_rows, (third_right, far_right)))
    near_sent = send(near_rows, near[1])
    third_right = across(third_right)
    out_right = added(near[1], after(far_right, near))
    kept = mixed(after(own_rows, (out_right, far_left)))
    out_left = added(near[0], after(far_left, kept))
    third_left = added(third[0], after(third_in, out_left))
    near_sent = share_of(after(near_sent, third_left))
    result = added(kept[1], near_sent, outward(out_right), third_right, half=1)
    near_in = inward(after(near[0], third_left))
    out_left, third_left = outward(out_left), across(third_left)
    return added(kept[0], near_in, out_left, third_left, half=0, into=result)


def solution(mesh):
    return jax.shard_map(
        shards,
        mesh=mesh,
        in_specs=(
            P("cand", "tensor"),
            P("cand"),
            P("cand", None),
            P(None, "tensor"),
            P(None, "tensor"),
            P(None, "tensor"),
            P("tensor", None),
            P(),
            P(),
        ),
        out_specs=P(("cand", "tensor"), None),
        check_vma=False,
    )
```

```python
import functools

import jax
import jax.numpy as jnp
import numpy as np
from jax import lax
from jax.experimental import pallas as pl
from jax.experimental.pallas import tpu as pltpu
from jax.sharding import PartitionSpec as P

MIB = 1024 * 1024
LOG2E = 1.4426950408889634
OWN, NEAR, THIRD, LAST, EIGHTHS = range(5)
OFFSETS = (0, 6, 2, 4, 1, 7, 3, 5)


def rope_tables(rows, width):
    half_width = width // 2
    frequency = (1000000.0 ** (-(np.arange(half_width) * 2.0 / width))).astype(np.float32)
    angle = np.arange(rows, dtype=np.float32)[:, None] * frequency[None, :]
    angle = angle.astype(np.float64)
    cosine, sine = np.cos(angle), np.sin(angle)
    return (
        jnp.asarray(np.concatenate([cosine, cosine], axis=1).astype(np.float32)),
        jnp.asarray(np.concatenate([-sine, sine], axis=1).astype(np.float32)),
    )


def norm_rope(vectors, gain, cosine, sine):
    scale = lax.rsqrt(jnp.mean(vectors * vectors, axis=-1, keepdims=True) + 1e-06)
    vectors = vectors * scale * gain
    return vectors * cosine + pltpu.roll(vectors, vectors.shape[-1] // 2, 1) * sine


def params(mebibytes):
    return pltpu.CompilerParams(vmem_limit_bytes=mebibytes * MIB)


def cost(flops):
    return pl.CostEstimate(flops=flops, bytes_accessed=1, transcendentals=0)


def after(array, cue):
    return lax.optimization_barrier((array, cue))[0]


def whole(*shape):
    return pl.BlockSpec(shape, lambda *_: (0,) * len(shape))


def resident(count):
    return [pl.BlockSpec(memory_space=pltpu.VMEM)] * count


def summed(refs):
    total = refs[0][...]
    for ref in refs[1:]:
        total = total + ref[...]
    return total


def partial_kernel(counts, with_acc, places_ref, *refs):
    rows = []
    for count in counts:
        rows.append(summed(refs[:count]))
        refs = refs[count:]
    hidden = jnp.concatenate(rows, axis=0) if len(rows) > 1 else rows[0]
    weights, outs = refs[:3], refs[-3:]
    accs = refs[3:6] if with_acc else (None,) * 3
    step = pl.program_id(0)

    def add(w_ref, acc_ref, out_ref):
        product = jnp.dot(hidden, w_ref[...], preferred_element_type=jnp.float32)
        out_ref[...] = product if acc_ref is None else product + acc_ref[...]

    add(weights[0], accs[0], outs[0])

    @pl.when(step == 0)
    def _():
        add(weights[1], accs[1], outs[1])
        add(weights[2], accs[2], outs[2])


def partial_projection(places, slot, parts, weights, accs):
    features = parts[0][0].shape[1]
    rows = sum(part[0].shape[0] for part in parts)
    arrivals = [array for part in parts for array in part]
    widths = [weight.shape[1] for weight in weights]
    tile = 512
    column = lambda height: pl.BlockSpec((height, tile), lambda i, p: (0, i))
    per_array = lambda height: [column(height), whole(height, widths[1]), whole(height, widths[2])]
    block = lambda width: pl.BlockSpec((features, width), lambda i, p: (p[slot], 0))
    in_specs = [whole(*array.shape) for array in arrivals]
    in_specs.append(pl.BlockSpec((features, tile), lambda i, p: (p[slot], i)))
    in_specs += [block(widths[1]), block(widths[2])]
    operands = [*arrivals, *weights]
    if accs is not None:
        in_specs += per_array(rows)
        operands += accs
    return pl.pallas_call(
        functools.partial(partial_kernel, [len(part) for part in parts], accs is not None),
        grid_spec=pltpu.PrefetchScalarGridSpec(
            num_scalar_prefetch=1,
            grid=(widths[0] // tile,),
            in_specs=in_specs,
            out_specs=per_array(rows),
        ),
        out_shape=[jax.ShapeDtypeStruct((rows, width), jnp.float32) for width in widths],
        compiler_params=params(20),
        cost_estimate=cost(1),
        name="partial_projection",
    )(places, *operands)


def keys_values_kernel(count, n_before, places_ref, *refs):
    before, refs = refs[:n_before], refs[n_before:]
    hidden = summed(refs[:count])
    wk_ref, wv_ref, acck_ref, accv_ref, gain_ref, cos_ref, sin_ref = refs[count : count + 7]
    refs = refs[count + 7 :]
    head = gain_ref.shape[1]
    out_ref = refs[0] if n_before == 0 else refs[1]
    keys = acck_ref[...] + jnp.dot(hidden, wk_ref[...], preferred_element_type=jnp.float32)
    values = accv_ref[...] + jnp.dot(hidden, wv_ref[...], preferred_element_type=jnp.float32)
    keys = norm_rope(keys, gain_ref[...], cos_ref[...], sin_ref[...])
    out_ref[:, :head] = keys.astype(jnp.bfloat16)
    out_ref[:, head:] = values.astype(jnp.bfloat16)
    if n_before:
        pos_ref, summary_ref = refs[0], refs[2]
        picks = pos_ref.shape[1]
        picked, start = None, 0
        for ref in (*before, out_ref):
            rows = ref.shape[0]
            row = lax.broadcasted_iota(jnp.int32, (rows, picks), 0) + start
            chosen = jnp.where(row == pos_ref[...], 1.0, 0.0).astype(jnp.bfloat16)
            found = lax.dot_general(
                chosen, ref[...], (((0,), (0,)), ((), ())), preferred_element_type=jnp.float32
            )
            picked = found if picked is None else picked + found
            start += rows
        summary_ref[...] = picked.astype(jnp.bfloat16)


def keys_values(places, hidden, part, weights, accs, gain, cosine, sine, before=(), positions=None):
    rows, features = hidden[0].shape
    head = gain.shape[1]
    row_part = pl.BlockSpec((rows, head), lambda i, p: (part, 0))
    block = pl.BlockSpec((features, head), lambda i, p: (p[LAST], 0))
    in_specs = [whole(*array.shape) for array in (*before, *hidden)]
    in_specs += [block, block, row_part, row_part, whole(1, head), row_part, row_part]
    operands = [*before, *hidden, *weights, *accs, gain, cosine, sine]
    out_shape = [jax.ShapeDtypeStruct((rows, 2 * head), jnp.bfloat16)]
    if before:
        in_specs.append(whole(*positions.shape))
        operands.append(positions)
        out_shape.append(jax.ShapeDtypeStruct((positions.shape[1], 2 * head), jnp.bfloat16))
    return pl.pallas_call(
        functools.partial(keys_values_kernel, len(hidden), len(before)),
        grid_spec=pltpu.PrefetchScalarGridSpec(
            num_scalar_prefetch=1,
            grid=(1,),
            in_specs=in_specs,
            out_specs=[whole(*shape.shape) for shape in out_shape],
        ),
        out_shape=out_shape,
        compiler_params=params(12),
        cost_estimate=cost(1),
        name="keys_values",
    )(places, *operands)


def queries_kernel(count, places_ref, *refs):
    hidden = summed(refs[:count])
    w_ref, acc_ref, gain_ref, cos_ref, sin_ref, q_ref = refs[count:]
    head = gain_ref.shape[1]
    proj = acc_ref[...] + jnp.dot(hidden, w_ref[...], preferred_element_type=jnp.float32)
    for start in range(0, proj.shape[1], head):
        one = norm_rope(proj[:, start : start + head], gain_ref[...], cos_ref[...], sin_ref[...])
        q_ref[:, start : start + head] = one.astype(jnp.bfloat16)


def queries_of(places, hidden, part, weights, acc, gain, cosine, sine):
    rows, features = hidden[0].shape
    head = gain.shape[1]
    width = weights.shape[1]
    tile = 4 * head
    row_part = pl.BlockSpec((rows, head), lambda i, p: (part, 0))
    return pl.pallas_call(
        functools.partial(queries_kernel, len(hidden)),
        grid_spec=pltpu.PrefetchScalarGridSpec(
            num_scalar_prefetch=1,
            grid=(width // tile,),
            in_specs=[whole(rows, features) for _ in hidden]
            + [
                pl.BlockSpec((features, tile), lambda i, p: (p[LAST], i)),
                pl.BlockSpec((rows, tile), lambda i, p: (part, i)),
                whole(1, head),
                row_part,
                row_part,
            ],
            out_specs=pl.BlockSpec((rows, tile), lambda i, p: (0, i)),
        ),
        out_shape=jax.ShapeDtypeStruct((rows, width), jnp.bfloat16),
        compiler_params=params(12),
        cost_estimate=cost(1),
        name="queries",
    )(places, *hidden, weights, acc, gain, cosine, sine)


def attention_kernel(slots, n_parts, n_others, stack, places_ref, length_ref, *refs):
    q_parts, refs = refs[:n_parts], refs[n_parts:]
    own_parts, refs = refs[:n_parts], refs[n_parts:]
    others, refs = refs[:n_others], refs[n_others:]
    o_refs, (keys_all, values_all) = refs[:-2], refs[-2:]
    part_rows, width = own_parts[0].shape
    head = width // 2
    picks = others[0].shape[0]
    cross = n_others * picks
    rows = o_refs[0].shape[0]

    start = 0
    for ref in (*others, *own_parts):
        stop = start + ref.shape[0]
        keys_all[start:stop, :] = ref[:, :head]
        values_all[start:stop, :] = ref[:, head:]
        start = stop

    scale = head ** (-0.5) * LOG2E
    own_rows = n_parts * part_rows
    for slot, o_ref in zip(slots, o_refs):
        first = places_ref[slot] * rows
        offset = pl.multiple_of(lax.rem(first, part_rows), rows)
        row = lax.broadcasted_iota(jnp.int32, (rows, own_rows), 0) + first
        column = lax.broadcasted_iota(jnp.int32, (rows, own_rows), 1)
        allowed = jnp.concatenate([column <= row] * stack, axis=0)
        position = lax.broadcasted_iota(jnp.int32, (rows, head), 0) + first
        kept = jnp.concatenate([position < length_ref[0]] * stack, axis=0)
        for left in range(0, o_ref.shape[1], stack * head):
            lanes = [slice(left + i * head, left + (i + 1) * head) for i in range(stack)]
            queries = [q_parts[0][pl.ds(offset, rows), lane] for lane in lanes]
            for part in range(1, n_parts):
                here = first >= part * part_rows
                queries = [
                    jnp.where(here, q_parts[part][pl.ds(offset, rows), lane], query)
                    for lane, query in zip(lanes, queries)
                ]
            scores = lax.dot_general(
                jnp.concatenate(queries, axis=0),
                keys_all[...],
                (((1,), (1,)), ((), ())),
                preferred_element_type=jnp.float32,
            )
            own = jnp.where(allowed, scores[:, cross:], -1e30)
            free = scores[:, :cross]
            largest = jnp.maximum(
                jnp.max(free, axis=1, keepdims=True), jnp.max(own, axis=1, keepdims=True)
            )
            free = jnp.exp2((free - largest) * scale)
            own = jnp.exp2((own - largest) * scale)
            total = jnp.sum(free, axis=1, keepdims=True) + jnp.sum(own, axis=1, keepdims=True)
            mixed = jnp.dot(
                free.astype(jnp.bfloat16), values_all[:cross, :], preferred_element_type=jnp.float32
            ) + jnp.dot(
                own.astype(jnp.bfloat16), values_all[cross:, :], preferred_element_type=jnp.float32
            )
            mixed = jnp.where(kept, mixed / total, 0.0).astype(jnp.bfloat16)
            for index, lane in enumerate(lanes):
                o_ref[:, lane] = mixed[index * rows : (index + 1) * rows, :]


def attention(places, slots, rows, lengths, queries, own, others):
    n_parts = len(own)
    part_rows, width = queries[0].shape
    head = own[0].shape[1] // 2
    picks = others[0].shape[0]
    reach = n_parts * part_rows + len(others) * picks
    return pl.pallas_call(
        functools.partial(attention_kernel, slots, n_parts, len(others), 512 // rows),
        grid_spec=pltpu.PrefetchScalarGridSpec(
            num_scalar_prefetch=2,
            grid=(1,),
            in_specs=resident(len(queries) + len(own) + len(others)),
            out_specs=resident(len(slots)),
            scratch_shapes=[
                pltpu.VMEM((reach, head), jnp.bfloat16),
                pltpu.VMEM((reach, head), jnp.bfloat16),
            ],
        ),
        out_shape=[jax.ShapeDtypeStruct((rows, width), jnp.bfloat16) for _ in slots],
        compiler_params=params(24 if reach <= 2048 else 56),
        cost_estimate=cost(1),
        name="attention",
    )(places, lengths, *queries, *own, *others)


def mix_kernel(which, tiles, rows_ref, w_ref, out_ref):
    width = out_ref.shape[1]
    tile = width // tiles
    for start in range(0, width, tile):
        left = which * width + start
        total = jnp.dot(
            rows_ref[...], w_ref[:, left : left + tile], preferred_element_type=jnp.float32
        )
        out_ref[:, start : start + tile] = total.astype(out_ref.dtype)


def mix(attended, w_out, which):
    rows = attended.shape[0]
    width = w_out.shape[1] // 2
    return pl.pallas_call(
        functools.partial(mix_kernel, which, 5),
        in_specs=resident(2),
        out_specs=resident(1)[0],
        out_shape=jax.ShapeDtypeStruct((rows, width), jnp.bfloat16),
        compiler_params=params(8),
        cost_estimate=cost(1),
        name="mix",
    )(attended, w_out)


def eighth_kernel(places_ref, w_ref, out_ref):
    out_ref[...] = w_ref[...]


def eighth(places, which, w_out, share):
    width = w_out.shape[1] // 2
    return pl.pallas_call(
        eighth_kernel,
        grid_spec=pltpu.PrefetchScalarGridSpec(
            num_scalar_prefetch=1,
            grid=(1,),
            in_specs=[pl.BlockSpec((share, width), lambda i, p: (p[EIGHTHS + which], 1))],
            out_specs=whole(share, width),
        ),
        out_shape=jax.ShapeDtypeStruct((share, width), w_out.dtype),
        compiler_params=params(8),
        cost_estimate=cost(1),
        name="eighth",
    )(places, w_out)


def mix_sent_kernel(tiles, places_ref, rows_ref, *refs):
    pieces, out_ref = refs[:-1], refs[-1]
    share = rows_ref.shape[1] // len(OFFSETS)
    rows = []
    for index in range(len(OFFSETS)):
        start = pl.multiple_of(places_ref[EIGHTHS + index] * share, share)
        rows.append(rows_ref[:, pl.ds(start, share)])
    rows = jnp.concatenate(rows, axis=1)
    tile = out_ref.shape[1] // tiles
    for start in range(0, out_ref.shape[1], tile):
        columns = slice(start, start + tile)
        weights = jnp.concatenate([piece[:, columns] for piece in pieces], axis=0)
        total = jnp.dot(rows, weights, preferred_element_type=jnp.float32)
        out_ref[:, columns] = total.astype(out_ref.dtype)


def mix_sent(places, attended, pieces):
    rows = attended.shape[0]
    width = pieces[0].shape[1]
    return pl.pallas_call(
        functools.partial(mix_sent_kernel, 5),
        grid_spec=pltpu.PrefetchScalarGridSpec(
            num_scalar_prefetch=1,
            grid=(1,),
            in_specs=resident(1 + len(pieces)),
            out_specs=resident(1)[0],
        ),
        out_shape=jax.ShapeDtypeStruct((rows, width), jnp.bfloat16),
        compiler_params=params(12),
        cost_estimate=cost(1),
        name="mix_sent",
    )(places, attended, *pieces)


def halves_kernel(ref, first_ref, second_ref):
    half = first_ref.shape[0]
    first_ref[...] = ref[:half, :]
    second_ref[...] = ref[half:, :]


def halves(array):
    rows, width = array.shape
    half = jax.ShapeDtypeStruct((rows // 2, width), array.dtype)
    return pl.pallas_call(
        halves_kernel,
        grid=(1,),
        in_specs=[whole(rows, width)],
        out_specs=[whole(rows // 2, width)] * 2,
        out_shape=[half, half],
        compiler_params=params(8),
        cost_estimate=cost(1),
        name="halves",
    )(array)


def add_kernel(count, *refs):
    total = refs[0][...].astype(jnp.float32)
    for ref in refs[1:count]:
        total = total + ref[...].astype(jnp.float32)
    refs[-1][...] = total.astype(jnp.bfloat16)


def added(*arrays, half=None, into=None):
    rows, width = arrays[0].shape
    wide = 1 if half is None else 2
    at = half or 0
    operands = list(arrays)
    in_specs = resident(len(arrays))
    aliases = {}
    if into is not None:
        operands.append(into)
        in_specs.append(pl.BlockSpec(memory_space=pl.ANY))
        aliases = {len(arrays): 0}
    return pl.pallas_call(
        functools.partial(add_kernel, len(arrays)),
        grid=(1,),
        in_specs=in_specs,
        out_specs=pl.BlockSpec((rows, width), lambda i: (0, at)),
        out_shape=jax.ShapeDtypeStruct((rows, wide * width), jnp.bfloat16),
        input_output_aliases=aliases,
        compiler_params=params(8),
        cost_estimate=cost(1),
        name="added",
    )(*operands)


def shards(hidden_in, lengths, summary_pos, w_query, w_key, w_value, w_out, q_gain, k_gain):
    rows_here = hidden_in.shape[0]
    head_width = q_gain.shape[0]
    place = lax.axis_index("tensor")
    n_cand = lax.axis_size("cand")
    assert lax.axis_size("tensor") == 4 and w_key.shape[1] == head_width

    def swap(array):
        return lax.ppermute(array, "tensor", [(0, 1), (1, 0), (2, 3), (3, 2)])

    def across(array):
        return lax.ppermute(array, "tensor", [(1, 2), (2, 1)])

    def outward(array):
        return lax.ppermute(array, "tensor", [(1, 0), (2, 3)])

    def inward(array):
        return lax.ppermute(array, "tensor", [(0, 1), (3, 2)])

    def between(array, offset):
        return lax.ppermute(array, "cand", [(i, i ^ offset) for i in range(n_cand)])

    low = place < 2
    near = jnp.bitwise_xor(place, 1)
    places = [place, near, jnp.where(low, 2, 1), jnp.where(low, 3, 0)]
    places += [jnp.bitwise_xor(lax.axis_index("cand"), offset) for offset in OFFSETS]
    places = jnp.stack(places).astype(jnp.int32)
    share = w_out.shape[0] // n_cand
    spread = n_cand == len(OFFSETS) and share % 128 == 0
    tables = rope_tables(rows_here, head_width)
    k_gain, q_gain = k_gain[None], q_gain[None]
    weights = [w_query, w_key, w_value]
    half = rows_here // 2

    from_near = swap(hidden_in)
    from_mid = [across(array) for array in halves(hidden_in)]
    accs = partial_projection(places, OWN, [[hidden_in]], weights, None)
    from_mid[0], accs = lax.optimization_barrier((from_mid[0], accs))
    to_outer = [outward(from_mid[0])]
    accs = partial_projection(after(places, from_mid[1]), NEAR, [[from_near]], weights, accs)
    from_near = halves(from_near)
    to_outer.append(outward(after(from_mid[1], from_near)))
    to_inner = [across(from_near[0])]
    to_inner.append(across(after(from_near[1], (to_outer[0], accs))))
    end = [outward(array) for array in to_inner]
    pieces = {}
    if spread:
        first, second = (eighth(places, i, w_out, share) for i in (0, 1))
        pieces[0] = inward(after(first, to_outer[0]))
        cue = to_outer[1]
        pieces[6] = inward(after(second, cue))
        first = after(pieces[0], cue)
        pieces[2], pieces[4] = between(first, 2), between(first, 4)
    cue = (to_inner, accs)
    accs = partial_projection(
        after(places, cue), THIRD, [[a, b] for a, b in zip(from_mid, to_outer)], weights, accs
    )

    final = [[a, b] for a, b in zip(to_inner, end)]
    (own_first,) = keys_values(places, final[0], 0, weights[1:], accs[1:], k_gain, *tables)
    first_queries = queries_of(places, final[0], 0, w_query, accs[0], q_gain, *tables)
    own_second, summary = keys_values(
        places,
        final[1],
        1,
        weights[1:],
        after(accs[1:], (first_queries, pieces)),
        k_gain,
        *tables,
        [own_first],
        summary_pos,
    )
    own = [own_first, own_second]
    others = [between(summary, offset) for offset in range(1, n_cand)]
    second_queries = queries_of(places, final[1], 1, w_query, accs[0], q_gain, *tables)
    queries = [first_queries, second_queries]

    if spread:
        cue = (others, second_queries)
        for offset in (0, 6, 2, 4):
            pieces[offset ^ 1] = between(after(pieces[offset], cue), 1)

    def attend(slots):
        return attention(places, slots, rows_here // 4, lengths, queries, own, others)

    def send(rows, part):
        return inward(rows if spread else part)

    def share_of(arrived):
        if not spread:
            return arrived
        return mix_sent(places, arrived, [pieces[offset] for offset in OFFSETS])

    def mixed(rows):
        return [mix(rows, w_out, which) for which in (0, 1)]

    (far_rows,) = attend((LAST,))
    far = mixed(far_rows)
    far_sent = send(far_rows, far[1])
    places = after(places, far)
    (third_rows,) = attend((THIRD,))
    far_sent = after(far_sent, third_rows)
    far_in = inward(after(far[0], far_sent))
    far_right = added(far[1], share_of(far_sent))
    places = after(places, far_right)
    near_rows, own_rows = attend((NEAR, OWN))
    third = mixed(after(third_rows, near_rows))
    third_sent = send(third_rows, third[1])
    far_right = across(far_right)
    far_left = added(far[0], after(far_in, third))
    third_sent = after(third_sent, far_left)
    far_left = across(far_left)
    third_in = inward(after(third[0], third_sent))
    third_right = added(third[1], share_of(third_sent))
    near = [None, mix(after(near_rows, (third_right, far_right)), w_out, 1)]
    near_sent = send(near_rows, near[1])
    third_right = across(third_right)
    out_right = added(near[1], far_right)
    near[0] = mix(after(near_rows, out_right), w_out, 0)
    out_left = added(near[0], far_left)
    third_left = added(third[0], after(third_in, out_left))
    kept = mixed(after(own_rows, third_left))
    near_sent = share_of(after(near_sent, third_left))
    result = added(kept[1], near_sent, outward(out_right), third_right, half=1)
    near_in = inward(after(near[0], third_left))
    out_left, third_left = outward(out_left), across(third_left)
    return added(kept[0], near_in, out_left, third_left, half=0, into=result)


def solution(mesh):
    return jax.shard_map(
        shards,
        mesh=mesh,
        in_specs=(
            P("cand", "tensor"),
            P("cand"),
            P("cand", None),
            P(None, "tensor"),
            P(None, "tensor"),
            P(None, "tensor"),
            P("tensor", None),
            P(),
            P(),
        ),
        out_specs=P(("cand", "tensor"), None),
        check_vma=False,
    )
```

```python
import functools

import jax
import jax.numpy as jnp
import numpy as np
from jax import lax
from jax.experimental import pallas as pl
from jax.experimental.pallas import tpu as pltpu
from jax.sharding import PartitionSpec as P

MIB = 1024 * 1024
LOG2E = 1.4426950408889634
OWN, NEAR, THIRD, LAST, EIGHTHS = range(5)
OFFSETS = (0, 6, 2, 4, 1, 7, 3, 5)


def rope_tables(rows, width):
    half_width = width // 2
    frequency = (1000000.0 ** (-(np.arange(half_width) * 2.0 / width))).astype(np.float32)
    angle = np.arange(rows, dtype=np.float32)[:, None] * frequency[None, :]
    angle = angle.astype(np.float64)
    cosine, sine = np.cos(angle), np.sin(angle)
    return (
        jnp.asarray(np.concatenate([cosine, cosine], axis=1).astype(np.float32)),
        jnp.asarray(np.concatenate([-sine, sine], axis=1).astype(np.float32)),
    )


def norm_rope(vectors, gain, cosine, sine):
    scale = lax.rsqrt(jnp.mean(vectors * vectors, axis=-1, keepdims=True) + 1e-06)
    vectors = vectors * scale * gain
    return vectors * cosine + pltpu.roll(vectors, vectors.shape[-1] // 2, 1) * sine


def params(mebibytes):
    return pltpu.CompilerParams(vmem_limit_bytes=mebibytes * MIB)


def cost(flops):
    return pl.CostEstimate(flops=flops, bytes_accessed=1, transcendentals=0)


def after(array, cue):
    return lax.optimization_barrier((array, cue))[0]


def whole(*shape):
    return pl.BlockSpec(shape, lambda *_: (0,) * len(shape))


def resident(count):
    return [pl.BlockSpec(memory_space=pltpu.VMEM)] * count


def summed(refs):
    total = refs[0][...]
    for ref in refs[1:]:
        total = total + ref[...]
    return total


def partial_kernel(counts, with_acc, places_ref, *refs):
    rows = []
    for count in counts:
        rows.append(summed(refs[:count]))
        refs = refs[count:]
    hidden = jnp.concatenate(rows, axis=0) if len(rows) > 1 else rows[0]
    weights, outs = refs[:3], refs[-3:]
    accs = refs[3:6] if with_acc else (None,) * 3
    step = pl.program_id(0)

    def add(w_ref, acc_ref, out_ref):
        product = jnp.dot(hidden, w_ref[...], preferred_element_type=jnp.float32)
        out_ref[...] = product if acc_ref is None else product + acc_ref[...]

    add(weights[0], accs[0], outs[0])

    @pl.when(step == 0)
    def _():
        add(weights[1], accs[1], outs[1])
        add(weights[2], accs[2], outs[2])


def partial_projection(places, slot, parts, weights, accs):
    features = parts[0][0].shape[1]
    rows = sum(part[0].shape[0] for part in parts)
    arrivals = [array for part in parts for array in part]
    widths = [weight.shape[1] for weight in weights]
    tile = 512
    column = lambda height: pl.BlockSpec((height, tile), lambda i, p: (0, i))
    per_array = lambda height: [column(height), whole(height, widths[1]), whole(height, widths[2])]
    block = lambda width: pl.BlockSpec((features, width), lambda i, p: (p[slot], 0))
    in_specs = [whole(*array.shape) for array in arrivals]
    in_specs.append(pl.BlockSpec((features, tile), lambda i, p: (p[slot], i)))
    in_specs += [block(widths[1]), block(widths[2])]
    operands = [*arrivals, *weights]
    if accs is not None:
        in_specs += per_array(rows)
        operands += accs
    return pl.pallas_call(
        functools.partial(partial_kernel, [len(part) for part in parts], accs is not None),
        grid_spec=pltpu.PrefetchScalarGridSpec(
            num_scalar_prefetch=1,
            grid=(widths[0] // tile,),
            in_specs=in_specs,
            out_specs=per_array(rows),
        ),
        out_shape=[jax.ShapeDtypeStruct((rows, width), jnp.float32) for width in widths],
        compiler_params=params(20),
        cost_estimate=cost(1),
        name="partial_projection",
    )(places, *operands)


def keys_values_kernel(count, n_before, places_ref, *refs):
    before, refs = refs[:n_before], refs[n_before:]
    hidden = summed(refs[:count])
    wk_ref, wv_ref, acck_ref, accv_ref, gain_ref, cos_ref, sin_ref = refs[count : count + 7]
    refs = refs[count + 7 :]
    head = gain_ref.shape[1]
    out_ref = refs[0] if n_before == 0 else refs[1]
    keys = acck_ref[...] + jnp.dot(hidden, wk_ref[...], preferred_element_type=jnp.float32)
    values = accv_ref[...] + jnp.dot(hidden, wv_ref[...], preferred_element_type=jnp.float32)
    keys = norm_rope(keys, gain_ref[...], cos_ref[...], sin_ref[...])
    out_ref[:, :head] = keys.astype(jnp.bfloat16)
    out_ref[:, head:] = values.astype(jnp.bfloat16)
    if n_before:
        pos_ref, summary_ref = refs[0], refs[2]
        picks = pos_ref.shape[1]
        picked, start = None, 0
        for ref in (*before, out_ref):
            rows = ref.shape[0]
            row = lax.broadcasted_iota(jnp.int32, (rows, picks), 0) + start
            chosen = jnp.where(row == pos_ref[...], 1.0, 0.0).astype(jnp.bfloat16)
            found = lax.dot_general(
                chosen, ref[...], (((0,), (0,)), ((), ())), preferred_element_type=jnp.float32
            )
            picked = found if picked is None else picked + found
            start += rows
        summary_ref[...] = picked.astype(jnp.bfloat16)


def keys_values(places, hidden, part, weights, accs, gain, cosine, sine, before=(), positions=None):
    rows, features = hidden[0].shape
    head = gain.shape[1]
    row_part = pl.BlockSpec((rows, head), lambda i, p: (part, 0))
    block = pl.BlockSpec((features, head), lambda i, p: (p[LAST], 0))
    in_specs = [whole(*array.shape) for array in (*before, *hidden)]
    in_specs += [block, block, row_part, row_part, whole(1, head), row_part, row_part]
    operands = [*before, *hidden, *weights, *accs, gain, cosine, sine]
    out_shape = [jax.ShapeDtypeStruct((rows, 2 * head), jnp.bfloat16)]
    if before:
        in_specs.append(whole(*positions.shape))
        operands.append(positions)
        out_shape.append(jax.ShapeDtypeStruct((positions.shape[1], 2 * head), jnp.bfloat16))
    return pl.pallas_call(
        functools.partial(keys_values_kernel, len(hidden), len(before)),
        grid_spec=pltpu.PrefetchScalarGridSpec(
            num_scalar_prefetch=1,
            grid=(1,),
            in_specs=in_specs,
            out_specs=[whole(*shape.shape) for shape in out_shape],
        ),
        out_shape=out_shape,
        compiler_params=params(12),
        cost_estimate=cost(1),
        name="keys_values",
    )(places, *operands)


def queries_kernel(count, places_ref, *refs):
    hidden = summed(refs[:count])
    w_ref, acc_ref, gain_ref, cos_ref, sin_ref, q_ref = refs[count:]
    head = gain_ref.shape[1]
    proj = acc_ref[...] + jnp.dot(hidden, w_ref[...], preferred_element_type=jnp.float32)
    for start in range(0, proj.shape[1], head):
        one = norm_rope(proj[:, start : start + head], gain_ref[...], cos_ref[...], sin_ref[...])
        q_ref[:, start : start + head] = one.astype(jnp.bfloat16)


def queries_of(places, hidden, part, weights, acc, gain, cosine, sine):
    rows, features = hidden[0].shape
    head = gain.shape[1]
    width = weights.shape[1]
    tile = 4 * head
    row_part = pl.BlockSpec((rows, head), lambda i, p: (part, 0))
    return pl.pallas_call(
        functools.partial(queries_kernel, len(hidden)),
        grid_spec=pltpu.PrefetchScalarGridSpec(
            num_scalar_prefetch=1,
            grid=(width // tile,),
            in_specs=[whole(rows, features) for _ in hidden]
            + [
                pl.BlockSpec((features, tile), lambda i, p: (p[LAST], i)),
                pl.BlockSpec((rows, tile), lambda i, p: (part, i)),
                whole(1, head),
                row_part,
                row_part,
            ],
            out_specs=pl.BlockSpec((rows, tile), lambda i, p: (0, i)),
        ),
        out_shape=jax.ShapeDtypeStruct((rows, width), jnp.bfloat16),
        compiler_params=params(12),
        cost_estimate=cost(1),
        name="queries",
    )(places, *hidden, weights, acc, gain, cosine, sine)


def attention_kernel(slots, n_parts, n_others, stack, places_ref, length_ref, *refs):
    q_parts, refs = refs[:n_parts], refs[n_parts:]
    own_parts, refs = refs[:n_parts], refs[n_parts:]
    others, refs = refs[:n_others], refs[n_others:]
    o_ref, keys_all, values_all = refs
    part_rows, width = own_parts[0].shape
    head = width // 2
    picks = others[0].shape[0]
    cross = n_others * picks
    rows = o_ref.shape[0] // len(slots)

    start = 0
    for ref in (*others, *own_parts):
        stop = start + ref.shape[0]
        keys_all[start:stop, :] = ref[:, :head]
        values_all[start:stop, :] = ref[:, head:]
        start = stop

    scale = head ** (-0.5) * LOG2E
    own_rows = n_parts * part_rows
    for block, slot in enumerate(slots):
        first = places_ref[slot] * rows
        offset = pl.multiple_of(lax.rem(first, part_rows), rows)
        row = lax.broadcasted_iota(jnp.int32, (rows, own_rows), 0) + first
        column = lax.broadcasted_iota(jnp.int32, (rows, own_rows), 1)
        allowed = jnp.concatenate([column <= row] * stack, axis=0)
        position = lax.broadcasted_iota(jnp.int32, (rows, head), 0) + first
        kept = jnp.concatenate([position < length_ref[0]] * stack, axis=0)
        for left in range(0, o_ref.shape[1], stack * head):
            lanes = [slice(left + i * head, left + (i + 1) * head) for i in range(stack)]
            queries = [q_parts[0][pl.ds(offset, rows), lane] for lane in lanes]
            for part in range(1, n_parts):
                here = first >= part * part_rows
                queries = [
                    jnp.where(here, q_parts[part][pl.ds(offset, rows), lane], query)
                    for lane, query in zip(lanes, queries)
                ]
            scores = lax.dot_general(
                jnp.concatenate(queries, axis=0),
                keys_all[...],
                (((1,), (1,)), ((), ())),
                preferred_element_type=jnp.float32,
            )
            own = jnp.where(allowed, scores[:, cross:], -1e30)
            free = scores[:, :cross]
            largest = jnp.maximum(
                jnp.max(free, axis=1, keepdims=True), jnp.max(own, axis=1, keepdims=True)
            )
            free = jnp.exp2((free - largest) * scale)
            own = jnp.exp2((own - largest) * scale)
            total = jnp.sum(free, axis=1, keepdims=True) + jnp.sum(own, axis=1, keepdims=True)
            mixed = jnp.dot(
                free.astype(jnp.bfloat16), values_all[:cross, :], preferred_element_type=jnp.float32
            ) + jnp.dot(
                own.astype(jnp.bfloat16), values_all[cross:, :], preferred_element_type=jnp.float32
            )
            mixed = jnp.where(kept, mixed / total, 0.0).astype(jnp.bfloat16)
            for index, lane in enumerate(lanes):
                o_ref[block * rows : (block + 1) * rows, lane] = mixed[
                    index * rows : (index + 1) * rows, :
                ]


def attention(places, slots, rows, lengths, queries, own, others):
    n_parts = len(own)
    part_rows, width = queries[0].shape
    head = own[0].shape[1] // 2
    picks = others[0].shape[0]
    reach = n_parts * part_rows + len(others) * picks
    return pl.pallas_call(
        functools.partial(attention_kernel, slots, n_parts, len(others), 512 // rows),
        grid_spec=pltpu.PrefetchScalarGridSpec(
            num_scalar_prefetch=2,
            grid=(1,),
            in_specs=resident(len(queries) + len(own) + len(others)),
            out_specs=resident(1)[0],
            scratch_shapes=[
                pltpu.VMEM((reach, head), jnp.bfloat16),
                pltpu.VMEM((reach, head), jnp.bfloat16),
            ],
        ),
        out_shape=jax.ShapeDtypeStruct((len(slots) * rows, width), jnp.bfloat16),
        compiler_params=params(24 if reach <= 2048 else 56),
        cost_estimate=cost(1),
        name="attention",
    )(places, lengths, *queries, *own, *others)


def mix_kernel(which, block, tiles, rows_ref, w_ref, out_ref):
    height, width = out_ref.shape
    rows = rows_ref[block * height : (block + 1) * height, :]
    tile = width // tiles
    for start in range(0, width, tile):
        left = which * width + start
        total = jnp.dot(rows, w_ref[:, left : left + tile], preferred_element_type=jnp.float32)
        out_ref[:, start : start + tile] = total.astype(out_ref.dtype)


def mix(attended, w_out, which, rows, block=0):
    width = w_out.shape[1] // 2
    return pl.pallas_call(
        functools.partial(mix_kernel, which, block, 5),
        in_specs=resident(2),
        out_specs=resident(1)[0],
        out_shape=jax.ShapeDtypeStruct((rows, width), jnp.bfloat16),
        compiler_params=params(8),
        cost_estimate=cost(1),
        name="mix",
    )(attended, w_out)


def eighth_kernel(places_ref, w_ref, out_ref):
    out_ref[...] = w_ref[...]


def eighth(places, which, w_out, share):
    width = w_out.shape[1] // 2
    return pl.pallas_call(
        eighth_kernel,
        grid_spec=pltpu.PrefetchScalarGridSpec(
            num_scalar_prefetch=1,
            grid=(1,),
            in_specs=[pl.BlockSpec((share, width), lambda i, p: (p[EIGHTHS + which], 1))],
            out_specs=whole(share, width),
        ),
        out_shape=jax.ShapeDtypeStruct((share, width), w_out.dtype),
        compiler_params=params(8),
        cost_estimate=cost(1),
        name="eighth",
    )(places, w_out)


def mix_sent_kernel(block, tiles, places_ref, rows_ref, *refs):
    pieces, out_ref = refs[:-1], refs[-1]
    height = out_ref.shape[0]
    share = rows_ref.shape[1] // len(OFFSETS)
    rows = []
    for index in range(len(OFFSETS)):
        start = pl.multiple_of(places_ref[EIGHTHS + index] * share, share)
        rows.append(rows_ref[block * height : (block + 1) * height, pl.ds(start, share)])
    rows = jnp.concatenate(rows, axis=1)
    tile = out_ref.shape[1] // tiles
    for start in range(0, out_ref.shape[1], tile):
        columns = slice(start, start + tile)
        weights = jnp.concatenate([piece[:, columns] for piece in pieces], axis=0)
        total = jnp.dot(rows, weights, preferred_element_type=jnp.float32)
        out_ref[:, columns] = total.astype(out_ref.dtype)


def mix_sent(places, attended, pieces, rows, block=0):
    width = pieces[0].shape[1]
    return pl.pallas_call(
        functools.partial(mix_sent_kernel, block, 5),
        grid_spec=pltpu.PrefetchScalarGridSpec(
            num_scalar_prefetch=1,
            grid=(1,),
            in_specs=resident(1 + len(pieces)),
            out_specs=resident(1)[0],
        ),
        out_shape=jax.ShapeDtypeStruct((rows, width), jnp.bfloat16),
        compiler_params=params(12),
        cost_estimate=cost(1),
        name="mix_sent",
    )(places, attended, *pieces)


def joined_kernel(*refs):
    start = 0
    for ref in refs[:-1]:
        stop = start + ref.shape[0]
        refs[-1][start:stop, :] = ref[...]
        start = stop


def joined(arrays):
    rows = sum(array.shape[0] for array in arrays)
    return pl.pallas_call(
        joined_kernel,
        in_specs=resident(len(arrays)),
        out_specs=resident(1)[0],
        out_shape=jax.ShapeDtypeStruct((rows, arrays[0].shape[1]), arrays[0].dtype),
        compiler_params=params(8),
        cost_estimate=cost(1),
        name="joined",
    )(*arrays)


def halves_kernel(ref, first_ref, second_ref):
    half = first_ref.shape[0]
    first_ref[...] = ref[:half, :]
    second_ref[...] = ref[half:, :]


def halves(array):
    rows, width = array.shape
    half = jax.ShapeDtypeStruct((rows // 2, width), array.dtype)
    return pl.pallas_call(
        halves_kernel,
        grid=(1,),
        in_specs=[whole(rows, width)],
        out_specs=[whole(rows // 2, width)] * 2,
        out_shape=[half, half],
        compiler_params=params(8),
        cost_estimate=cost(1),
        name="halves",
    )(array)


def add_kernel(count, *refs):
    total = refs[0][...].astype(jnp.float32)
    for ref in refs[1:count]:
        total = total + ref[...].astype(jnp.float32)
    refs[-1][...] = total.astype(jnp.bfloat16)


def added(*arrays, half=None, into=None):
    rows, width = arrays[0].shape
    wide = 1 if half is None else 2
    at = half or 0
    operands = list(arrays)
    in_specs = resident(len(arrays))
    aliases = {}
    if into is not None:
        operands.append(into)
        in_specs.append(pl.BlockSpec(memory_space=pl.ANY))
        aliases = {len(arrays): 0}
    return pl.pallas_call(
        functools.partial(add_kernel, len(arrays)),
        grid=(1,),
        in_specs=in_specs,
        out_specs=pl.BlockSpec((rows, width), lambda i: (0, at)),
        out_shape=jax.ShapeDtypeStruct((rows, wide * width), jnp.bfloat16),
        input_output_aliases=aliases,
        compiler_params=params(8),
        cost_estimate=cost(1),
        name="added",
    )(*operands)


def shards(hidden_in, lengths, summary_pos, w_query, w_key, w_value, w_out, q_gain, k_gain):
    rows_here = hidden_in.shape[0]
    head_width = q_gain.shape[0]
    place = lax.axis_index("tensor")
    n_cand = lax.axis_size("cand")
    assert lax.axis_size("tensor") == 4 and w_key.shape[1] == head_width

    def swap(array):
        return lax.ppermute(array, "tensor", [(0, 1), (1, 0), (2, 3), (3, 2)])

    def across(array):
        return lax.ppermute(array, "tensor", [(1, 2), (2, 1)])

    def outward(array):
        return lax.ppermute(array, "tensor", [(1, 0), (2, 3)])

    def inward(array):
        return lax.ppermute(array, "tensor", [(0, 1), (3, 2)])

    def between(array, offset):
        return lax.ppermute(array, "cand", [(i, i ^ offset) for i in range(n_cand)])

    low = place < 2
    near = jnp.bitwise_xor(place, 1)
    places = [place, near, jnp.where(low, 2, 1), jnp.where(low, 3, 0)]
    places += [jnp.bitwise_xor(lax.axis_index("cand"), offset) for offset in OFFSETS]
    places = jnp.stack(places).astype(jnp.int32)
    share = w_out.shape[0] // n_cand
    spread = n_cand == len(OFFSETS) and share % 128 == 0
    tables = rope_tables(rows_here, head_width)
    k_gain, q_gain = k_gain[None], q_gain[None]
    weights = [w_query, w_key, w_value]
    half = rows_here // 2

    from_near = swap(hidden_in)
    from_mid = [across(array) for array in halves(hidden_in)]
    accs = partial_projection(places, OWN, [[hidden_in]], weights, None)
    from_mid[0], accs = lax.optimization_barrier((from_mid[0], accs))
    to_outer = [outward(from_mid[0])]
    accs = partial_projection(after(places, from_mid[1]), NEAR, [[from_near]], weights, accs)
    from_near = halves(from_near)
    to_outer.append(outward(after(from_mid[1], from_near)))
    to_inner = [across(from_near[0])]
    to_inner.append(across(after(from_near[1], (to_outer[0], accs))))
    end = [outward(array) for array in to_inner]
    pieces = {}
    if spread:
        first, second = (eighth(places, i, w_out, share) for i in (0, 1))
        pieces[0] = inward(after(first, to_outer[0]))
        cue = to_outer[1]
        pieces[6] = inward(after(second, cue))
        first = after(pieces[0], cue)
        pieces[2], pieces[4] = between(first, 2), between(first, 4)
    cue = (to_inner, accs)
    accs = partial_projection(
        after(places, cue), THIRD, [[a, b] for a, b in zip(from_mid, to_outer)], weights, accs
    )

    pieces = [joined([pieces[offset] for offset in OFFSETS[:4]])] if spread else []
    final = [[a, b] for a, b in zip(to_inner, end)]
    (own_first,) = keys_values(places, final[0], 0, weights[1:], accs[1:], k_gain, *tables)
    first_queries = queries_of(places, final[0], 0, w_query, accs[0], q_gain, *tables)
    own_second, summary = keys_values(
        places,
        final[1],
        1,
        weights[1:],
        after(accs[1:], (first_queries, pieces)),
        k_gain,
        *tables,
        [own_first],
        summary_pos,
    )
    own = [own_first, own_second]
    others = [between(summary, offset) for offset in range(1, n_cand)]
    second_queries = queries_of(places, final[1], 1, w_query, accs[0], q_gain, *tables)
    queries = [first_queries, second_queries]

    if spread:
        pieces.append(between(after(pieces[0], (others, second_queries)), 1))
    part = rows_here // 4

    def attend(*slots):
        return attention(places, slots, part, lengths, queries, own, others)

    def mixed(rows, which, block=0):
        return mix(rows, w_out, which, part, block)

    def share_of(arrived, block=0):
        return mix_sent(places, arrived, pieces, part, block)

    far_rows = attend(LAST)
    far = [mixed(far_rows, which) for which in (0, 1)]
    places = after(places, far)
    rows = attend(THIRD, NEAR)
    if spread:
        far_sent = after(inward(far_rows), rows)
        far_in = inward(after(far[0], far_sent))
        far_share = share_of(far_sent)
        rows_sent = inward(rows)
    else:
        far_in, far_share = inward(far[0]), inward(far[1])
    far_right = added(far[1], far_share)
    far_left = added(far[0], after(far_in, far_right))
    third = [mixed(after(rows, far_left), which) for which in (0, 1)]
    far_right = across(far_right)
    if spread:
        rows_sent = after(rows_sent, third)
        third_in = inward(after(third[0], rows_sent))
        third_share = share_of(rows_sent)
    else:
        third_in, third_share = inward(third[0]), inward(third[1])
    far_left = across(far_left)
    third_right = added(third[1], third_share)
    near = [None, mixed(after(rows, (third_right, far_right)), 1, 1)]
    third_right = across(third_right)
    out_right = added(near[1], far_right)
    near[0] = mixed(after(rows, out_right), 0, 1)
    out_left = added(near[0], far_left)
    third_left = added(third[0], after(third_in, out_left))
    near_in = inward(after(near[0], third_left))
    places = after(places, third_left)
    own_rows = attend(OWN)
    kept = [mixed(own_rows, which) for which in (0, 1)]
    near_share = share_of(after(rows_sent, kept), 1) if spread else inward(near[1])
    result = added(kept[1], near_share, outward(out_right), third_right, half=1)
    out_left, third_left = outward(out_left), across(third_left)
    return added(kept[0], near_in, out_left, third_left, half=0, into=result)


def solution(mesh):
    return jax.shard_map(
        shards,
        mesh=mesh,
        in_specs=(
            P("cand", "tensor"),
            P("cand"),
            P("cand", None),
            P(None, "tensor"),
            P(None, "tensor"),
            P(None, "tensor"),
            P("tensor", None),
            P(),
            P(),
        ),
        out_specs=P(("cand", "tensor"), None),
        check_vma=False,
    )
```

```python
import functools

import jax
import jax.numpy as jnp
import numpy as np
from jax import lax
from jax.experimental import pallas as pl
from jax.experimental.pallas import tpu as pltpu
from jax.sharding import PartitionSpec as P

MIB = 1024 * 1024
LOG2E = 1.4426950408889634
OWN, NEAR, THIRD, LAST, EIGHTHS = range(5)
OFFSETS = (0, 6, 2, 4, 1, 7, 3, 5)


def rope_tables(rows, width):
    half_width = width // 2
    frequency = (1000000.0 ** (-(np.arange(half_width) * 2.0 / width))).astype(np.float32)
    angle = np.arange(rows, dtype=np.float32)[:, None] * frequency[None, :]
    angle = angle.astype(np.float64)
    cosine, sine = np.cos(angle), np.sin(angle)
    return (
        jnp.asarray(np.concatenate([cosine, cosine], axis=1).astype(np.float32)),
        jnp.asarray(np.concatenate([-sine, sine], axis=1).astype(np.float32)),
    )


def norm_rope(vectors, gain, cosine, sine):
    scale = lax.rsqrt(jnp.mean(vectors * vectors, axis=-1, keepdims=True) + 1e-06)
    vectors = vectors * scale * gain
    return vectors * cosine + pltpu.roll(vectors, vectors.shape[-1] // 2, 1) * sine


def params(mebibytes):
    return pltpu.CompilerParams(vmem_limit_bytes=mebibytes * MIB)


def cost(flops):
    return pl.CostEstimate(flops=flops, bytes_accessed=1, transcendentals=0)


def after(array, cue):
    return lax.optimization_barrier((array, cue))[0]


def whole(*shape):
    return pl.BlockSpec(shape, lambda *_: (0,) * len(shape))


def resident(count):
    return [pl.BlockSpec(memory_space=pltpu.VMEM)] * count


def summed(refs):
    total = refs[0][...]
    for ref in refs[1:]:
        total = total + ref[...]
    return total


def partial_kernel(counts, with_acc, places_ref, *refs):
    rows = []
    for count in counts:
        rows.append(summed(refs[:count]))
        refs = refs[count:]
    hidden = jnp.concatenate(rows, axis=0) if len(rows) > 1 else rows[0]
    weights, outs = refs[:3], refs[-3:]
    accs = refs[3:6] if with_acc else (None,) * 3
    step = pl.program_id(0)

    def add(w_ref, acc_ref, out_ref):
        product = jnp.dot(hidden, w_ref[...], preferred_element_type=jnp.float32)
        out_ref[...] = product if acc_ref is None else product + acc_ref[...]

    add(weights[0], accs[0], outs[0])

    @pl.when(step == 0)
    def _():
        add(weights[1], accs[1], outs[1])
        add(weights[2], accs[2], outs[2])


def partial_projection(places, slot, parts, weights, accs):
    features = parts[0][0].shape[1]
    rows = sum(part[0].shape[0] for part in parts)
    arrivals = [array for part in parts for array in part]
    widths = [weight.shape[1] for weight in weights]
    tile = 512
    column = lambda height: pl.BlockSpec((height, tile), lambda i, p: (0, i))
    per_array = lambda height: [column(height), whole(height, widths[1]), whole(height, widths[2])]
    block = lambda width: pl.BlockSpec((features, width), lambda i, p: (p[slot], 0))
    in_specs = [whole(*array.shape) for array in arrivals]
    in_specs.append(pl.BlockSpec((features, tile), lambda i, p: (p[slot], i)))
    in_specs += [block(widths[1]), block(widths[2])]
    operands = [*arrivals, *weights]
    if accs is not None:
        in_specs += per_array(rows)
        operands += accs
    return pl.pallas_call(
        functools.partial(partial_kernel, [len(part) for part in parts], accs is not None),
        grid_spec=pltpu.PrefetchScalarGridSpec(
            num_scalar_prefetch=1,
            grid=(widths[0] // tile,),
            in_specs=in_specs,
            out_specs=per_array(rows),
        ),
        out_shape=[jax.ShapeDtypeStruct((rows, width), jnp.float32) for width in widths],
        compiler_params=params(20),
        cost_estimate=cost(1),
        name="partial_projection",
    )(places, *operands)


def keys_values_kernel(count, n_before, places_ref, *refs):
    before, refs = refs[:n_before], refs[n_before:]
    hidden = summed(refs[:count])
    wk_ref, wv_ref, acck_ref, accv_ref, gain_ref, cos_ref, sin_ref = refs[count : count + 7]
    refs = refs[count + 7 :]
    head = gain_ref.shape[1]
    out_ref = refs[0] if n_before == 0 else refs[1]
    keys = acck_ref[...] + jnp.dot(hidden, wk_ref[...], preferred_element_type=jnp.float32)
    values = accv_ref[...] + jnp.dot(hidden, wv_ref[...], preferred_element_type=jnp.float32)
    keys = norm_rope(keys, gain_ref[...], cos_ref[...], sin_ref[...])
    out_ref[:, :head] = keys.astype(jnp.bfloat16)
    out_ref[:, head:] = values.astype(jnp.bfloat16)
    if n_before:
        pos_ref, summary_ref = refs[0], refs[2]
        picks = pos_ref.shape[1]
        picked, start = None, 0
        for ref in (*before, out_ref):
            rows = ref.shape[0]
            row = lax.broadcasted_iota(jnp.int32, (rows, picks), 0) + start
            chosen = jnp.where(row == pos_ref[...], 1.0, 0.0).astype(jnp.bfloat16)
            found = lax.dot_general(
                chosen, ref[...], (((0,), (0,)), ((), ())), preferred_element_type=jnp.float32
            )
            picked = found if picked is None else picked + found
            start += rows
        summary_ref[...] = picked.astype(jnp.bfloat16)


def keys_values(places, hidden, part, weights, accs, gain, cosine, sine, before=(), positions=None):
    rows, features = hidden[0].shape
    head = gain.shape[1]
    row_part = pl.BlockSpec((rows, head), lambda i, p: (part, 0))
    block = pl.BlockSpec((features, head), lambda i, p: (p[LAST], 0))
    in_specs = [whole(*array.shape) for array in (*before, *hidden)]
    in_specs += [block, block, row_part, row_part, whole(1, head), row_part, row_part]
    operands = [*before, *hidden, *weights, *accs, gain, cosine, sine]
    out_shape = [jax.ShapeDtypeStruct((rows, 2 * head), jnp.bfloat16)]
    if before:
        in_specs.append(whole(*positions.shape))
        operands.append(positions)
        out_shape.append(jax.ShapeDtypeStruct((positions.shape[1], 2 * head), jnp.bfloat16))
    return pl.pallas_call(
        functools.partial(keys_values_kernel, len(hidden), len(before)),
        grid_spec=pltpu.PrefetchScalarGridSpec(
            num_scalar_prefetch=1,
            grid=(1,),
            in_specs=in_specs,
            out_specs=[whole(*shape.shape) for shape in out_shape],
        ),
        out_shape=out_shape,
        compiler_params=params(12),
        cost_estimate=cost(1),
        name="keys_values",
    )(places, *operands)


def queries_kernel(count, places_ref, *refs):
    hidden = summed(refs[:count])
    w_ref, acc_ref, gain_ref, cos_ref, sin_ref, q_ref = refs[count:]
    head = gain_ref.shape[1]
    proj = acc_ref[...] + jnp.dot(hidden, w_ref[...], preferred_element_type=jnp.float32)
    for start in range(0, proj.shape[1], head):
        one = norm_rope(proj[:, start : start + head], gain_ref[...], cos_ref[...], sin_ref[...])
        q_ref[:, start : start + head] = one.astype(jnp.bfloat16)


def queries_of(places, hidden, part, weights, acc, gain, cosine, sine):
    rows, features = hidden[0].shape
    head = gain.shape[1]
    width = weights.shape[1]
    tile = 4 * head
    row_part = pl.BlockSpec((rows, head), lambda i, p: (part, 0))
    return pl.pallas_call(
        functools.partial(queries_kernel, len(hidden)),
        grid_spec=pltpu.PrefetchScalarGridSpec(
            num_scalar_prefetch=1,
            grid=(width // tile,),
            in_specs=[whole(rows, features) for _ in hidden]
            + [
                pl.BlockSpec((features, tile), lambda i, p: (p[LAST], i)),
                pl.BlockSpec((rows, tile), lambda i, p: (part, i)),
                whole(1, head),
                row_part,
                row_part,
            ],
            out_specs=pl.BlockSpec((rows, tile), lambda i, p: (0, i)),
        ),
        out_shape=jax.ShapeDtypeStruct((rows, width), jnp.bfloat16),
        compiler_params=params(12),
        cost_estimate=cost(1),
        name="queries",
    )(places, *hidden, weights, acc, gain, cosine, sine)


def attention_kernel(slots, n_parts, n_others, stack, places_ref, length_ref, *refs):
    q_parts, refs = refs[:n_parts], refs[n_parts:]
    own_parts, refs = refs[:n_parts], refs[n_parts:]
    others, refs = refs[:n_others], refs[n_others:]
    o_refs, (keys_all, values_all) = refs[:-2], refs[-2:]
    part_rows, width = own_parts[0].shape
    head = width // 2
    picks = others[0].shape[0]
    cross = n_others * picks
    rows = o_refs[0].shape[0]

    start = 0
    for ref in (*others, *own_parts):
        stop = start + ref.shape[0]
        keys_all[start:stop, :] = ref[:, :head]
        values_all[start:stop, :] = ref[:, head:]
        start = stop

    scale = head ** (-0.5) * LOG2E
    own_rows = n_parts * part_rows
    for slot, o_ref in zip(slots, o_refs):
        first = places_ref[slot] * rows
        offset = pl.multiple_of(lax.rem(first, part_rows), rows)
        row = lax.broadcasted_iota(jnp.int32, (rows, own_rows), 0) + first
        column = lax.broadcasted_iota(jnp.int32, (rows, own_rows), 1)
        allowed = jnp.concatenate([column <= row] * stack, axis=0)
        position = lax.broadcasted_iota(jnp.int32, (rows, head), 0) + first
        kept = jnp.concatenate([position < length_ref[0]] * stack, axis=0)
        for left in range(0, o_ref.shape[1], stack * head):
            lanes = [slice(left + i * head, left + (i + 1) * head) for i in range(stack)]
            queries = [q_parts[0][pl.ds(offset, rows), lane] for lane in lanes]
            for part in range(1, n_parts):
                here = first >= part * part_rows
                queries = [
                    jnp.where(here, q_parts[part][pl.ds(offset, rows), lane], query)
                    for lane, query in zip(lanes, queries)
                ]
            scores = lax.dot_general(
                jnp.concatenate(queries, axis=0),
                keys_all[...],
                (((1,), (1,)), ((), ())),
                preferred_element_type=jnp.float32,
            )
            own = jnp.where(allowed, scores[:, cross:], -1e30)
            free = scores[:, :cross]
            largest = jnp.maximum(
                jnp.max(free, axis=1, keepdims=True), jnp.max(own, axis=1, keepdims=True)
            )
            free = jnp.exp2((free - largest) * scale)
            own = jnp.exp2((own - largest) * scale)
            total = jnp.sum(free, axis=1, keepdims=True) + jnp.sum(own, axis=1, keepdims=True)
            mixed = jnp.dot(
                free.astype(jnp.bfloat16), values_all[:cross, :], preferred_element_type=jnp.float32
            ) + jnp.dot(
                own.astype(jnp.bfloat16), values_all[cross:, :], preferred_element_type=jnp.float32
            )
            mixed = jnp.where(kept, mixed / total, 0.0).astype(jnp.bfloat16)
            for index, lane in enumerate(lanes):
                o_ref[:, lane] = mixed[index * rows : (index + 1) * rows, :]


def attention(places, slots, rows, lengths, queries, own, others):
    n_parts = len(own)
    part_rows, width = queries[0].shape
    head = own[0].shape[1] // 2
    picks = others[0].shape[0]
    reach = n_parts * part_rows + len(others) * picks
    return pl.pallas_call(
        functools.partial(attention_kernel, slots, n_parts, len(others), 512 // rows),
        grid_spec=pltpu.PrefetchScalarGridSpec(
            num_scalar_prefetch=2,
            grid=(1,),
            in_specs=resident(len(queries) + len(own) + len(others)),
            out_specs=resident(len(slots)),
            scratch_shapes=[
                pltpu.VMEM((reach, head), jnp.bfloat16),
                pltpu.VMEM((reach, head), jnp.bfloat16),
            ],
        ),
        out_shape=[jax.ShapeDtypeStruct((rows, width), jnp.bfloat16) for _ in slots],
        compiler_params=params(24 if reach <= 2048 else 56),
        cost_estimate=cost(1),
        name="attention",
    )(places, lengths, *queries, *own, *others)


def mix_kernel(which, tiles, rows_ref, w_ref, out_ref):
    width = out_ref.shape[1]
    tile = width // tiles
    for start in range(0, width, tile):
        left = which * width + start
        total = jnp.dot(
            rows_ref[...], w_ref[:, left : left + tile], preferred_element_type=jnp.float32
        )
        out_ref[:, start : start + tile] = total.astype(out_ref.dtype)


def mix(attended, w_out, which):
    rows = attended.shape[0]
    width = w_out.shape[1] // 2
    return pl.pallas_call(
        functools.partial(mix_kernel, which, 5),
        in_specs=resident(2),
        out_specs=resident(1)[0],
        out_shape=jax.ShapeDtypeStruct((rows, width), jnp.bfloat16),
        compiler_params=params(8),
        cost_estimate=cost(1),
        name="mix",
    )(attended, w_out)


def eighth_kernel(places_ref, w_ref, out_ref):
    out_ref[...] = w_ref[...]


def eighth(places, which, w_out, share):
    width = w_out.shape[1] // 2
    return pl.pallas_call(
        eighth_kernel,
        grid_spec=pltpu.PrefetchScalarGridSpec(
            num_scalar_prefetch=1,
            grid=(1,),
            in_specs=[pl.BlockSpec((share, width), lambda i, p: (p[EIGHTHS + which], 1))],
            out_specs=whole(share, width),
        ),
        out_shape=jax.ShapeDtypeStruct((share, width), w_out.dtype),
        compiler_params=params(8),
        cost_estimate=cost(1),
        name="eighth",
    )(places, w_out)


def mix_sent_kernel(tiles, places_ref, rows_ref, *refs):
    pieces, out_ref = refs[:-1], refs[-1]
    share = rows_ref.shape[1] // len(OFFSETS)
    rows = []
    for index in range(len(OFFSETS)):
        start = pl.multiple_of(places_ref[EIGHTHS + index] * share, share)
        rows.append(rows_ref[:, pl.ds(start, share)])
    rows = jnp.concatenate(rows, axis=1)
    tile = out_ref.shape[1] // tiles
    for start in range(0, out_ref.shape[1], tile):
        columns = slice(start, start + tile)
        weights = jnp.concatenate([piece[:, columns] for piece in pieces], axis=0)
        total = jnp.dot(rows, weights, preferred_element_type=jnp.float32)
        out_ref[:, columns] = total.astype(out_ref.dtype)


def mix_sent(places, attended, pieces):
    rows = attended.shape[0]
    width = pieces[0].shape[1]
    return pl.pallas_call(
        functools.partial(mix_sent_kernel, 5),
        grid_spec=pltpu.PrefetchScalarGridSpec(
            num_scalar_prefetch=1,
            grid=(1,),
            in_specs=resident(1 + len(pieces)),
            out_specs=resident(1)[0],
        ),
        out_shape=jax.ShapeDtypeStruct((rows, width), jnp.bfloat16),
        compiler_params=params(12),
        cost_estimate=cost(1),
        name="mix_sent",
    )(places, attended, *pieces)


def halves_kernel(ref, first_ref, second_ref):
    half = first_ref.shape[0]
    first_ref[...] = ref[:half, :]
    second_ref[...] = ref[half:, :]


def halves(array):
    rows, width = array.shape
    half = jax.ShapeDtypeStruct((rows // 2, width), array.dtype)
    return pl.pallas_call(
        halves_kernel,
        grid=(1,),
        in_specs=[whole(rows, width)],
        out_specs=[whole(rows // 2, width)] * 2,
        out_shape=[half, half],
        compiler_params=params(8),
        cost_estimate=cost(1),
        name="halves",
    )(array)


def add_kernel(count, *refs):
    total = refs[0][...].astype(jnp.float32)
    for ref in refs[1:count]:
        total = total + ref[...].astype(jnp.float32)
    refs[-1][...] = total.astype(jnp.bfloat16)


def added(*arrays, half=None, into=None):
    rows, width = arrays[0].shape
    wide = 1 if half is None else 2
    at = half or 0
    operands = list(arrays)
    in_specs = resident(len(arrays))
    aliases = {}
    if into is not None:
        operands.append(into)
        in_specs.append(pl.BlockSpec(memory_space=pl.ANY))
        aliases = {len(arrays): 0}
    return pl.pallas_call(
        functools.partial(add_kernel, len(arrays)),
        grid=(1,),
        in_specs=in_specs,
        out_specs=pl.BlockSpec((rows, width), lambda i: (0, at)),
        out_shape=jax.ShapeDtypeStruct((rows, wide * width), jnp.bfloat16),
        input_output_aliases=aliases,
        compiler_params=params(8),
        cost_estimate=cost(1),
        name="added",
    )(*operands)


def shards(hidden_in, lengths, summary_pos, w_query, w_key, w_value, w_out, q_gain, k_gain):
    rows_here = hidden_in.shape[0]
    head_width = q_gain.shape[0]
    place = lax.axis_index("tensor")
    n_cand = lax.axis_size("cand")
    assert lax.axis_size("tensor") == 4 and w_key.shape[1] == head_width

    def swap(array):
        return lax.ppermute(array, "tensor", [(0, 1), (1, 0), (2, 3), (3, 2)])

    def across(array):
        return lax.ppermute(array, "tensor", [(1, 2), (2, 1)])

    def outward(array):
        return lax.ppermute(array, "tensor", [(1, 0), (2, 3)])

    def inward(array):
        return lax.ppermute(array, "tensor", [(0, 1), (3, 2)])

    def between(array, offset):
        return lax.ppermute(array, "cand", [(i, i ^ offset) for i in range(n_cand)])

    low = place < 2
    near = jnp.bitwise_xor(place, 1)
    places = [place, near, jnp.where(low, 2, 1), jnp.where(low, 3, 0)]
    places += [jnp.bitwise_xor(lax.axis_index("cand"), offset) for offset in OFFSETS]
    places = jnp.stack(places).astype(jnp.int32)
    share = w_out.shape[0] // n_cand
    spread = n_cand == len(OFFSETS) and share % 128 == 0
    tables = rope_tables(rows_here, head_width)
    k_gain, q_gain = k_gain[None], q_gain[None]
    weights = [w_query, w_key, w_value]
    half = rows_here // 2

    from_near = swap(hidden_in)
    from_mid = [across(array) for array in halves(hidden_in)]
    accs = partial_projection(places, OWN, [[hidden_in]], weights, None)
    from_mid[0], accs = lax.optimization_barrier((from_mid[0], accs))
    to_outer = [outward(from_mid[0])]
    accs = partial_projection(after(places, from_mid[1]), NEAR, [[from_near]], weights, accs)
    from_near = halves(from_near)
    to_outer.append(outward(after(from_mid[1], from_near)))
    to_inner = [across(from_near[0])]
    to_inner.append(across(after(from_near[1], (to_outer[0], accs))))
    end = [outward(array) for array in to_inner]
    pieces = {}
    if spread:
        first, second = (eighth(places, i, w_out, share) for i in (0, 1))
        pieces[0] = inward(after(first, to_outer[0]))
        cue = to_outer[1]
        pieces[6] = inward(after(second, cue))
        first = after(pieces[0], cue)
        pieces[2], pieces[4] = between(first, 2), between(first, 4)
    cue = (to_inner, accs)
    accs = partial_projection(
        after(places, cue), THIRD, [[a, b] for a, b in zip(from_mid, to_outer)], weights, accs
    )

    final = [[a, b] for a, b in zip(to_inner, end)]
    (own_first,) = keys_values(places, final[0], 0, weights[1:], accs[1:], k_gain, *tables)
    first_queries = queries_of(places, final[0], 0, w_query, accs[0], q_gain, *tables)
    own_second, summary = keys_values(
        places,
        final[1],
        1,
        weights[1:],
        after(accs[1:], (first_queries, pieces)),
        k_gain,
        *tables,
        [own_first],
        summary_pos,
    )
    own = [own_first, own_second]
    others = [between(summary, offset) for offset in reversed(range(1, n_cand))]
    second_queries = queries_of(places, final[1], 1, w_query, accs[0], q_gain, *tables)
    queries = [first_queries, second_queries]

    if spread:
        cue = (others, second_queries)
        for offset in (0, 6, 2, 4):
            pieces[offset ^ 1] = between(after(pieces[offset], cue), 1)

    def attend(slots):
        return attention(places, slots, rows_here // 4, lengths, queries, own, others)

    def send(rows, part):
        return inward(rows if spread else part)

    def share_of(arrived):
        if not spread:
            return arrived
        return mix_sent(places, arrived, [pieces[offset] for offset in OFFSETS])

    def mixed(rows):
        return [mix(rows, w_out, which) for which in (0, 1)]

    (far_rows,) = attend((LAST,))
    far = mixed(far_rows)
    far_sent = send(far_rows, far[1])
    places = after(places, far)
    (third_rows,) = attend((THIRD,))
    far_sent = after(far_sent, third_rows)
    far_in = inward(after(far[0], far_sent))
    far_right = added(far[1], share_of(far_sent))
    places = after(places, far_right)
    near_rows, own_rows = attend((NEAR, OWN))
    third = mixed(after(third_rows, near_rows))
    third_sent = send(third_rows, third[1])
    far_right = across(far_right)
    far_left = added(far[0], after(far_in, third))
    third_sent = after(third_sent, far_left)
    far_left = across(far_left)
    third_in = inward(after(third[0], third_sent))
    third_right = added(third[1], share_of(third_sent))
    near = [None, mix(after(near_rows, (third_right, far_right)), w_out, 1)]
    near_sent = send(near_rows, near[1])
    third_right = across(third_right)
    out_right = added(near[1], far_right)
    near[0] = mix(after(near_rows, out_right), w_out, 0)
    out_left = added(near[0], far_left)
    third_left = added(third[0], after(third_in, out_left))
    kept = mixed(after(own_rows, third_left))
    near_sent = share_of(after(near_sent, third_left))
    result = added(kept[1], near_sent, outward(out_right), third_right, half=1)
    near_in = inward(after(near[0], third_left))
    out_left, third_left = outward(out_left), across(third_left)
    return added(kept[0], near_in, out_left, third_left, half=0, into=result)


def solution(mesh):
    return jax.shard_map(
        shards,
        mesh=mesh,
        in_specs=(
            P("cand", "tensor"),
            P("cand"),
            P("cand", None),
            P(None, "tensor"),
            P(None, "tensor"),
            P(None, "tensor"),
            P("tensor", None),
            P(),
            P(),
        ),
        out_specs=P(("cand", "tensor"), None),
        check_vma=False,
    )
```

```python
import functools

import jax
import jax.numpy as jnp
import numpy as np
from jax import lax
from jax.experimental import pallas as pl
from jax.experimental.pallas import tpu as pltpu
from jax.sharding import PartitionSpec as P

MIB = 1024 * 1024
LOG2E = 1.4426950408889634
OWN, NEAR, THIRD, LAST, EIGHTHS = range(5)
OFFSETS = (0, 6, 2, 4, 1, 7, 3, 5)


def rope_tables(rows, width):
    half_width = width // 2
    frequency = (1000000.0 ** (-(np.arange(half_width) * 2.0 / width))).astype(np.float32)
    angle = np.arange(rows, dtype=np.float32)[:, None] * frequency[None, :]
    angle = angle.astype(np.float64)
    cosine, sine = np.cos(angle), np.sin(angle)
    return (
        jnp.asarray(np.concatenate([cosine, cosine], axis=1).astype(np.float32)),
        jnp.asarray(np.concatenate([-sine, sine], axis=1).astype(np.float32)),
    )


def norm_rope(vectors, gain, cosine, sine):
    scale = lax.rsqrt(jnp.mean(vectors * vectors, axis=-1, keepdims=True) + 1e-06)
    vectors = vectors * scale * gain
    return vectors * cosine + pltpu.roll(vectors, vectors.shape[-1] // 2, 1) * sine


def params(mebibytes):
    return pltpu.CompilerParams(vmem_limit_bytes=mebibytes * MIB)


def cost(flops):
    return pl.CostEstimate(flops=flops, bytes_accessed=1, transcendentals=0)


def after(array, cue):
    return lax.optimization_barrier((array, cue))[0]


def whole(*shape):
    return pl.BlockSpec(shape, lambda *_: (0,) * len(shape))


def resident(count):
    return [pl.BlockSpec(memory_space=pltpu.VMEM)] * count


def summed(refs):
    total = refs[0][...]
    for ref in refs[1:]:
        total = total + ref[...]
    return total


def partial_kernel(counts, with_acc, places_ref, *refs):
    rows = []
    for count in counts:
        rows.append(summed(refs[:count]))
        refs = refs[count:]
    hidden = jnp.concatenate(rows, axis=0) if len(rows) > 1 else rows[0]
    weights, outs = refs[:3], refs[-3:]
    accs = refs[3:6] if with_acc else (None,) * 3
    step = pl.program_id(0)

    def add(w_ref, acc_ref, out_ref):
        product = jnp.dot(hidden, w_ref[...], preferred_element_type=jnp.float32)
        out_ref[...] = product if acc_ref is None else product + acc_ref[...]

    add(weights[0], accs[0], outs[0])

    @pl.when(step == 0)
    def _():
        add(weights[1], accs[1], outs[1])
        add(weights[2], accs[2], outs[2])


def partial_projection(places, slot, parts, weights, accs):
    features = parts[0][0].shape[1]
    rows = sum(part[0].shape[0] for part in parts)
    arrivals = [array for part in parts for array in part]
    widths = [weight.shape[1] for weight in weights]
    tile = 512
    column = lambda height: pl.BlockSpec((height, tile), lambda i, p: (0, i))
    per_array = lambda height: [column(height), whole(height, widths[1]), whole(height, widths[2])]
    block = lambda width: pl.BlockSpec((features, width), lambda i, p: (p[slot], 0))
    in_specs = [whole(*array.shape) for array in arrivals]
    in_specs.append(pl.BlockSpec((features, tile), lambda i, p: (p[slot], i)))
    in_specs += [block(widths[1]), block(widths[2])]
    operands = [*arrivals, *weights]
    if accs is not None:
        in_specs += per_array(rows)
        operands += accs
    return pl.pallas_call(
        functools.partial(partial_kernel, [len(part) for part in parts], accs is not None),
        grid_spec=pltpu.PrefetchScalarGridSpec(
            num_scalar_prefetch=1,
            grid=(widths[0] // tile,),
            in_specs=in_specs,
            out_specs=per_array(rows),
        ),
        out_shape=[jax.ShapeDtypeStruct((rows, width), jnp.float32) for width in widths],
        compiler_params=params(20),
        cost_estimate=cost(1),
        name="partial_projection",
    )(places, *operands)


def keys_values_kernel(count, n_before, places_ref, *refs):
    before, refs = refs[:n_before], refs[n_before:]
    hidden = summed(refs[:count])
    wk_ref, wv_ref, acck_ref, accv_ref, gain_ref, cos_ref, sin_ref = refs[count : count + 7]
    refs = refs[count + 7 :]
    head = gain_ref.shape[1]
    out_ref = refs[0] if n_before == 0 else refs[1]
    keys = acck_ref[...] + jnp.dot(hidden, wk_ref[...], preferred_element_type=jnp.float32)
    values = accv_ref[...] + jnp.dot(hidden, wv_ref[...], preferred_element_type=jnp.float32)
    keys = norm_rope(keys, gain_ref[...], cos_ref[...], sin_ref[...])
    out_ref[:, :head] = keys.astype(jnp.bfloat16)
    out_ref[:, head:] = values.astype(jnp.bfloat16)
    if n_before:
        pos_ref, summary_ref = refs[0], refs[2]
        picks = pos_ref.shape[1]
        picked, start = None, 0
        for ref in (*before, out_ref):
            rows = ref.shape[0]
            row = lax.broadcasted_iota(jnp.int32, (rows, picks), 0) + start
            chosen = jnp.where(row == pos_ref[...], 1.0, 0.0).astype(jnp.bfloat16)
            found = lax.dot_general(
                chosen, ref[...], (((0,), (0,)), ((), ())), preferred_element_type=jnp.float32
            )
            picked = found if picked is None else picked + found
            start += rows
        summary_ref[...] = picked.astype(jnp.bfloat16)


def keys_values(places, hidden, part, weights, accs, gain, cosine, sine, before=(), positions=None):
    rows, features = hidden[0].shape
    head = gain.shape[1]
    row_part = pl.BlockSpec((rows, head), lambda i, p: (part, 0))
    block = pl.BlockSpec((features, head), lambda i, p: (p[LAST], 0))
    in_specs = [whole(*array.shape) for array in (*before, *hidden)]
    in_specs += [block, block, row_part, row_part, whole(1, head), row_part, row_part]
    operands = [*before, *hidden, *weights, *accs, gain, cosine, sine]
    out_shape = [jax.ShapeDtypeStruct((rows, 2 * head), jnp.bfloat16)]
    if before:
        in_specs.append(whole(*positions.shape))
        operands.append(positions)
        out_shape.append(jax.ShapeDtypeStruct((positions.shape[1], 2 * head), jnp.bfloat16))
    return pl.pallas_call(
        functools.partial(keys_values_kernel, len(hidden), len(before)),
        grid_spec=pltpu.PrefetchScalarGridSpec(
            num_scalar_prefetch=1,
            grid=(1,),
            in_specs=in_specs,
            out_specs=[whole(*shape.shape) for shape in out_shape],
        ),
        out_shape=out_shape,
        compiler_params=params(12),
        cost_estimate=cost(1),
        name="keys_values",
    )(places, *operands)


def queries_kernel(count, places_ref, *refs):
    hidden = summed(refs[:count])
    w_ref, acc_ref, gain_ref, cos_ref, sin_ref, q_ref = refs[count:]
    head = gain_ref.shape[1]
    proj = acc_ref[...] + jnp.dot(hidden, w_ref[...], preferred_element_type=jnp.float32)
    for start in range(0, proj.shape[1], head):
        one = norm_rope(proj[:, start : start + head], gain_ref[...], cos_ref[...], sin_ref[...])
        q_ref[:, start : start + head] = one.astype(jnp.bfloat16)


def queries_of(places, hidden, part, weights, acc, gain, cosine, sine):
    rows, features = hidden[0].shape
    head = gain.shape[1]
    width = weights.shape[1]
    tile = 4 * head
    row_part = pl.BlockSpec((rows, head), lambda i, p: (part, 0))
    return pl.pallas_call(
        functools.partial(queries_kernel, len(hidden)),
        grid_spec=pltpu.PrefetchScalarGridSpec(
            num_scalar_prefetch=1,
            grid=(width // tile,),
            in_specs=[whole(rows, features) for _ in hidden]
            + [
                pl.BlockSpec((features, tile), lambda i, p: (p[LAST], i)),
                pl.BlockSpec((rows, tile), lambda i, p: (part, i)),
                whole(1, head),
                row_part,
                row_part,
            ],
            out_specs=pl.BlockSpec((rows, tile), lambda i, p: (0, i)),
        ),
        out_shape=jax.ShapeDtypeStruct((rows, width), jnp.bfloat16),
        compiler_params=params(12),
        cost_estimate=cost(1),
        name="queries",
    )(places, *hidden, weights, acc, gain, cosine, sine)


def attention_kernel(slots, n_parts, n_others, stack, places_ref, length_ref, *refs):
    q_parts, refs = refs[:n_parts], refs[n_parts:]
    own_parts, refs = refs[:n_parts], refs[n_parts:]
    others, refs = refs[:n_others], refs[n_others:]
    o_refs, (keys_all, values_all) = refs[:-2], refs[-2:]
    part_rows, width = own_parts[0].shape
    head = width // 2
    picks = others[0].shape[0]
    cross = n_others * picks
    rows = o_refs[0].shape[0]

    start = 0
    for ref in (*others, *own_parts):
        stop = start + ref.shape[0]
        keys_all[start:stop, :] = ref[:, :head]
        values_all[start:stop, :] = ref[:, head:]
        start = stop

    scale = head ** (-0.5) * LOG2E
    own_rows = n_parts * part_rows
    for slot, o_ref in zip(slots, o_refs):
        first = places_ref[slot] * rows
        offset = pl.multiple_of(lax.rem(first, part_rows), rows)
        row = lax.broadcasted_iota(jnp.int32, (rows, own_rows), 0) + first
        column = lax.broadcasted_iota(jnp.int32, (rows, own_rows), 1)
        allowed = jnp.concatenate([column <= row] * stack, axis=0)
        position = lax.broadcasted_iota(jnp.int32, (rows, head), 0) + first
        kept = jnp.concatenate([position < length_ref[0]] * stack, axis=0)
        for left in range(0, o_ref.shape[1], stack * head):
            lanes = [slice(left + i * head, left + (i + 1) * head) for i in range(stack)]
            queries = [q_parts[0][pl.ds(offset, rows), lane] for lane in lanes]
            for part in range(1, n_parts):
                here = first >= part * part_rows
                queries = [
                    jnp.where(here, q_parts[part][pl.ds(offset, rows), lane], query)
                    for lane, query in zip(lanes, queries)
                ]
            scores = lax.dot_general(
                jnp.concatenate(queries, axis=0),
                keys_all[...],
                (((1,), (1,)), ((), ())),
                preferred_element_type=jnp.float32,
            )
            own = jnp.where(allowed, scores[:, cross:], -1e30)
            free = scores[:, :cross]
            largest = jnp.maximum(
                jnp.max(free, axis=1, keepdims=True), jnp.max(own, axis=1, keepdims=True)
            )
            free = jnp.exp2((free - largest) * scale)
            own = jnp.exp2((own - largest) * scale)
            total = jnp.sum(free, axis=1, keepdims=True) + jnp.sum(own, axis=1, keepdims=True)
            mixed = jnp.dot(
                free.astype(jnp.bfloat16), values_all[:cross, :], preferred_element_type=jnp.float32
            ) + jnp.dot(
                own.astype(jnp.bfloat16), values_all[cross:, :], preferred_element_type=jnp.float32
            )
            mixed = jnp.where(kept, mixed / total, 0.0).astype(jnp.bfloat16)
            for index, lane in enumerate(lanes):
                o_ref[:, lane] = mixed[index * rows : (index + 1) * rows, :]


def attention(places, slots, rows, lengths, queries, own, others):
    n_parts = len(own)
    part_rows, width = queries[0].shape
    head = own[0].shape[1] // 2
    picks = others[0].shape[0]
    reach = n_parts * part_rows + len(others) * picks
    return pl.pallas_call(
        functools.partial(attention_kernel, slots, n_parts, len(others), 512 // rows),
        grid_spec=pltpu.PrefetchScalarGridSpec(
            num_scalar_prefetch=2,
            grid=(1,),
            in_specs=resident(len(queries) + len(own) + len(others)),
            out_specs=resident(len(slots)),
            scratch_shapes=[
                pltpu.VMEM((reach, head), jnp.bfloat16),
                pltpu.VMEM((reach, head), jnp.bfloat16),
            ],
        ),
        out_shape=[jax.ShapeDtypeStruct((rows, width), jnp.bfloat16) for _ in slots],
        compiler_params=params(24 if reach <= 2048 else 56),
        cost_estimate=cost(1),
        name="attention",
    )(places, lengths, *queries, *own, *others)


def mix_kernel(which, tiles, rows_ref, w_ref, out_ref):
    width = out_ref.shape[1]
    tile = width // tiles
    for start in range(0, width, tile):
        left = which * width + start
        total = jnp.dot(
            rows_ref[...], w_ref[:, left : left + tile], preferred_element_type=jnp.float32
        )
        out_ref[:, start : start + tile] = total.astype(out_ref.dtype)


def mix(attended, w_out, which):
    rows = attended.shape[0]
    width = w_out.shape[1] // 2
    return pl.pallas_call(
        functools.partial(mix_kernel, which, 5),
        in_specs=resident(2),
        out_specs=resident(1)[0],
        out_shape=jax.ShapeDtypeStruct((rows, width), jnp.bfloat16),
        compiler_params=params(8),
        cost_estimate=cost(1),
        name="mix",
    )(attended, w_out)


def eighth_kernel(places_ref, w_ref, out_ref):
    out_ref[...] = w_ref[...]


def eighth(places, which, w_out, share):
    width = w_out.shape[1] // 2
    return pl.pallas_call(
        eighth_kernel,
        grid_spec=pltpu.PrefetchScalarGridSpec(
            num_scalar_prefetch=1,
            grid=(1,),
            in_specs=[pl.BlockSpec((share, width), lambda i, p: (p[EIGHTHS + which], 1))],
            out_specs=whole(share, width),
        ),
        out_shape=jax.ShapeDtypeStruct((share, width), w_out.dtype),
        compiler_params=params(8),
        cost_estimate=cost(1),
        name="eighth",
    )(places, w_out)


def mix_sent_kernel(tiles, places_ref, rows_ref, *refs):
    pieces, out_ref = refs[:-1], refs[-1]
    share = rows_ref.shape[1] // len(OFFSETS)
    rows = []
    for index in range(len(OFFSETS)):
        start = pl.multiple_of(places_ref[EIGHTHS + index] * share, share)
        rows.append(rows_ref[:, pl.ds(start, share)])
    rows = jnp.concatenate(rows, axis=1)
    tile = out_ref.shape[1] // tiles
    for start in range(0, out_ref.shape[1], tile):
        columns = slice(start, start + tile)
        weights = jnp.concatenate([piece[:, columns] for piece in pieces], axis=0)
        total = jnp.dot(rows, weights, preferred_element_type=jnp.float32)
        out_ref[:, columns] = total.astype(out_ref.dtype)


def mix_sent(places, attended, pieces):
    rows = attended.shape[0]
    width = pieces[0].shape[1]
    return pl.pallas_call(
        functools.partial(mix_sent_kernel, 5),
        grid_spec=pltpu.PrefetchScalarGridSpec(
            num_scalar_prefetch=1,
            grid=(1,),
            in_specs=resident(1 + len(pieces)),
            out_specs=resident(1)[0],
        ),
        out_shape=jax.ShapeDtypeStruct((rows, width), jnp.bfloat16),
        compiler_params=params(12),
        cost_estimate=cost(1),
        name="mix_sent",
    )(places, attended, *pieces)


def joined_kernel(*refs):
    start = 0
    for ref in refs[:-1]:
        stop = start + ref.shape[0]
        refs[-1][start:stop, :] = ref[...]
        start = stop


def joined(arrays):
    rows = sum(array.shape[0] for array in arrays)
    return pl.pallas_call(
        joined_kernel,
        in_specs=resident(len(arrays)),
        out_specs=resident(1)[0],
        out_shape=jax.ShapeDtypeStruct((rows, arrays[0].shape[1]), arrays[0].dtype),
        compiler_params=params(8),
        cost_estimate=cost(1),
        name="joined",
    )(*arrays)


def halves_kernel(ref, first_ref, second_ref):
    half = first_ref.shape[0]
    first_ref[...] = ref[:half, :]
    second_ref[...] = ref[half:, :]


def halves(array):
    rows, width = array.shape
    half = jax.ShapeDtypeStruct((rows // 2, width), array.dtype)
    return pl.pallas_call(
        halves_kernel,
        grid=(1,),
        in_specs=[whole(rows, width)],
        out_specs=[whole(rows // 2, width)] * 2,
        out_shape=[half, half],
        compiler_params=params(8),
        cost_estimate=cost(1),
        name="halves",
    )(array)


def add_kernel(count, *refs):
    total = refs[0][...].astype(jnp.float32)
    for ref in refs[1:count]:
        total = total + ref[...].astype(jnp.float32)
    refs[-1][...] = total.astype(jnp.bfloat16)


def added(*arrays, half=None, into=None):
    rows, width = arrays[0].shape
    wide = 1 if half is None else 2
    at = half or 0
    operands = list(arrays)
    in_specs = resident(len(arrays))
    aliases = {}
    if into is not None:
        operands.append(into)
        in_specs.append(pl.BlockSpec(memory_space=pl.ANY))
        aliases = {len(arrays): 0}
    return pl.pallas_call(
        functools.partial(add_kernel, len(arrays)),
        grid=(1,),
        in_specs=in_specs,
        out_specs=pl.BlockSpec((rows, width), lambda i: (0, at)),
        out_shape=jax.ShapeDtypeStruct((rows, wide * width), jnp.bfloat16),
        input_output_aliases=aliases,
        compiler_params=params(8),
        cost_estimate=cost(1),
        name="added",
    )(*operands)


def shards(hidden_in, lengths, summary_pos, w_query, w_key, w_value, w_out, q_gain, k_gain):
    rows_here = hidden_in.shape[0]
    head_width = q_gain.shape[0]
    place = lax.axis_index("tensor")
    n_cand = lax.axis_size("cand")
    assert lax.axis_size("tensor") == 4 and w_key.shape[1] == head_width

    def swap(array):
        return lax.ppermute(array, "tensor", [(0, 1), (1, 0), (2, 3), (3, 2)])

    def across(array):
        return lax.ppermute(array, "tensor", [(1, 2), (2, 1)])

    def outward(array):
        return lax.ppermute(array, "tensor", [(1, 0), (2, 3)])

    def inward(array):
        return lax.ppermute(array, "tensor", [(0, 1), (3, 2)])

    def between(array, offset):
        return lax.ppermute(array, "cand", [(i, i ^ offset) for i in range(n_cand)])

    low = place < 2
    near = jnp.bitwise_xor(place, 1)
    places = [place, near, jnp.where(low, 2, 1), jnp.where(low, 3, 0)]
    places += [jnp.bitwise_xor(lax.axis_index("cand"), offset) for offset in OFFSETS]
    places = jnp.stack(places).astype(jnp.int32)
    share = w_out.shape[0] // n_cand
    spread = n_cand == len(OFFSETS) and share % 128 == 0
    tables = rope_tables(rows_here, head_width)
    k_gain, q_gain = k_gain[None], q_gain[None]
    weights = [w_query, w_key, w_value]
    half = rows_here // 2

    from_near = swap(hidden_in)
    from_mid = [across(array) for array in halves(hidden_in)]
    accs = partial_projection(places, OWN, [[hidden_in]], weights, None)
    from_mid[0], accs = lax.optimization_barrier((from_mid[0], accs))
    to_outer = [outward(from_mid[0])]
    accs = partial_projection(after(places, from_mid[1]), NEAR, [[from_near]], weights, accs)
    from_near = halves(from_near)
    to_outer.append(outward(after(from_mid[1], from_near)))
    to_inner = [across(from_near[0])]
    to_inner.append(across(after(from_near[1], (to_outer[0], accs))))
    end = [outward(array) for array in to_inner]
    pieces = {}
    if spread:
        first, second = (eighth(places, i, w_out, share) for i in (0, 1))
        pieces[0] = inward(after(first, to_outer[0]))
        cue = to_outer[1]
        pieces[6] = inward(after(second, cue))
        first = after(pieces[0], cue)
        pieces[2], pieces[4] = between(first, 2), between(first, 4)
    cue = (to_inner, accs)
    accs = partial_projection(
        after(places, cue), THIRD, [[a, b] for a, b in zip(from_mid, to_outer)], weights, accs
    )

    pieces = [joined([pieces[offset] for offset in OFFSETS[:4]])] if spread else []
    final = [[a, b] for a, b in zip(to_inner, end)]
    (own_first,) = keys_values(places, final[0], 0, weights[1:], accs[1:], k_gain, *tables)
    first_queries = queries_of(places, final[0], 0, w_query, accs[0], q_gain, *tables)
    own_second, summary = keys_values(
        places,
        final[1],
        1,
        weights[1:],
        after(accs[1:], (first_queries, pieces)),
        k_gain,
        *tables,
        [own_first],
        summary_pos,
    )
    own = [own_first, own_second]
    others = [between(summary, offset) for offset in reversed(range(1, n_cand))]
    second_queries = queries_of(places, final[1], 1, w_query, accs[0], q_gain, *tables)
    queries = [first_queries, second_queries]

    if spread:
        pieces.append(between(after(pieces[0], (others, second_queries)), 1))

    def attend(slots):
        return attention(places, slots, rows_here // 4, lengths, queries, own, others)

    def send(rows, part):
        return inward(rows if spread else part)

    def share_of(arrived):
        if not spread:
            return arrived
        return mix_sent(places, arrived, pieces)

    def mixed(rows):
        return [mix(rows, w_out, which) for which in (0, 1)]

    (far_rows,) = attend((LAST,))
    far = mixed(far_rows)
    far_sent = send(far_rows, far[1])
    places = after(places, far)
    (third_rows,) = attend((THIRD,))
    far_in = inward(far[0])
    far_right = added(far[1], share_of(after(far_sent, third_rows)))
    places = after(places, far_right)
    near_rows, own_rows = attend((NEAR, OWN))
    third = mixed(after(third_rows, near_rows))
    third_sent = send(third_rows, third[1])
    far_right = across(far_right)
    far_left = added(far[0], after(far_in, third))
    third_sent = after(third_sent, far_left)
    far_left = across(far_left)
    third_in = inward(after(third[0], (third_sent, far_right)))
    third_right = added(third[1], share_of(third_sent))
    near = [None, mix(after(near_rows, (third_right, far_right)), w_out, 1)]
    near_sent = send(near_rows, near[1])
    third_right = across(third_right)
    out_right = added(near[1], far_right)
    near[0] = mix(after(near_rows, out_right), w_out, 0)
    out_left = added(near[0], far_left)
    third_left = added(third[0], after(third_in, out_left))
    kept = mixed(after(own_rows, third_left))
    near_sent = share_of(after(near_sent, third_left))
    result = added(kept[1], near_sent, outward(out_right), third_right, half=1)
    near_in = inward(after(near[0], third_left))
    out_left, third_left = outward(out_left), across(third_left)
    return added(kept[0], near_in, out_left, third_left, half=0, into=result)


def solution(mesh):
    return jax.shard_map(
        shards,
        mesh=mesh,
        in_specs=(
            P("cand", "tensor"),
            P("cand"),
            P("cand", None),
            P(None, "tensor"),
            P(None, "tensor"),
            P(None, "tensor"),
            P("tensor", None),
            P(),
            P(),
        ),
        out_specs=P(("cand", "tensor"), None),
        check_vma=False,
    )
```

```python
import functools

import jax
import jax.numpy as jnp
import numpy as np
from jax import lax
from jax.experimental import pallas as pl
from jax.experimental.pallas import tpu as pltpu
from jax.sharding import PartitionSpec as P

MIB = 1024 * 1024
LOG2E = 1.4426950408889634
OWN, NEAR, THIRD, LAST, EIGHTHS = range(5)
OFFSETS = (0, 6, 2, 4, 1, 7, 3, 5)


def rope_tables(rows, width):
    half_width = width // 2
    frequency = (1000000.0 ** (-(np.arange(half_width) * 2.0 / width))).astype(np.float32)
    angle = np.arange(rows, dtype=np.float32)[:, None] * frequency[None, :]
    angle = angle.astype(np.float64)
    cosine, sine = np.cos(angle), np.sin(angle)
    return (
        jnp.asarray(np.concatenate([cosine, cosine], axis=1).astype(np.float32)),
        jnp.asarray(np.concatenate([-sine, sine], axis=1).astype(np.float32)),
    )


def norm_rope(vectors, gain, cosine, sine):
    scale = lax.rsqrt(jnp.mean(vectors * vectors, axis=-1, keepdims=True) + 1e-06)
    vectors = vectors * scale * gain
    return vectors * cosine + pltpu.roll(vectors, vectors.shape[-1] // 2, 1) * sine


def params(mebibytes):
    return pltpu.CompilerParams(vmem_limit_bytes=mebibytes * MIB)


def cost(flops):
    return pl.CostEstimate(flops=flops, bytes_accessed=1, transcendentals=0)


def after(array, cue):
    return lax.optimization_barrier((array, cue))[0]


def whole(*shape):
    return pl.BlockSpec(shape, lambda *_: (0,) * len(shape))


def resident(count):
    return [pl.BlockSpec(memory_space=pltpu.VMEM)] * count


def summed(refs):
    total = refs[0][...]
    for ref in refs[1:]:
        total = total + ref[...]
    return total


def partial_kernel(counts, with_acc, places_ref, *refs):
    rows = []
    for count in counts:
        rows.append(summed(refs[:count]))
        refs = refs[count:]
    hidden = jnp.concatenate(rows, axis=0) if len(rows) > 1 else rows[0]
    weights, outs = refs[:3], refs[-3:]
    accs = refs[3:6] if with_acc else (None,) * 3
    step = pl.program_id(0)

    def add(w_ref, acc_ref, out_ref):
        product = jnp.dot(hidden, w_ref[...], preferred_element_type=jnp.float32)
        out_ref[...] = product if acc_ref is None else product + acc_ref[...]

    add(weights[0], accs[0], outs[0])

    @pl.when(step == 0)
    def _():
        add(weights[1], accs[1], outs[1])
        add(weights[2], accs[2], outs[2])


def partial_projection(places, slot, parts, weights, accs):
    features = parts[0][0].shape[1]
    rows = sum(part[0].shape[0] for part in parts)
    arrivals = [array for part in parts for array in part]
    widths = [weight.shape[1] for weight in weights]
    tile = 512
    column = lambda height: pl.BlockSpec((height, tile), lambda i, p: (0, i))
    per_array = lambda height: [column(height), whole(height, widths[1]), whole(height, widths[2])]
    block = lambda width: pl.BlockSpec((features, width), lambda i, p: (p[slot], 0))
    in_specs = [whole(*array.shape) for array in arrivals]
    in_specs.append(pl.BlockSpec((features, tile), lambda i, p: (p[slot], i)))
    in_specs += [block(widths[1]), block(widths[2])]
    operands = [*arrivals, *weights]
    if accs is not None:
        in_specs += per_array(rows)
        operands += accs
    return pl.pallas_call(
        functools.partial(partial_kernel, [len(part) for part in parts], accs is not None),
        grid_spec=pltpu.PrefetchScalarGridSpec(
            num_scalar_prefetch=1,
            grid=(widths[0] // tile,),
            in_specs=in_specs,
            out_specs=per_array(rows),
        ),
        out_shape=[jax.ShapeDtypeStruct((rows, width), jnp.float32) for width in widths],
        compiler_params=params(20),
        cost_estimate=cost(1),
        name="partial_projection",
    )(places, *operands)


def keys_values_kernel(count, n_before, places_ref, *refs):
    before, refs = refs[:n_before], refs[n_before:]
    hidden = summed(refs[:count])
    wk_ref, wv_ref, acck_ref, accv_ref, gain_ref, cos_ref, sin_ref = refs[count : count + 7]
    refs = refs[count + 7 :]
    head = gain_ref.shape[1]
    out_ref = refs[0] if n_before == 0 else refs[1]
    keys = acck_ref[...] + jnp.dot(hidden, wk_ref[...], preferred_element_type=jnp.float32)
    values = accv_ref[...] + jnp.dot(hidden, wv_ref[...], preferred_element_type=jnp.float32)
    keys = norm_rope(keys, gain_ref[...], cos_ref[...], sin_ref[...])
    out_ref[:, :head] = keys.astype(jnp.bfloat16)
    out_ref[:, head:] = values.astype(jnp.bfloat16)
    if n_before:
        pos_ref, summary_ref = refs[0], refs[2]
        picks = pos_ref.shape[1]
        picked, start = None, 0
        for ref in (*before, out_ref):
            rows = ref.shape[0]
            row = lax.broadcasted_iota(jnp.int32, (rows, picks), 0) + start
            chosen = jnp.where(row == pos_ref[...], 1.0, 0.0).astype(jnp.bfloat16)
            found = lax.dot_general(
                chosen, ref[...], (((0,), (0,)), ((), ())), preferred_element_type=jnp.float32
            )
            picked = found if picked is None else picked + found
            start += rows
        summary_ref[...] = picked.astype(jnp.bfloat16)


def keys_values(places, hidden, part, weights, accs, gain, cosine, sine, before=(), positions=None):
    rows, features = hidden[0].shape
    head = gain.shape[1]
    row_part = pl.BlockSpec((rows, head), lambda i, p: (part, 0))
    block = pl.BlockSpec((features, head), lambda i, p: (p[LAST], 0))
    in_specs = [whole(*array.shape) for array in (*before, *hidden)]
    in_specs += [block, block, row_part, row_part, whole(1, head), row_part, row_part]
    operands = [*before, *hidden, *weights, *accs, gain, cosine, sine]
    out_shape = [jax.ShapeDtypeStruct((rows, 2 * head), jnp.bfloat16)]
    if before:
        in_specs.append(whole(*positions.shape))
        operands.append(positions)
        out_shape.append(jax.ShapeDtypeStruct((positions.shape[1], 2 * head), jnp.bfloat16))
    return pl.pallas_call(
        functools.partial(keys_values_kernel, len(hidden), len(before)),
        grid_spec=pltpu.PrefetchScalarGridSpec(
            num_scalar_prefetch=1,
            grid=(1,),
            in_specs=in_specs,
            out_specs=[whole(*shape.shape) for shape in out_shape],
        ),
        out_shape=out_shape,
        compiler_params=params(12),
        cost_estimate=cost(1),
        name="keys_values",
    )(places, *operands)


def queries_kernel(count, places_ref, *refs):
    hidden = summed(refs[:count])
    w_ref, acc_ref, gain_ref, cos_ref, sin_ref, q_ref = refs[count:]
    head = gain_ref.shape[1]
    proj = acc_ref[...] + jnp.dot(hidden, w_ref[...], preferred_element_type=jnp.float32)
    for start in range(0, proj.shape[1], head):
        one = norm_rope(proj[:, start : start + head], gain_ref[...], cos_ref[...], sin_ref[...])
        q_ref[:, start : start + head] = one.astype(jnp.bfloat16)


def queries_of(places, hidden, part, weights, acc, gain, cosine, sine):
    rows, features = hidden[0].shape
    head = gain.shape[1]
    width = weights.shape[1]
    tile = 4 * head
    row_part = pl.BlockSpec((rows, head), lambda i, p: (part, 0))
    return pl.pallas_call(
        functools.partial(queries_kernel, len(hidden)),
        grid_spec=pltpu.PrefetchScalarGridSpec(
            num_scalar_prefetch=1,
            grid=(width // tile,),
            in_specs=[whole(rows, features) for _ in hidden]
            + [
                pl.BlockSpec((features, tile), lambda i, p: (p[LAST], i)),
                pl.BlockSpec((rows, tile), lambda i, p: (part, i)),
                whole(1, head),
                row_part,
                row_part,
            ],
            out_specs=pl.BlockSpec((rows, tile), lambda i, p: (0, i)),
        ),
        out_shape=jax.ShapeDtypeStruct((rows, width), jnp.bfloat16),
        compiler_params=params(12),
        cost_estimate=cost(1),
        name="queries",
    )(places, *hidden, weights, acc, gain, cosine, sine)


def attention_kernel(slots, n_parts, n_others, stack, places_ref, length_ref, *refs):
    q_parts, refs = refs[:n_parts], refs[n_parts:]
    own_parts, refs = refs[:n_parts], refs[n_parts:]
    others, refs = refs[:n_others], refs[n_others:]
    o_refs, (keys_all, values_all) = refs[:-2], refs[-2:]
    part_rows, width = own_parts[0].shape
    head = width // 2
    picks = others[0].shape[0]
    cross = n_others * picks
    rows = o_refs[0].shape[0]

    start = 0
    for ref in (*others, *own_parts):
        stop = start + ref.shape[0]
        keys_all[start:stop, :] = ref[:, :head]
        values_all[start:stop, :] = ref[:, head:]
        start = stop

    scale = head ** (-0.5) * LOG2E
    own_rows = n_parts * part_rows
    for slot, o_ref in zip(slots, o_refs):
        first = places_ref[slot] * rows
        offset = pl.multiple_of(lax.rem(first, part_rows), rows)
        row = lax.broadcasted_iota(jnp.int32, (rows, own_rows), 0) + first
        column = lax.broadcasted_iota(jnp.int32, (rows, own_rows), 1)
        allowed = jnp.concatenate([column <= row] * stack, axis=0)
        position = lax.broadcasted_iota(jnp.int32, (rows, head), 0) + first
        kept = jnp.concatenate([position < length_ref[0]] * stack, axis=0)
        for left in range(0, o_ref.shape[1], stack * head):
            lanes = [slice(left + i * head, left + (i + 1) * head) for i in range(stack)]
            queries = [q_parts[0][pl.ds(offset, rows), lane] for lane in lanes]
            for part in range(1, n_parts):
                here = first >= part * part_rows
                queries = [
                    jnp.where(here, q_parts[part][pl.ds(offset, rows), lane], query)
                    for lane, query in zip(lanes, queries)
                ]
            scores = lax.dot_general(
                jnp.concatenate(queries, axis=0),
                keys_all[...],
                (((1,), (1,)), ((), ())),
                preferred_element_type=jnp.float32,
            )
            own = jnp.where(allowed, scores[:, cross:], -1e30)
            free = scores[:, :cross]
            largest = jnp.maximum(
                jnp.max(free, axis=1, keepdims=True), jnp.max(own, axis=1, keepdims=True)
            )
            free = jnp.exp2((free - largest) * scale)
            own = jnp.exp2((own - largest) * scale)
            total = jnp.sum(free, axis=1, keepdims=True) + jnp.sum(own, axis=1, keepdims=True)
            mixed = jnp.dot(
                free.astype(jnp.bfloat16), values_all[:cross, :], preferred_element_type=jnp.float32
            ) + jnp.dot(
                own.astype(jnp.bfloat16), values_all[cross:, :], preferred_element_type=jnp.float32
            )
            mixed = jnp.where(kept, mixed / total, 0.0).astype(jnp.bfloat16)
            for index, lane in enumerate(lanes):
                o_ref[:, lane] = mixed[index * rows : (index + 1) * rows, :]


def attention(places, slots, rows, lengths, queries, own, others):
    n_parts = len(own)
    part_rows, width = queries[0].shape
    head = own[0].shape[1] // 2
    picks = others[0].shape[0]
    reach = n_parts * part_rows + len(others) * picks
    return pl.pallas_call(
        functools.partial(attention_kernel, slots, n_parts, len(others), 512 // rows),
        grid_spec=pltpu.PrefetchScalarGridSpec(
            num_scalar_prefetch=2,
            grid=(1,),
            in_specs=resident(len(queries) + len(own) + len(others)),
            out_specs=resident(len(slots)),
            scratch_shapes=[
                pltpu.VMEM((reach, head), jnp.bfloat16),
                pltpu.VMEM((reach, head), jnp.bfloat16),
            ],
        ),
        out_shape=[jax.ShapeDtypeStruct((rows, width), jnp.bfloat16) for _ in slots],
        compiler_params=params(24 if reach <= 2048 else 56),
        cost_estimate=cost(1),
        name="attention",
    )(places, lengths, *queries, *own, *others)


def mix_kernel(which, tiles, rows_ref, w_ref, out_ref):
    width = out_ref.shape[1]
    tile = width // tiles
    for start in range(0, width, tile):
        left = which * width + start
        total = jnp.dot(
            rows_ref[...], w_ref[:, left : left + tile], preferred_element_type=jnp.float32
        )
        out_ref[:, start : start + tile] = total.astype(out_ref.dtype)


def mix(attended, w_out, which):
    rows = attended.shape[0]
    width = w_out.shape[1] // 2
    return pl.pallas_call(
        functools.partial(mix_kernel, which, 5),
        in_specs=resident(2),
        out_specs=resident(1)[0],
        out_shape=jax.ShapeDtypeStruct((rows, width), jnp.bfloat16),
        compiler_params=params(8),
        cost_estimate=cost(1),
        name="mix",
    )(attended, w_out)


def eighth_kernel(places_ref, w_ref, out_ref):
    out_ref[...] = w_ref[...]


def eighth(places, which, w_out, share):
    width = w_out.shape[1] // 2
    return pl.pallas_call(
        eighth_kernel,
        grid_spec=pltpu.PrefetchScalarGridSpec(
            num_scalar_prefetch=1,
            grid=(1,),
            in_specs=[pl.BlockSpec((share, width), lambda i, p: (p[EIGHTHS + which], 1))],
            out_specs=whole(share, width),
        ),
        out_shape=jax.ShapeDtypeStruct((share, width), w_out.dtype),
        compiler_params=params(8),
        cost_estimate=cost(1),
        name="eighth",
    )(places, w_out)


def mix_sent_kernel(tiles, places_ref, rows_ref, *refs):
    pieces, out_ref = refs[:-1], refs[-1]
    share = rows_ref.shape[1] // len(OFFSETS)
    rows = []
    for index in range(len(OFFSETS)):
        start = pl.multiple_of(places_ref[EIGHTHS + index] * share, share)
        rows.append(rows_ref[:, pl.ds(start, share)])
    rows = jnp.concatenate(rows, axis=1)
    tile = out_ref.shape[1] // tiles
    for start in range(0, out_ref.shape[1], tile):
        columns = slice(start, start + tile)
        weights = jnp.concatenate([piece[:, columns] for piece in pieces], axis=0)
        total = jnp.dot(rows, weights, preferred_element_type=jnp.float32)
        out_ref[:, columns] = total.astype(out_ref.dtype)


def mix_sent(places, attended, pieces):
    rows = attended.shape[0]
    width = pieces[0].shape[1]
    return pl.pallas_call(
        functools.partial(mix_sent_kernel, 5),
        grid_spec=pltpu.PrefetchScalarGridSpec(
            num_scalar_prefetch=1,
            grid=(1,),
            in_specs=resident(1 + len(pieces)),
            out_specs=resident(1)[0],
        ),
        out_shape=jax.ShapeDtypeStruct((rows, width), jnp.bfloat16),
        compiler_params=params(12),
        cost_estimate=cost(1),
        name="mix_sent",
    )(places, attended, *pieces)


def joined_kernel(*refs):
    start = 0
    for ref in refs[:-1]:
        stop = start + ref.shape[0]
        refs[-1][start:stop, :] = ref[...]
        start = stop


def joined(arrays):
    rows = sum(array.shape[0] for array in arrays)
    return pl.pallas_call(
        joined_kernel,
        in_specs=resident(len(arrays)),
        out_specs=resident(1)[0],
        out_shape=jax.ShapeDtypeStruct((rows, arrays[0].shape[1]), arrays[0].dtype),
        compiler_params=params(8),
        cost_estimate=cost(1),
        name="joined",
    )(*arrays)


def halves_kernel(ref, first_ref, second_ref):
    half = first_ref.shape[0]
    first_ref[...] = ref[:half, :]
    second_ref[...] = ref[half:, :]


def halves(array):
    rows, width = array.shape
    half = jax.ShapeDtypeStruct((rows // 2, width), array.dtype)
    return pl.pallas_call(
        halves_kernel,
        grid=(1,),
        in_specs=[whole(rows, width)],
        out_specs=[whole(rows // 2, width)] * 2,
        out_shape=[half, half],
        compiler_params=params(8),
        cost_estimate=cost(1),
        name="halves",
    )(array)


def add_kernel(count, *refs):
    total = refs[0][...].astype(jnp.float32)
    for ref in refs[1:count]:
        total = total + ref[...].astype(jnp.float32)
    refs[-1][...] = total.astype(jnp.bfloat16)


def added(*arrays, half=None, into=None):
    rows, width = arrays[0].shape
    wide = 1 if half is None else 2
    at = half or 0
    operands = list(arrays)
    in_specs = resident(len(arrays))
    aliases = {}
    if into is not None:
        operands.append(into)
        in_specs.append(pl.BlockSpec(memory_space=pl.ANY))
        aliases = {len(arrays): 0}
    return pl.pallas_call(
        functools.partial(add_kernel, len(arrays)),
        grid=(1,),
        in_specs=in_specs,
        out_specs=pl.BlockSpec((rows, width), lambda i: (0, at)),
        out_shape=jax.ShapeDtypeStruct((rows, wide * width), jnp.bfloat16),
        input_output_aliases=aliases,
        compiler_params=params(8),
        cost_estimate=cost(1),
        name="added",
    )(*operands)


def shards(hidden_in, lengths, summary_pos, w_query, w_key, w_value, w_out, q_gain, k_gain):
    rows_here = hidden_in.shape[0]
    head_width = q_gain.shape[0]
    place = lax.axis_index("tensor")
    n_cand = lax.axis_size("cand")
    assert lax.axis_size("tensor") == 4 and w_key.shape[1] == head_width

    def swap(array):
        return lax.ppermute(array, "tensor", [(0, 1), (1, 0), (2, 3), (3, 2)])

    def across(array):
        return lax.ppermute(array, "tensor", [(1, 2), (2, 1)])

    def outward(array):
        return lax.ppermute(array, "tensor", [(1, 0), (2, 3)])

    def inward(array):
        return lax.ppermute(array, "tensor", [(0, 1), (3, 2)])

    def between(array, offset):
        return lax.ppermute(array, "cand", [(i, i ^ offset) for i in range(n_cand)])

    low = place < 2
    near = jnp.bitwise_xor(place, 1)
    places = [place, near, jnp.where(low, 2, 1), jnp.where(low, 3, 0)]
    places += [jnp.bitwise_xor(lax.axis_index("cand"), offset) for offset in OFFSETS]
    places = jnp.stack(places).astype(jnp.int32)
    share = w_out.shape[0] // n_cand
    spread = n_cand == len(OFFSETS) and share % 128 == 0
    tables = rope_tables(rows_here, head_width)
    k_gain, q_gain = k_gain[None], q_gain[None]
    weights = [w_query, w_key, w_value]
    half = rows_here // 2

    from_near = swap(hidden_in)
    from_mid = [across(array) for array in halves(hidden_in)]
    accs = partial_projection(places, OWN, [[hidden_in]], weights, None)
    from_mid[0], accs = lax.optimization_barrier((from_mid[0], accs))
    to_outer = [outward(from_mid[0])]
    accs = partial_projection(after(places, from_mid[1]), NEAR, [[from_near]], weights, accs)
    from_near = halves(from_near)
    to_outer.append(outward(after(from_mid[1], from_near)))
    to_inner = [across(from_near[0])]
    to_inner.append(across(after(from_near[1], (to_outer[0], accs))))
    end = [outward(array) for array in to_inner]
    pieces = {}
    if spread:
        first, second = (eighth(places, i, w_out, share) for i in (0, 1))
        pieces[0] = inward(after(first, to_outer[0]))
        cue = to_outer[1]
        pieces[6] = inward(after(second, cue))
        first = after(pieces[0], cue)
        pieces[2], pieces[4] = between(first, 2), between(first, 4)
    cue = (to_inner, accs)
    accs = partial_projection(
        after(places, cue), THIRD, [[a, b] for a, b in zip(from_mid, to_outer)], weights, accs
    )

    pieces = [joined([pieces[offset] for offset in OFFSETS[:4]])] if spread else []
    final = [[a, b] for a, b in zip(to_inner, end)]
    (own_first,) = keys_values(places, final[0], 0, weights[1:], accs[1:], k_gain, *tables)
    first_queries = queries_of(places, final[0], 0, w_query, accs[0], q_gain, *tables)
    own_second, summary = keys_values(
        places,
        final[1],
        1,
        weights[1:],
        after(accs[1:], (first_queries, pieces)),
        k_gain,
        *tables,
        [own_first],
        summary_pos,
    )
    own = [own_first, own_second]
    others = [between(summary, offset) for offset in reversed(range(1, n_cand))]
    second_queries = queries_of(places, final[1], 1, w_query, accs[0], q_gain, *tables)
    queries = [first_queries, second_queries]

    if spread:
        pieces.append(between(after(pieces[0], (others, second_queries)), 1))

    def attend(slots):
        return attention(places, slots, rows_here // 4, lengths, queries, own, others)

    def send(rows, part):
        return inward(rows if spread else part)

    def share_of(arrived):
        if not spread:
            return arrived
        return mix_sent(places, arrived, pieces)

    def mixed(rows):
        return [mix(rows, w_out, which) for which in (0, 1)]

    (far_rows,) = attend((LAST,))
    far = mixed(far_rows)
    far_sent = send(far_rows, far[1])
    places = after(places, far)
    (third_rows,) = attend((THIRD,))
    far_in = inward(far[0])
    far_right = added(far[1], share_of(after(far_sent, third_rows)))
    places = after(places, far_right)
    near_rows, own_rows = attend((NEAR, OWN))
    third = mixed(after(third_rows, near_rows))
    third_sent = send(third_rows, third[1])
    far_right = across(far_right)
    far_left = added(far[0], after(far_in, third))
    third_sent = after(third_sent, far_left)
    far_left = across(far_left)
    near_sent = inward(near_rows) if spread else ()
    third_in = inward(after(third[0], (third_sent, far_right, near_sent)))
    third_right = added(third[1], share_of(third_sent))
    near = [None, mix(after(near_rows, (third_right, far_right)), w_out, 1)]
    third_right = across(third_right)
    out_right = added(near[1], far_right)
    near[0] = mix(after(near_rows, out_right), w_out, 0)
    out_left = added(near[0], far_left)
    third_left = added(third[0], after(third_in, out_left))
    kept = mixed(after(own_rows, third_left))
    near_share = share_of(after(near_sent, third_left)) if spread else inward(near[1])
    result = added(kept[1], near_share, outward(out_right), third_right, half=1)
    near_in = inward(after(near[0], third_left))
    out_left, third_left = outward(out_left), across(third_left)
    return added(kept[0], near_in, out_left, third_left, half=0, into=result)


def solution(mesh):
    return jax.shard_map(
        shards,
        mesh=mesh,
        in_specs=(
            P("cand", "tensor"),
            P("cand"),
            P("cand", None),
            P(None, "tensor"),
            P(None, "tensor"),
            P(None, "tensor"),
            P("tensor", None),
            P(),
            P(),
        ),
        out_specs=P(("cand", "tensor"), None),
        check_vma=False,
    )
```

```python
import functools

import jax
import jax.numpy as jnp
import numpy as np
from jax import lax
from jax.experimental import pallas as pl
from jax.experimental.pallas import tpu as pltpu
from jax.sharding import PartitionSpec as P

MIB = 1024 * 1024
LOG2E = 1.4426950408889634
OWN, NEAR, THIRD, LAST, EIGHTHS = range(5)
OFFSETS = (0, 6, 2, 4, 1, 7, 3, 5)


def rope_tables(rows, width):
    half_width = width // 2
    frequency = (1000000.0 ** (-(np.arange(half_width) * 2.0 / width))).astype(np.float32)
    angle = np.arange(rows, dtype=np.float32)[:, None] * frequency[None, :]
    angle = angle.astype(np.float64)
    cosine, sine = np.cos(angle), np.sin(angle)
    return (
        jnp.asarray(np.concatenate([cosine, cosine], axis=1).astype(np.float32)),
        jnp.asarray(np.concatenate([-sine, sine], axis=1).astype(np.float32)),
    )


def norm_rope(vectors, gain, cosine, sine):
    scale = lax.rsqrt(jnp.mean(vectors * vectors, axis=-1, keepdims=True) + 1e-06)
    vectors = vectors * scale * gain
    return vectors * cosine + pltpu.roll(vectors, vectors.shape[-1] // 2, 1) * sine


def params(mebibytes):
    return pltpu.CompilerParams(vmem_limit_bytes=mebibytes * MIB)


def cost(flops):
    return pl.CostEstimate(flops=flops, bytes_accessed=1, transcendentals=0)


def after(array, cue):
    return lax.optimization_barrier((array, cue))[0]


def whole(*shape):
    return pl.BlockSpec(shape, lambda *_: (0,) * len(shape))


def resident(count):
    return [pl.BlockSpec(memory_space=pltpu.VMEM)] * count


def summed(refs):
    total = refs[0][...]
    for ref in refs[1:]:
        total = total + ref[...]
    return total


def partial_kernel(counts, with_acc, places_ref, *refs):
    rows = []
    for count in counts:
        rows.append(summed(refs[:count]))
        refs = refs[count:]
    hidden = jnp.concatenate(rows, axis=0) if len(rows) > 1 else rows[0]
    weights, outs = refs[:3], refs[-3:]
    accs = refs[3:6] if with_acc else (None,) * 3
    step = pl.program_id(0)

    def add(w_ref, acc_ref, out_ref):
        product = jnp.dot(hidden, w_ref[...], preferred_element_type=jnp.float32)
        out_ref[...] = product if acc_ref is None else product + acc_ref[...]

    add(weights[0], accs[0], outs[0])

    @pl.when(step == 0)
    def _():
        add(weights[1], accs[1], outs[1])
        add(weights[2], accs[2], outs[2])


def partial_projection(places, slot, parts, weights, accs):
    features = parts[0][0].shape[1]
    rows = sum(part[0].shape[0] for part in parts)
    arrivals = [array for part in parts for array in part]
    widths = [weight.shape[1] for weight in weights]
    tile = 512
    column = lambda height: pl.BlockSpec((height, tile), lambda i, p: (0, i))
    per_array = lambda height: [column(height), whole(height, widths[1]), whole(height, widths[2])]
    block = lambda width: pl.BlockSpec((features, width), lambda i, p: (p[slot], 0))
    in_specs = [whole(*array.shape) for array in arrivals]
    in_specs.append(pl.BlockSpec((features, tile), lambda i, p: (p[slot], i)))
    in_specs += [block(widths[1]), block(widths[2])]
    operands = [*arrivals, *weights]
    if accs is not None:
        in_specs += per_array(rows)
        operands += accs
    return pl.pallas_call(
        functools.partial(partial_kernel, [len(part) for part in parts], accs is not None),
        grid_spec=pltpu.PrefetchScalarGridSpec(
            num_scalar_prefetch=1,
            grid=(widths[0] // tile,),
            in_specs=in_specs,
            out_specs=per_array(rows),
        ),
        out_shape=[jax.ShapeDtypeStruct((rows, width), jnp.float32) for width in widths],
        compiler_params=params(20),
        cost_estimate=cost(1),
        name="partial_projection",
    )(places, *operands)


def keys_values_kernel(count, n_before, places_ref, *refs):
    before, refs = refs[:n_before], refs[n_before:]
    hidden = summed(refs[:count])
    wk_ref, wv_ref, acck_ref, accv_ref, gain_ref, cos_ref, sin_ref = refs[count : count + 7]
    refs = refs[count + 7 :]
    head = gain_ref.shape[1]
    out_ref = refs[0] if n_before == 0 else refs[1]
    keys = acck_ref[...] + jnp.dot(hidden, wk_ref[...], preferred_element_type=jnp.float32)
    values = accv_ref[...] + jnp.dot(hidden, wv_ref[...], preferred_element_type=jnp.float32)
    keys = norm_rope(keys, gain_ref[...], cos_ref[...], sin_ref[...])
    out_ref[:, :head] = keys.astype(jnp.bfloat16)
    out_ref[:, head:] = values.astype(jnp.bfloat16)
    if n_before:
        pos_ref, summary_ref = refs[0], refs[2]
        picks = pos_ref.shape[1]
        picked, start = None, 0
        for ref in (*before, out_ref):
            rows = ref.shape[0]
            row = lax.broadcasted_iota(jnp.int32, (rows, picks), 0) + start
            chosen = jnp.where(row == pos_ref[...], 1.0, 0.0).astype(jnp.bfloat16)
            found = lax.dot_general(
                chosen, ref[...], (((0,), (0,)), ((), ())), preferred_element_type=jnp.float32
            )
            picked = found if picked is None else picked + found
            start += rows
        summary_ref[...] = picked.astype(jnp.bfloat16)


def keys_values(places, hidden, part, weights, accs, gain, cosine, sine, before=(), positions=None):
    rows, features = hidden[0].shape
    head = gain.shape[1]
    row_part = pl.BlockSpec((rows, head), lambda i, p: (part, 0))
    block = pl.BlockSpec((features, head), lambda i, p: (p[LAST], 0))
    in_specs = [whole(*array.shape) for array in (*before, *hidden)]
    in_specs += [block, block, row_part, row_part, whole(1, head), row_part, row_part]
    operands = [*before, *hidden, *weights, *accs, gain, cosine, sine]
    out_shape = [jax.ShapeDtypeStruct((rows, 2 * head), jnp.bfloat16)]
    if before:
        in_specs.append(whole(*positions.shape))
        operands.append(positions)
        out_shape.append(jax.ShapeDtypeStruct((positions.shape[1], 2 * head), jnp.bfloat16))
    return pl.pallas_call(
        functools.partial(keys_values_kernel, len(hidden), len(before)),
        grid_spec=pltpu.PrefetchScalarGridSpec(
            num_scalar_prefetch=1,
            grid=(1,),
            in_specs=in_specs,
            out_specs=[whole(*shape.shape) for shape in out_shape],
        ),
        out_shape=out_shape,
        compiler_params=params(12),
        cost_estimate=cost(1),
        name="keys_values",
    )(places, *operands)


def queries_kernel(count, places_ref, *refs):
    hidden = summed(refs[:count])
    w_ref, acc_ref, gain_ref, cos_ref, sin_ref, q_ref = refs[count:]
    head = gain_ref.shape[1]
    proj = acc_ref[...] + jnp.dot(hidden, w_ref[...], preferred_element_type=jnp.float32)
    for start in range(0, proj.shape[1], head):
        one = norm_rope(proj[:, start : start + head], gain_ref[...], cos_ref[...], sin_ref[...])
        q_ref[:, start : start + head] = one.astype(jnp.bfloat16)


def queries_of(places, hidden, part, weights, acc, gain, cosine, sine):
    rows, features = hidden[0].shape
    head = gain.shape[1]
    width = weights.shape[1]
    tile = 4 * head
    row_part = pl.BlockSpec((rows, head), lambda i, p: (part, 0))
    return pl.pallas_call(
        functools.partial(queries_kernel, len(hidden)),
        grid_spec=pltpu.PrefetchScalarGridSpec(
            num_scalar_prefetch=1,
            grid=(width // tile,),
            in_specs=[whole(rows, features) for _ in hidden]
            + [
                pl.BlockSpec((features, tile), lambda i, p: (p[LAST], i)),
                pl.BlockSpec((rows, tile), lambda i, p: (part, i)),
                whole(1, head),
                row_part,
                row_part,
            ],
            out_specs=pl.BlockSpec((rows, tile), lambda i, p: (0, i)),
        ),
        out_shape=jax.ShapeDtypeStruct((rows, width), jnp.bfloat16),
        compiler_params=params(12),
        cost_estimate=cost(1),
        name="queries",
    )(places, *hidden, weights, acc, gain, cosine, sine)


def attention_kernel(slots, n_parts, n_others, stack, places_ref, length_ref, *refs):
    q_parts, refs = refs[:n_parts], refs[n_parts:]
    own_parts, refs = refs[:n_parts], refs[n_parts:]
    others, refs = refs[:n_others], refs[n_others:]
    o_refs, (keys_all, values_all) = refs[:-2], refs[-2:]
    part_rows, width = own_parts[0].shape
    head = width // 2
    picks = others[0].shape[0]
    cross = n_others * picks
    rows = o_refs[0].shape[0]

    start = 0
    for ref in (*others, *own_parts):
        stop = start + ref.shape[0]
        keys_all[start:stop, :] = ref[:, :head]
        values_all[start:stop, :] = ref[:, head:]
        start = stop

    scale = head ** (-0.5) * LOG2E
    own_rows = n_parts * part_rows
    for slot, o_ref in zip(slots, o_refs):
        first = places_ref[slot] * rows
        offset = pl.multiple_of(lax.rem(first, part_rows), rows)
        row = lax.broadcasted_iota(jnp.int32, (rows, own_rows), 0) + first
        column = lax.broadcasted_iota(jnp.int32, (rows, own_rows), 1)
        allowed = jnp.concatenate([column <= row] * stack, axis=0)
        position = lax.broadcasted_iota(jnp.int32, (rows, head), 0) + first
        kept = jnp.concatenate([position < length_ref[0]] * stack, axis=0)
        for left in range(0, o_ref.shape[1], stack * head):
            lanes = [slice(left + i * head, left + (i + 1) * head) for i in range(stack)]
            queries = [q_parts[0][pl.ds(offset, rows), lane] for lane in lanes]
            for part in range(1, n_parts):
                here = first >= part * part_rows
                queries = [
                    jnp.where(here, q_parts[part][pl.ds(offset, rows), lane], query)
                    for lane, query in zip(lanes, queries)
                ]
            scores = lax.dot_general(
                jnp.concatenate(queries, axis=0),
                keys_all[...],
                (((1,), (1,)), ((), ())),
                preferred_element_type=jnp.float32,
            )
            own = jnp.where(allowed, scores[:, cross:], -1e30)
            free = scores[:, :cross]
            largest = jnp.maximum(
                jnp.max(free, axis=1, keepdims=True), jnp.max(own, axis=1, keepdims=True)
            )
            free = jnp.exp2((free - largest) * scale)
            own = jnp.exp2((own - largest) * scale)
            total = jnp.sum(free, axis=1, keepdims=True) + jnp.sum(own, axis=1, keepdims=True)
            mixed = jnp.dot(
                free.astype(jnp.bfloat16), values_all[:cross, :], preferred_element_type=jnp.float32
            ) + jnp.dot(
                own.astype(jnp.bfloat16), values_all[cross:, :], preferred_element_type=jnp.float32
            )
            mixed = jnp.where(kept, mixed / total, 0.0).astype(jnp.bfloat16)
            for index, lane in enumerate(lanes):
                o_ref[:, lane] = mixed[index * rows : (index + 1) * rows, :]


def attention(places, slots, rows, lengths, queries, own, others):
    n_parts = len(own)
    part_rows, width = queries[0].shape
    head = own[0].shape[1] // 2
    picks = others[0].shape[0]
    reach = n_parts * part_rows + len(others) * picks
    return pl.pallas_call(
        functools.partial(attention_kernel, slots, n_parts, len(others), 512 // rows),
        grid_spec=pltpu.PrefetchScalarGridSpec(
            num_scalar_prefetch=2,
            grid=(1,),
            in_specs=resident(len(queries) + len(own) + len(others)),
            out_specs=resident(len(slots)),
            scratch_shapes=[
                pltpu.VMEM((reach, head), jnp.bfloat16),
                pltpu.VMEM((reach, head), jnp.bfloat16),
            ],
        ),
        out_shape=[jax.ShapeDtypeStruct((rows, width), jnp.bfloat16) for _ in slots],
        compiler_params=params(24 if reach <= 2048 else 56),
        cost_estimate=cost(1),
        name="attention",
    )(places, lengths, *queries, *own, *others)


def mix_kernel(which, tiles, rows_ref, w_ref, out_ref):
    width = out_ref.shape[1]
    tile = width // tiles
    for start in range(0, width, tile):
        left = which * width + start
        total = jnp.dot(
            rows_ref[...], w_ref[:, left : left + tile], preferred_element_type=jnp.float32
        )
        out_ref[:, start : start + tile] = total.astype(out_ref.dtype)


def mix(attended, w_out, which):
    rows = attended.shape[0]
    width = w_out.shape[1] // 2
    return pl.pallas_call(
        functools.partial(mix_kernel, which, 5),
        in_specs=resident(2),
        out_specs=resident(1)[0],
        out_shape=jax.ShapeDtypeStruct((rows, width), jnp.bfloat16),
        compiler_params=params(8),
        cost_estimate=cost(1),
        name="mix",
    )(attended, w_out)


def eighth_kernel(places_ref, w_ref, out_ref):
    out_ref[...] = w_ref[...]


def eighth(places, which, w_out, share):
    width = w_out.shape[1] // 2
    return pl.pallas_call(
        eighth_kernel,
        grid_spec=pltpu.PrefetchScalarGridSpec(
            num_scalar_prefetch=1,
            grid=(1,),
            in_specs=[pl.BlockSpec((share, width), lambda i, p: (p[EIGHTHS + which], 1))],
            out_specs=whole(share, width),
        ),
        out_shape=jax.ShapeDtypeStruct((share, width), w_out.dtype),
        compiler_params=params(8),
        cost_estimate=cost(1),
        name="eighth",
    )(places, w_out)


def mix_sent_kernel(tiles, places_ref, rows_ref, *refs):
    pieces, out_ref = refs[:-1], refs[-1]
    share = rows_ref.shape[1] // len(OFFSETS)
    rows = []
    for index in range(len(OFFSETS)):
        start = pl.multiple_of(places_ref[EIGHTHS + index] * share, share)
        rows.append(rows_ref[:, pl.ds(start, share)])
    rows = jnp.concatenate(rows, axis=1)
    tile = out_ref.shape[1] // tiles
    for start in range(0, out_ref.shape[1], tile):
        columns = slice(start, start + tile)
        weights = jnp.concatenate([piece[:, columns] for piece in pieces], axis=0)
        total = jnp.dot(rows, weights, preferred_element_type=jnp.float32)
        out_ref[:, columns] = total.astype(out_ref.dtype)


def mix_sent(places, attended, pieces):
    rows = attended.shape[0]
    width = pieces[0].shape[1]
    return pl.pallas_call(
        functools.partial(mix_sent_kernel, 5),
        grid_spec=pltpu.PrefetchScalarGridSpec(
            num_scalar_prefetch=1,
            grid=(1,),
            in_specs=resident(1 + len(pieces)),
            out_specs=resident(1)[0],
        ),
        out_shape=jax.ShapeDtypeStruct((rows, width), jnp.bfloat16),
        compiler_params=params(12),
        cost_estimate=cost(1),
        name="mix_sent",
    )(places, attended, *pieces)


def joined_kernel(*refs):
    start = 0
    for ref in refs[:-1]:
        stop = start + ref.shape[0]
        refs[-1][start:stop, :] = ref[...]
        start = stop


def joined(arrays):
    rows = sum(array.shape[0] for array in arrays)
    return pl.pallas_call(
        joined_kernel,
        in_specs=resident(len(arrays)),
        out_specs=resident(1)[0],
        out_shape=jax.ShapeDtypeStruct((rows, arrays[0].shape[1]), arrays[0].dtype),
        compiler_params=params(8),
        cost_estimate=cost(1),
        name="joined",
    )(*arrays)


def halves_kernel(ref, first_ref, second_ref):
    half = first_ref.shape[0]
    first_ref[...] = ref[:half, :]
    second_ref[...] = ref[half:, :]


def halves(array):
    rows, width = array.shape
    half = jax.ShapeDtypeStruct((rows // 2, width), array.dtype)
    return pl.pallas_call(
        halves_kernel,
        grid=(1,),
        in_specs=[whole(rows, width)],
        out_specs=[whole(rows // 2, width)] * 2,
        out_shape=[half, half],
        compiler_params=params(8),
        cost_estimate=cost(1),
        name="halves",
    )(array)


def add_kernel(count, *refs):
    total = refs[0][...].astype(jnp.float32)
    for ref in refs[1:count]:
        total = total + ref[...].astype(jnp.float32)
    refs[-1][...] = total.astype(jnp.bfloat16)


def added(*arrays, half=None, into=None):
    rows, width = arrays[0].shape
    wide = 1 if half is None else 2
    at = half or 0
    operands = list(arrays)
    in_specs = resident(len(arrays))
    aliases = {}
    if into is not None:
        operands.append(into)
        in_specs.append(pl.BlockSpec(memory_space=pl.ANY))
        aliases = {len(arrays): 0}
    return pl.pallas_call(
        functools.partial(add_kernel, len(arrays)),
        grid=(1,),
        in_specs=in_specs,
        out_specs=pl.BlockSpec((rows, width), lambda i: (0, at)),
        out_shape=jax.ShapeDtypeStruct((rows, wide * width), jnp.bfloat16),
        input_output_aliases=aliases,
        compiler_params=params(8),
        cost_estimate=cost(1),
        name="added",
    )(*operands)


def shards(hidden_in, lengths, summary_pos, w_query, w_key, w_value, w_out, q_gain, k_gain):
    rows_here = hidden_in.shape[0]
    head_width = q_gain.shape[0]
    place = lax.axis_index("tensor")
    n_cand = lax.axis_size("cand")
    assert lax.axis_size("tensor") == 4 and w_key.shape[1] == head_width

    def swap(array):
        return lax.ppermute(array, "tensor", [(0, 1), (1, 0), (2, 3), (3, 2)])

    def across(array):
        return lax.ppermute(array, "tensor", [(1, 2), (2, 1)])

    def outward(array):
        return lax.ppermute(array, "tensor", [(1, 0), (2, 3)])

    def inward(array):
        return lax.ppermute(array, "tensor", [(0, 1), (3, 2)])

    def between(array, offset):
        return lax.ppermute(array, "cand", [(i, i ^ offset) for i in range(n_cand)])

    low = place < 2
    near = jnp.bitwise_xor(place, 1)
    places = [place, near, jnp.where(low, 2, 1), jnp.where(low, 3, 0)]
    places += [jnp.bitwise_xor(lax.axis_index("cand"), offset) for offset in OFFSETS]
    places = jnp.stack(places).astype(jnp.int32)
    share = w_out.shape[0] // n_cand
    spread = n_cand == len(OFFSETS) and share % 128 == 0
    tables = rope_tables(rows_here, head_width)
    k_gain, q_gain = k_gain[None], q_gain[None]
    weights = [w_query, w_key, w_value]
    half = rows_here // 2

    from_near = swap(hidden_in)
    from_mid = [across(array) for array in halves(hidden_in)]
    accs = partial_projection(places, OWN, [[hidden_in]], weights, None)
    from_mid[0], accs = lax.optimization_barrier((from_mid[0], accs))
    to_outer = [outward(from_mid[0])]
    accs = partial_projection(after(places, from_mid[1]), NEAR, [[from_near]], weights, accs)
    from_near = halves(from_near)
    to_outer.append(outward(after(from_mid[1], from_near)))
    to_inner = [across(from_near[0])]
    to_inner.append(across(after(from_near[1], (to_outer[0], accs))))
    end = [outward(array) for array in to_inner]
    pieces = {}
    if spread:
        first, second = (eighth(places, i, w_out, share) for i in (0, 1))
        pieces[0] = inward(after(first, to_outer[0]))
        cue = to_outer[1]
        pieces[6] = inward(after(second, cue))
        first = after(pieces[0], cue)
        pieces[2], pieces[4] = between(first, 2), between(first, 4)
    cue = (to_inner, accs)
    accs = partial_projection(
        after(places, cue), THIRD, [[a, b] for a, b in zip(from_mid, to_outer)], weights, accs
    )

    pieces = [joined([pieces[offset] for offset in OFFSETS[:4]])] if spread else []
    final = [[a, b] for a, b in zip(to_inner, end)]
    (own_first,) = keys_values(places, final[0], 0, weights[1:], accs[1:], k_gain, *tables)
    first_queries = queries_of(places, final[0], 0, w_query, accs[0], q_gain, *tables)
    own_second, summary = keys_values(
        places,
        final[1],
        1,
        weights[1:],
        after(accs[1:], (first_queries, pieces)),
        k_gain,
        *tables,
        [own_first],
        summary_pos,
    )
    own = [own_first, own_second]
    others = [between(summary, offset) for offset in reversed(range(1, n_cand))]
    second_queries = queries_of(places, final[1], 1, w_query, accs[0], q_gain, *tables)
    queries = [first_queries, second_queries]

    if spread:
        pieces.append(between(after(pieces[0], (others, second_queries)), 1))

    def attend(slots):
        return attention(places, slots, rows_here // 4, lengths, queries, own, others)

    def send(rows, part):
        return inward(rows if spread else part)

    def share_of(arrived):
        if not spread:
            return arrived
        return mix_sent(places, arrived, pieces)

    def mixed(rows):
        return [mix(rows, w_out, which) for which in (0, 1)]

    (far_rows,) = attend((LAST,))
    far = mixed(far_rows)
    far_sent = send(far_rows, far[1])
    places = after(places, far)
    (third_rows,) = attend((THIRD,))
    far_in = inward(far[0])
    far_right = added(far[1], share_of(after(far_sent, third_rows)))
    places = after(places, far_right)
    near_rows, own_rows = attend((NEAR, OWN))
    third = mixed(after(third_rows, near_rows))
    third_sent = send(third_rows, third[1])
    far_right = across(far_right)
    far_left = added(far[0], after(far_in, third))
    third_sent = after(third_sent, far_left)
    far_left = across(far_left)
    third_in = inward(after(third[0], (third_sent, far_right)))
    third_right = added(third[1], share_of(third_sent))
    near = [None, mix(after(near_rows, (third_right, far_right)), w_out, 1)]
    near_sent = send(near_rows, near[1])
    third_right = across(third_right)
    out_right = added(near[1], far_right)
    near[0] = mix(after(near_rows, out_right), w_out, 0)
    out_left = added(near[0], far_left)
    third_left = added(third[0], after(third_in, out_left))
    kept = mixed(after(own_rows, third_left))
    near_sent = share_of(after(near_sent, third_left))
    result = added(kept[1], near_sent, outward(out_right), third_right, half=1)
    near_in = inward(after(near[0], third_left))
    out_left, third_left = outward(out_left), across(third_left)
    kept[0] = added(kept[0], near_in, out_left)
    return added(kept[0], third_left, half=0, into=result)


def solution(mesh):
    return jax.shard_map(
        shards,
        mesh=mesh,
        in_specs=(
            P("cand", "tensor"),
            P("cand"),
            P("cand", None),
            P(None, "tensor"),
            P(None, "tensor"),
            P(None, "tensor"),
            P("tensor", None),
            P(),
            P(),
        ),
        out_specs=P(("cand", "tensor"), None),
        check_vma=False,
    )
```
